32 devices in a mesh: section: 2 (over x), tensor: 2 (over core), dp: 8 (over z, y).
Axes of the slice: x: 2, y: 2, z: 4, core: 2. Of those that a mesh axis runs over, the one named last changes fastest.
Arguments:
- tokens: bfloat16 [2048, 2048], P('dp'), may hold values from -6 to 6
- segments: int32 [16, 128], P('dp'), may hold values from 0 to 3, never falling along the last dimension, each value on 1 to 64 neighbouring positions
- cotangent: bfloat16 [2048, 2048], P('dp'), may hold values from -6 to 6
- norm_gain: bfloat16 [2, 2, 2048], P('section'), may hold values from 0.5 to 1.5
- norm_bias: bfloat16 [2, 2, 2048], P('section'), may hold values from -1 to 1
- qkv_weight: bfloat16 [2, 2048, 8, 768], P('section', 'dp', 'tensor'), may hold values from -0.125 to 0.125
- qkv_bias: bfloat16 [2, 8, 768], P('section', 'tensor'), may hold values from -1.5 to 1.5
- out_weight: bfloat16 [2, 8, 256, 2048], P('section', 'tensor', 'dp'), may hold values from -0.5 to 0.5
- out_bias: bfloat16 [2, 2048], P('section'), may hold values from -1 to 1
- up_weight: bfloat16 [2, 2048, 8192], P('section', 'dp', 'tensor'), may hold values from -0.125 to 0.125
- up_bias: bfloat16 [2, 8192], P('section', 'tensor'), may hold values from -1.5 to 1.5
- down_weight: bfloat16 [2, 8192, 2048], P('section', ('tensor', 'dp')), may hold values from -0.0625 to 0.0625
- down_bias: bfloat16 [2, 2048], P('section'), may hold values from -1 to 1
Outputs:
- layer_outputs: bfloat16 [2, 2048, 2048], P('section', 'dp')
- input_gradients: float32 [2, 2048, 2048], P('section', 'dp')
- norm_gain_grad: float32 [2, 2, 2048], P('section')
- norm_bias_grad: float32 [2, 2, 2048], P('section')
- qkv_weight_grad: float32 [2, 2048, 8, 768], P('section', 'dp', 'tensor')
- qkv_bias_grad: float32 [2, 8, 768], P('section', 'tensor')
- out_weight_grad: float32 [2, 8, 256, 2048], P('section', 'tensor', 'dp')
- out_bias_grad: float32 [2, 2048], P('section')
- up_weight_grad: float32 [2, 2048, 8192], P('section', 'dp', 'tensor')
- up_bias_grad: float32 [2, 8192], P('section', 'tensor')
- down_weight_grad: float32 [2, 8192, 2048], P('section', ('tensor', 'dp'))
- down_bias_grad: float32 [2, 2048], P('section')
The draws below stay inside these ranges and needn't reach their ends.
Inputs may be any that keep to these rules, and one draw needn't show every extreme that they name: `segments`: each row is one packed sequence: its segment numbers never fall along the row, a document holds 1 to 64 positions, and some document holds exactly 64.
All inputs are finite; a program needn't handle non-finite values.
Results may differ from the reference program's by a relative error of at most 0.018.
Values may be sent and summed in bfloat16 or wider, within the bound.
No kernel may reach another device: no remote copies, remote signals or barrier semaphores. Data moves between devices by JAX's collectives and lax.ppermute only.
A program may use at most 320 MiB of HBM per device.

```python
import math
import jax
import jax.numpy as jnp
import numpy as np
from jax import lax

D = 2048
HEADS = 8
HD = 256
FF = 8192
ROT = 64
LAYERS = 2
SEQ = 128
ROWS = 16
TOKENS = 2048


def spiked(entries, stream_key, source, target, parts, factor):
    def block_of(dim):
        return (jnp.arange(entries.shape[dim]) // (entries.shape[dim] // parts)).reshape((-1,) + (1,) * (entries.ndim - 1 - dim))

    one_side = jax.random.permutation(stream_key, parts)[block_of(target)]
    far = (block_of(target) + parts // 2) % parts
    return jnp.where((block_of(source) == one_side) | (block_of(source) == far), factor * entries, entries)


def level_of(rng, dims, pieces, least, largest):
    factor_of, own = 1.0, jax.random.fold_in(rng, 6)
    for axis_at, parts in pieces:
        steps = jnp.exp(jax.random.uniform(jax.random.fold_in(own, axis_at), (parts,), jnp.float32, least / len(pieces), largest / len(pieces)))
        factor_of = factor_of * jnp.repeat(steps, dims[axis_at] // parts).reshape([-1 if axis == axis_at else 1 for axis in range(len(dims))])
    return factor_of


def profile(amount, total, limit, skew):
    loads = [(1 << 20) // math.isqrt(rank ** skew) + 1 for rank in range(2, amount + 1)]
    surplus, counts = total - limit - (amount - 1), [1] * (amount - 1)
    while surplus > 0:
        candidates = [i for i in range(amount - 1) if counts[i] < limit]
        mass, left = sum([loads[i] for i in candidates]), surplus
        for i in candidates:
            extra = min(limit - counts[i], max(1, left * loads[i] // mass), surplus)
            counts[i] = counts[i] + extra
            surplus = surplus - extra
    return np.array([limit] + counts)


def ragged_sizes(key, number_of, total, limit, slope):
    if number_of == 2:
        one = jax.random.randint(key, (), max(1, total - limit), min(limit, total - 1) + 1)
        return jnp.stack([one, total - one])
    tallies = jnp.asarray(profile(number_of, total, limit, slope), jnp.int32)
    twos = (number_of - 1) // 2
    donor, sink = tallies[1:1 + 2 * twos:2], tallies[2:2 + 2 * twos:2]
    slack = jnp.minimum(donor - 1, limit - sink)
    moved = jax.random.randint(jax.random.fold_in(key, 1), (twos,), 0, 1 << 20) % (slack + 1)
    tallies = tallies.at[1:1 + 2 * twos:2].set(donor - moved).at[2:2 + 2 * twos:2].set(sink + moved)
    return tallies[jax.random.permutation(jax.random.fold_in(key, 2), number_of)]


def noise(stream_key, shape, scale, limit, shards=(), held_as=jnp.bfloat16):
    entries = jax.random.normal(stream_key, shape, jnp.float32) * scale
    if len(shards) > 0:
        entries = level_of(stream_key, shape, shards, -0.22, 0.18) * entries
    return jnp.clip(entries, min=-limit, max=limit).astype(held_as)


def noise_with(rng, shape, scale, most, shards, heavy, held_as=jnp.bfloat16):
    values = scale * jax.random.normal(rng, shape, jnp.float32)
    if shards:
        values = values * level_of(rng, shape, shards, -0.22, 0.18)
    return jnp.clip(spiked(values, jax.random.fold_in(rng, 3), *heavy), -most, most).astype(held_as)


def setup_inputs(seed: int = 0) -> dict:
    keys = jax.random.split(jax.random.key(seed), 14)
    tokens = noise_with(keys[0], (TOKENS, D), 1.0, 6.0, ((0, 8),), (0, 1, 8, 2.0))
    segments = jax.vmap(lambda own: jnp.searchsorted(jnp.cumsum(ragged_sizes(own, 4, SEQ, SEQ // 2, 1)), jnp.arange(SEQ), side="right"))(jax.random.split(keys[1], ROWS)).reshape((ROWS, SEQ)).astype(jnp.int32)
    cotangent = noise(keys[2], (TOKENS, D), 1.0, 6.0, ((0, 8),))
    norm_gain = jnp.clip(1.0 + 0.1 * jax.random.normal(keys[3], (LAYERS, 2, D), jnp.float32), 0.5, 1.5).astype(jnp.bfloat16)
    norm_bias = noise(keys[4], (LAYERS, 2, D), 0.2, 1.0, ((0, 2),))
    qkv_weight = noise(keys[5], (LAYERS, D, HEADS, 3 * HD), D ** -0.5, 0.125, ((0, 2), (1, 8), (2, 2)))
    qkv_bias = noise(keys[6], (LAYERS, HEADS, 3 * HD), 0.3, 1.5, ((0, 2), (1, 2)))
    out_weight = noise(keys[7], (LAYERS, HEADS, HD, D), (HEADS * HD // 16) ** -0.5, 0.5, ((0, 2), (1, 2), (2, 8)))
    out_bias = noise(keys[8], (LAYERS, D), 0.2, 1.0, ((0, 2),))
    up_weight = noise(keys[9], (LAYERS, D, FF), D ** -0.5, 0.125, ((0, 2), (1, 8), (2, 2)))
    up_bias = noise(keys[10], (LAYERS, FF), 0.3, 1.5, ((0, 2), (1, 2)))
    down_weight = noise(keys[11], (LAYERS, FF, D), FF ** -0.5, 0.0625, ((0, 2), (1, 16)))
    down_bias = noise(keys[12], (LAYERS, D), 0.2, 1.0, ((0, 2),))
    return dict(tokens=tokens, segments=segments, cotangent=cotangent, norm_gain=norm_gain, norm_bias=norm_bias, qkv_weight=qkv_weight, qkv_bias=qkv_bias, out_weight=out_weight, out_bias=out_bias, up_weight=up_weight, up_bias=up_bias, down_weight=down_weight, down_bias=down_bias)


@jax.custom_vjp
def low(v):
    return lax.optimization_barrier(v.astype(jnp.bfloat16)).astype(jnp.float32)

@jax.custom_vjp
def low_back(v):
    return v

def low_keep(v):
    return (low(v), None)

def low_pass(kept, grad):
    return (grad,)

def back_keep(v):
    return (v, None)

def back_low(kept, grad):
    return (low(grad),)
low.defvjp(low_keep, low_pass)
low_back.defvjp(back_keep, back_low)
NORM_EPSILON = 1e-05
MASK_VALUE = -1e+30

def product(left_side, right_side):
    return jnp.dot(left_side, right_side, precision=lax.Precision.HIGHEST, preferred_element_type=jnp.float32)

def layer_norm(values, norm_gain, shift_bias):
    centered = values - lax.optimization_barrier(jnp.mean(values, axis=-1, keepdims=True))
    inverse = lax.rsqrt(lax.optimization_barrier(jnp.mean(centered * centered, axis=-1, keepdims=True)) + NORM_EPSILON)
    return centered * inverse * norm_gain + shift_bias

def document_tables(segment):
    places = jnp.arange(SEQ, dtype=jnp.int32)
    same_doc = segment[:, None] == segment[None, :]
    earlier = places[None, :] < places[:, None]
    position = lax.optimization_barrier(jnp.sum(jnp.where(same_doc & earlier, 1, 0).astype(jnp.int32), axis=1)).astype(jnp.int32)
    allowed = same_doc & (places[None, :] <= places[:, None])
    return (position, allowed)

def rotary_tables(position):
    half_width = ROT // 2
    exponent = jnp.arange(half_width, dtype=jnp.float32) * (2.0 / ROT)
    frequency = 10000.0 ** (-exponent)
    angles = position.astype(jnp.float32)[:, None] * frequency[None, :]
    cosine_table = jnp.cos(angles)
    sine_table = jnp.sin(angles)
    return (jnp.concatenate([cosine_table, cosine_table], axis=1), jnp.concatenate([sine_table, sine_table], axis=1))

def rotate(values, cosine_table, sine_table):
    half_width = ROT // 2
    turned = values[..., :ROT]
    swapped = jnp.concatenate([-turned[..., half_width:], turned[..., :half_width]], axis=-1)
    turned = turned * cosine_table[:, None, :] + swapped * sine_table[:, None, :]
    return jnp.concatenate([turned, values[..., ROT:]], axis=-1)

def attend_sequence(packed):
    qkv_rows, segment = packed
    position, allowed = document_tables(segment)
    cosine_table, sine_table = rotary_tables(position)
    queries = low(rotate(qkv_rows[:, :, 0, :], cosine_table, sine_table))
    key_rows = low(rotate(qkv_rows[:, :, 1, :], cosine_table, sine_table))
    values = low(qkv_rows[:, :, 2, :])
    scores = jnp.einsum('qhd,khd->hqk', queries, key_rows, precision=lax.Precision.HIGHEST) * (1.0 / math.sqrt(HD))
    scores = low_back(scores)
    scores = jnp.where(allowed[None], scores, MASK_VALUE)
    attention = low(jax.nn.softmax(scores, axis=-1))
    return jnp.einsum('hqk,khd->qhd', attention, values, precision=lax.Precision.HIGHEST)

def residual_block(inputs, segments, norm_gain, norm_bias, qkv_weight, qkv_bias, out_weight, out_bias, up_weight, up_bias, down_weight, down_bias):
    first_norm = layer_norm(inputs, norm_gain[0], norm_bias[0])
    second_norm = layer_norm(inputs, norm_gain[1], norm_bias[1])
    joined = product(low(first_norm), qkv_weight.reshape(D, HEADS * 3 * HD)) + qkv_bias.reshape(HEADS * 3 * HD)
    joined = low_back(joined).reshape(ROWS, SEQ, HEADS, 3, HD)
    attended = lax.map(jax.checkpoint(attend_sequence), (joined, segments))
    attended = low(low_back(attended)).reshape(TOKENS, HEADS * HD)
    hidden = low_back(product(low(second_norm), up_weight) + up_bias)
    active = low(jax.nn.gelu(hidden, approximate=False))
    branch = product(attended, out_weight.reshape(HEADS * HD, D)) + product(active, down_weight)
    return inputs + branch + out_bias + down_bias

def widen(array):
    return array.astype(jnp.float32)

def reference(tokens, segments, cotangent, norm_gain, norm_bias, qkv_weight, qkv_bias, out_weight, out_bias, up_weight, up_bias, down_weight, down_bias):
    parameters = tuple((widen(item) for item in (norm_gain, norm_bias, qkv_weight, qkv_bias, out_weight, out_bias, up_weight, up_bias, down_weight, down_bias)))

    def forward(inputs, shift_in, weights):
        first_out = residual_block(inputs, segments, *[item[0] for item in weights])
        passed = low_back(low(first_out)) + shift_in
        second_out = residual_block(passed, segments, *[item[1] for item in weights])
        return (first_out, second_out)
    no_shift = jnp.zeros((TOKENS, D), jnp.float32)
    (first_out, second_out), pullback = jax.vjp(forward, widen(tokens), no_shift, parameters)
    token_grad, passed_grad, weight_grads = pullback((jnp.zeros_like(first_out), widen(cotangent)))
    layer_outputs = jnp.stack([first_out, second_out]).astype(jnp.bfloat16)
    input_gradients = jnp.stack([token_grad, passed_grad])
    return (layer_outputs, input_gradients, weight_grads[0], weight_grads[1], weight_grads[2], weight_grads[3], weight_grads[4], weight_grads[5], weight_grads[6], weight_grads[7], weight_grads[8], weight_grads[9])
```

```python
import math

import jax
import jax.numpy as jnp
from jax import lax
from jax.sharding import PartitionSpec as P

ROT = 64
NORM_EPSILON = 1e-05
MASK_VALUE = -1e30
ROOT_HALF = 0.7071067811865476
DENSITY_SCALE = 0.3989422804014327
F32 = jnp.float32
BF16 = jnp.bfloat16


def contract_rows(left_side, right_side):
    return lax.dot_general(
        left_side, right_side, (((0,), (0,)), ((), ())), preferred_element_type=F32
    )


def contract_cols(left_side, right_side):
    return lax.dot_general(
        left_side, right_side, (((1,), (1,)), ((), ())), preferred_element_type=F32
    )


def matmul(left_side, right_side):
    return jnp.dot(left_side, right_side, preferred_element_type=F32)


def normalize(values):
    centered = values - jnp.mean(values, axis=-1, keepdims=True)
    inverse = lax.rsqrt(jnp.mean(centered * centered, axis=-1, keepdims=True) + NORM_EPSILON)
    return (centered * inverse, inverse)


def document_tables(segments):
    places = jnp.arange(segments.shape[1], dtype=jnp.int32)
    same_doc = segments[:, :, None] == segments[:, None, :]
    earlier = places[None, :] < places[:, None]
    position = jnp.sum(jnp.where(same_doc & earlier, 1, 0).astype(jnp.int32), axis=2)
    allowed = same_doc & (places[None, :] <= places[:, None])
    return (position, allowed)


def rotary_tables(position):
    exponent = jnp.arange(ROT // 2, dtype=F32) * (2.0 / ROT)
    frequency = 10000.0 ** (-exponent)
    angles = position.astype(F32)[..., None] * frequency
    return (jnp.cos(angles), jnp.sin(angles))


def rotate(values, cosine, sine):
    half = ROT // 2
    first, second = values[..., :half], values[..., half:ROT]
    return jnp.concatenate(
        [first * cosine - second * sine, second * cosine + first * sine, values[..., ROT:]],
        axis=-1,
    )


class Layout:
    def __init__(self, mesh, heads):
        self.sections = mesh.shape["section"]
        self.cores = mesh.shape["tensor"]
        self.dp = mesh.shape["dp"]
        self.chips = heads
        self.groups = self.dp // heads
        self.core_heads = heads // self.cores
        self.ring = list(range(0, heads, 2)) + list(range(heads - 1, 0, -2))

    def place(self):
        dp_index = lax.axis_index("dp")
        self.core = lax.axis_index("tensor")
        self.chip = dp_index // self.groups
        self.group = dp_index % self.groups

    def between_chips(self, block, target_of, sections=None):
        if sections is None:
            pairs = [
                (chip * self.groups + group, target_of(chip) * self.groups + group)
                for chip in range(self.chips)
                for group in range(self.groups)
            ]
            return lax.ppermute(block, "dp", pairs)
        pairs = [
            (
                section * self.dp + chip * self.groups + group,
                section * self.dp + target_of(chip) * self.groups + group,
            )
            for section in sections
            for chip in range(self.chips)
            for group in range(self.groups)
        ]
        return lax.ppermute(block, ("section", "dp"), pairs)

    def ring_step(self, block, distance, sections=None):
        size = len(self.ring)

        def target_of(chip):
            return self.ring[(self.ring.index(chip) + distance) % size]

        return self.between_chips(block, target_of, sections)

    def between_groups(self, block, distance):
        pairs = [
            (chip * self.groups + group, chip * self.groups + (group + distance) % self.groups)
            for chip in range(self.chips)
            for group in range(self.groups)
        ]
        return lax.ppermute(block, "dp", pairs)

    def other_core(self, block):
        return lax.ppermute(block, "tensor", [(0, 1), (1, 0)])

    def gather_groups(self, block, axis):
        if self.groups == 1:
            return block
        size = block.shape[axis]
        shape = list(block.shape)
        shape[axis] = size * self.groups
        total = jnp.zeros(shape, block.dtype)
        for distance in range(self.groups):
            part = self.between_groups(block, distance) if distance else block
            source = (self.group - distance) % self.groups
            total = lax.dynamic_update_slice_in_dim(total, part, source * size, axis)
        return total

    def scatter_groups(self, block, axis):
        if self.groups == 1:
            return block.astype(F32)
        size = block.shape[axis] // self.groups
        total = lax.dynamic_slice_in_dim(block, self.group * size, size, axis).astype(F32)
        for distance in range(1, self.groups):
            target = (self.group + distance) % self.groups
            part = lax.dynamic_slice_in_dim(block, target * size, size, axis)
            total = total + self.between_groups(part.astype(BF16), distance).astype(F32)
        return total

    def ring_gather(self, block, sections=None):
        half = self.chips // 2
        below, above = [block], []
        for _ in range(half):
            below.append(self.ring_step(below[-1], -1, sections))
        moving = block
        for _ in range(self.chips - 1 - half):
            moving = self.ring_step(moving, 1, sections)
            above.append(moving)
        return jnp.concatenate(below + above[::-1], axis=0)

    def ring_scatter(self, partial, sections=None):
        half = self.chips // 2
        rows = partial.shape[0] // self.chips
        pieces = [partial[k * rows : (k + 1) * rows] for k in range(self.chips)]
        total = pieces[0].astype(F32)
        moving = pieces[half].astype(BF16)
        for k in range(half - 1, -1, -1):
            arrived = self.ring_step(moving, 1, sections).astype(F32)
            if k == 0:
                total = total + arrived
            else:
                moving = (arrived + pieces[k].astype(F32)).astype(BF16)
        moving = pieces[half + 1].astype(BF16)
        for k in range(half + 2, self.chips + 1):
            arrived = self.ring_step(moving, -1, sections).astype(F32)
            if k == self.chips:
                total = total + arrived
            else:
                moving = (arrived + pieces[k].astype(F32)).astype(BF16)
        return total

    def head_route(self, turn):
        pairs = []
        for core in range(self.cores):
            for chip in range(self.chips):
                head = (chip // self.cores + turn) % self.core_heads
                target_core, target = chip % self.cores, core * self.core_heads + head
                for group in range(self.groups):
                    pairs.append(
                        (
                            core * self.dp + chip * self.groups + group,
                            target_core * self.dp + target * self.groups + group,
                        )
                    )
        return pairs

    def heads_out(self, blocks):
        rows, cols = blocks.shape[1:]
        held = jnp.zeros((self.core_heads, rows, cols), blocks.dtype)
        for turn in range(self.core_heads):
            head = (self.chip // self.cores + turn) % self.core_heads
            block = lax.dynamic_index_in_dim(blocks, head, 0, keepdims=True)
            block = lax.ppermute(block, ("tensor", "dp"), self.head_route(turn))
            slot = (self.chip - turn) % self.core_heads
            held = lax.dynamic_update_slice_in_dim(held, block, slot, 0)
        other = self.other_core(held)
        first = self.core == 0
        whole = jnp.stack(
            [jnp.where(first, held, other), jnp.where(first, other, held)], axis=1
        )
        return whole.reshape(self.chips * rows, cols)

    def heads_back(self, whole):
        rows = whole.shape[0] // self.chips
        cols = whole.shape[1]
        split = whole.reshape(self.core_heads, self.cores, rows, cols)
        first = self.core == 0
        own = jnp.where(first, split[:, 0], split[:, 1])
        given = jnp.where(first, split[:, 1], split[:, 0]).astype(BF16)
        held = (own + self.other_core(given).astype(F32)).astype(BF16)
        blocks = jnp.zeros((self.core_heads, rows, cols), BF16)
        for turn in range(self.core_heads):
            slot = (self.chip - turn) % self.core_heads
            block = lax.dynamic_index_in_dim(held, slot, 0, keepdims=True)
            pairs = [(target, source) for source, target in self.head_route(turn)]
            block = lax.ppermute(block, ("tensor", "dp"), pairs)
            head = (self.chip // self.cores + turn) % self.core_heads
            blocks = lax.dynamic_update_slice_in_dim(blocks, block, head, 0)
        return blocks

    def columns_out(self, block):
        rows = block.shape[0]
        width = block.shape[1] // self.chips
        whole = jnp.zeros((rows * self.chips, width), block.dtype)
        for mask in range(self.chips):
            source = self.chip ^ mask
            part = lax.dynamic_slice_in_dim(block, source * width, width, 1)
            if mask:
                part = self.between_chips(part, lambda chip: chip ^ mask)
            whole = lax.dynamic_update_slice_in_dim(whole, part, source * rows, 0)
        return jnp.concatenate([whole, self.other_core(whole)], axis=1)

    def columns_back(self, whole):
        rows = whole.shape[0] // self.chips
        width = whole.shape[1] // self.cores
        held = whole[:, :width] + self.other_core(whole[:, width:].astype(BF16)).astype(F32)
        held = held.astype(BF16)
        block = jnp.zeros((rows, width * self.chips), BF16)
        for mask in range(self.chips):
            source = self.chip ^ mask
            part = lax.dynamic_slice_in_dim(held, source * rows, rows, 0)
            if mask:
                part = self.between_chips(part, lambda chip: chip ^ mask)
            block = lax.dynamic_update_slice_in_dim(block, part, source * width, 1)
        return block


def attention_parts(joined, tables):
    cosine, sine, allowed = tables
    sequences, length = allowed.shape[:2]
    head_size = joined.shape[1] // 3
    joined = joined.reshape(sequences, length, 3, head_size)
    queries = rotate(joined[:, :, 0], cosine, sine).astype(BF16)
    key_rows = rotate(joined[:, :, 1], cosine, sine).astype(BF16)
    values = joined[:, :, 2].astype(BF16)
    scores = jnp.einsum("sqd,skd->sqk", queries, key_rows, preferred_element_type=F32)
    scores = jnp.where(allowed, scores * (1.0 / math.sqrt(head_size)), MASK_VALUE)
    powered = jnp.exp(scores - jnp.max(scores, axis=-1, keepdims=True))
    attention = powered / jnp.sum(powered, axis=-1, keepdims=True)
    attended = jnp.einsum(
        "sqk,skd->sqd", attention.astype(BF16), values, preferred_element_type=F32
    ).astype(BF16)
    return (queries, key_rows, values, attention, attended.reshape(sequences * length, head_size))


def attention_back(parts, attended_grad, tables):
    queries, key_rows, values, attention, _ = parts
    cosine, sine, _ = tables
    sequences, length, head_size = queries.shape
    scale = 1.0 / math.sqrt(head_size)
    attended_grad = attended_grad.reshape(sequences, length, head_size)
    values_grad = jnp.einsum(
        "sqk,sqd->skd", attention.astype(BF16), attended_grad, preferred_element_type=F32
    )
    attention_grad = jnp.einsum(
        "sqd,skd->sqk", attended_grad, values, preferred_element_type=F32
    )
    row_dots = jnp.sum(attention_grad * attention, axis=-1, keepdims=True)
    scores_grad = (attention * (attention_grad - row_dots)).astype(BF16)
    queries_grad = scale * jnp.einsum(
        "sqk,skd->sqd", scores_grad, key_rows, preferred_element_type=F32
    )
    keys_grad = scale * jnp.einsum(
        "sqk,sqd->skd", scores_grad, queries, preferred_element_type=F32
    )
    return (
        jnp.stack(
            [rotate(queries_grad, cosine, -sine), rotate(keys_grad, cosine, -sine), values_grad],
            axis=2,
        )
        .reshape(sequences * length, 3 * head_size)
        .astype(BF16)
    )


def on_device(
    layout,
    tokens,
    segments,
    cotangent,
    norm_gain,
    norm_bias,
    qkv_weight,
    qkv_bias,
    out_weight,
    out_bias,
    up_weight,
    up_bias,
    down_weight,
    down_bias,
):
    layout.place()
    first_section = lax.axis_index("section") == 0
    cores, chips, chip, core = layout.cores, layout.chips, layout.chip, layout.core
    length = segments.shape[1]
    width = tokens.shape[1]
    core_heads, joined_size = qkv_weight.shape[2:]
    head_size = joined_size // 3
    hidden_part = up_weight.shape[2] // chips

    def core_rows(block):
        return lax.dynamic_slice_in_dim(block, core * length, length, 0)

    def both_cores(rows):
        other = layout.other_core(rows)
        return jnp.concatenate(
            [jnp.where(core == 0, rows, other), jnp.where(core == 0, other, rows)], axis=0
        )

    gains = norm_gain[0].astype(F32)
    shifts = norm_bias[0].astype(F32)
    own_tokens = core_rows(tokens).astype(F32)
    own_cotangent = core_rows(cotangent)
    own_normed, own_inverse = normalize(own_tokens)
    gathered = layout.ring_gather(
        jnp.where(first_section, own_normed.astype(BF16), own_cotangent)
    )

    ring = jnp.array(layout.ring, jnp.int32)
    ring_place = jnp.array([layout.ring.index(c) for c in range(chips)], jnp.int32)
    chip_of = ring[(ring_place[chip] + jnp.arange(chips)) % chips]
    all_segments = lax.all_gather(segments, "dp", axis=0, tiled=True)
    own_segments = all_segments[(chip_of * layout.groups + layout.group) * cores + core]
    position, allowed = document_tables(own_segments)
    tables = rotary_tables(position) + (allowed,)

    shard = qkv_weight.shape[1]
    at = lax.axis_index("dp") * shard
    qkv_scaled = qkv_weight[0].astype(F32) * lax.dynamic_slice_in_dim(gains[0], at, shard)[:, None, None]
    up_scaled = up_weight[0].astype(F32) * lax.dynamic_slice_in_dim(gains[1], at, shard)[:, None]
    joined_weight = layout.heads_out(
        layout.gather_groups(qkv_scaled.astype(BF16).transpose(1, 0, 2), 1)
    )
    out_matrix = layout.heads_out(layout.gather_groups(out_weight[0], 1))
    hidden_weight = layout.columns_out(layout.gather_groups(up_scaled.astype(BF16), 0))
    down_own = layout.gather_groups(down_weight[0], 0)
    down_matrix = jnp.concatenate([down_own, layout.other_core(down_own)], axis=0)

    all_joined_bias = lax.all_gather(qkv_bias[0].astype(F32), "tensor", axis=0, tiled=True)
    all_up_bias = lax.all_gather(up_bias[0].astype(F32), "tensor", axis=0)
    joined_bias = lax.dynamic_index_in_dim(all_joined_bias, chip, 0, keepdims=False)
    hidden_bias = lax.dynamic_slice_in_dim(all_up_bias, chip * hidden_part, hidden_part, 1)
    hidden_bias = jnp.concatenate(
        [
            lax.dynamic_index_in_dim(hidden_bias, core, 0, keepdims=False),
            lax.dynamic_index_in_dim(hidden_bias, 1 - core, 0, keepdims=False),
        ]
    )
    ratio = (shifts / gains).astype(BF16)
    joined_bias = joined_bias + matmul(ratio[:1], joined_weight)[0]
    hidden_bias = hidden_bias + matmul(ratio[1:], hidden_weight)[0]
    row_bias = (out_bias[0].astype(F32) + down_bias[0].astype(F32))[None]

    def forward(normed):
        joined = matmul(normed, joined_weight) + joined_bias
        parts = attention_parts(joined, tables)
        hidden = matmul(normed, hidden_weight) + hidden_bias
        active = jax.nn.gelu(hidden, approximate=False).astype(BF16)
        return (parts, hidden, active)

    def branch(parts, active):
        return matmul(parts[-1], out_matrix) + matmul(active, down_matrix)

    def backward(upstream, parts, hidden):
        attended_grad = contract_cols(upstream, out_matrix).astype(BF16)
        active_grad = contract_cols(upstream, down_matrix)
        normal_cdf = 0.5 * (1.0 + lax.erf(hidden * ROOT_HALF))
        normal_pdf = jnp.exp(-0.5 * hidden * hidden) * DENSITY_SCALE
        hidden_grad = (active_grad * (normal_cdf + hidden * normal_pdf)).astype(BF16)
        joined_grad = attention_back(parts, attended_grad, tables)
        scaled = contract_cols(joined_grad, joined_weight) + contract_cols(
            hidden_grad, hidden_weight
        )
        return (scaled, joined_grad, hidden_grad)

    def norm_back(upstream, scaled, normed, inverse):
        return upstream.astype(F32) + inverse * (
            scaled
            - jnp.mean(scaled, axis=-1, keepdims=True)
            - normed * jnp.mean(scaled * normed, axis=-1, keepdims=True)
        )

    parts, _, active = forward(gathered)
    branch_rows = layout.ring_scatter(branch(parts, active), (0,))
    first_out = (own_tokens + branch_rows + row_bias).astype(BF16)

    arrived = lax.ppermute(first_out, "section", [(0, 1)])
    layer_input = jnp.where(first_section, own_tokens, arrived.astype(F32))
    own_normed, own_inverse = normalize(layer_input)
    normed = layout.ring_gather(own_normed.astype(BF16))
    parts, hidden, active = forward(normed)

    scaled, _, _ = backward(gathered, parts, hidden)
    scaled_rows = layout.ring_scatter(scaled, (1,))
    second_grad = norm_back(own_cotangent, scaled_rows, own_normed, own_inverse)

    arrived_grad = lax.ppermute(second_grad.astype(BF16), "section", [(1, 0)])
    own_upstream = jnp.where(first_section, arrived_grad, own_cotangent)
    upstream = layout.ring_gather(own_upstream)
    scaled, joined_grad, hidden_grad = backward(upstream, parts, hidden)

    branch_rows = layout.ring_scatter(branch(parts, active), (1,))
    second_out = (layer_input + branch_rows + row_bias).astype(BF16)
    layer_outputs = both_cores(jnp.where(first_section, first_out, second_out))

    scaled_rows = layout.ring_scatter(scaled, (0,))
    first_grad = norm_back(own_upstream, scaled_rows, own_normed, own_inverse)
    input_gradients = both_cores(jnp.where(first_section, first_grad, second_grad))

    out_grad = contract_rows(parts[-1], upstream)
    down_grad = contract_rows(active, upstream)
    hidden_weight_grad = contract_rows(normed, hidden_grad)
    joined_weight_grad = contract_rows(normed, joined_grad)
    joined_bias_part = jnp.sum(joined_grad, axis=0, dtype=F32)
    hidden_bias_part = jnp.sum(hidden_grad, axis=0, dtype=F32)

    gain_part = jnp.stack(
        [
            jnp.sum(joined_weight_grad * joined_weight, axis=1),
            jnp.sum(hidden_weight_grad * hidden_weight, axis=1),
        ]
    ) / gains
    shift_part = jnp.stack(
        [
            jnp.sum(joined_weight * joined_bias_part, axis=1),
            jnp.sum(hidden_weight * hidden_bias_part, axis=1),
        ]
    ) / gains
    joined_bias_all = lax.dynamic_update_slice(
        jnp.zeros((chips, joined_size), F32), joined_bias_part[None], (chip, 0)
    )
    hidden_bias_all = jnp.zeros((cores, chips, hidden_part), F32)
    hidden_bias_all = lax.dynamic_update_slice(
        hidden_bias_all, hidden_bias_part[None, None, :hidden_part], (core, chip, 0)
    )
    hidden_bias_all = lax.dynamic_update_slice(
        hidden_bias_all, hidden_bias_part[None, None, hidden_part:], (1 - core, chip, 0)
    )
    vectors = (
        gain_part,
        shift_part,
        joined_bias_all,
        jnp.sum(own_upstream, axis=0, dtype=F32),
        hidden_bias_all,
    )
    sizes = [item.size for item in vectors]
    joint = jnp.concatenate([item.reshape(-1) for item in vectors])
    joint = lax.psum(joint, ("tensor", "dp"))
    summed, start = [], 0
    for item, size in zip(vectors, sizes):
        summed.append(joint[start : start + size].reshape(item.shape))
        start += size
    gain_grad, shift_grad, joined_bias_all, out_bias_grad, hidden_bias_all = summed
    joined_bias_grad = lax.dynamic_slice_in_dim(joined_bias_all, core * core_heads, core_heads, 0)
    up_bias_grad = lax.dynamic_index_in_dim(hidden_bias_all, core, 0, keepdims=False).reshape(-1)

    out_weight_grad = layout.scatter_groups(layout.heads_back(out_grad), 1)
    own_half = down_grad.shape[0] // cores
    down_weight_grad = down_grad[:own_half] + layout.other_core(
        down_grad[own_half:].astype(BF16)
    ).astype(F32)
    if layout.groups > 1:
        down_weight_grad = layout.scatter_groups(down_weight_grad, 0)
    up_plain = layout.scatter_groups(layout.columns_back(hidden_weight_grad), 0)
    joined_plain = layout.scatter_groups(layout.heads_back(joined_weight_grad), 1)
    gain_rows = lax.dynamic_slice_in_dim(gains, at, shard, 1)
    shift_rows = lax.dynamic_slice_in_dim(shifts, at, shard, 1)
    up_weight_grad = up_plain * gain_rows[1][:, None] + shift_rows[1][:, None] * up_bias_grad
    joined_weight_grad = (
        joined_plain.transpose(1, 0, 2) * gain_rows[0][:, None, None]
        + shift_rows[0][:, None, None] * joined_bias_grad
    )

    return (
        layer_outputs[None],
        input_gradients[None],
        gain_grad[None],
        shift_grad[None],
        joined_weight_grad[None],
        joined_bias_grad[None],
        out_weight_grad[None],
        out_bias_grad[None],
        up_weight_grad[None],
        up_bias_grad[None],
        down_weight_grad[None],
        out_bias_grad[None],
    )


def solution(mesh):
    def whole(*arrays):
        layout = Layout(mesh, arrays[5].shape[2])

        def local(*blocks):
            return on_device(layout, *blocks)

        return jax.shard_map(
            local,
            mesh=mesh,
            in_specs=(
                P("dp", None),
                P("dp", None),
                P("dp", None),
                P("section", None, None),
                P("section", None, None),
                P("section", "dp", "tensor", None),
                P("section", "tensor", None),
                P("section", "tensor", "dp", None),
                P("section", None),
                P("section", "dp", "tensor"),
                P("section", "tensor"),
                P("section", ("tensor", "dp"), None),
                P("section", None),
            ),
            out_specs=(
                P("section", "dp", None),
                P("section", "dp", None),
                P("section", None, None),
                P("section", None, None),
                P("section", "dp", "tensor", None),
                P("section", "tensor", None),
                P("section", "tensor", "dp", None),
                P("section", None),
                P("section", "dp", "tensor"),
                P("section", "tensor"),
                P("section", ("tensor", "dp"), None),
                P("section", None),
            ),
            check_vma=False,
        )(*arrays)

    return whole
```

```python
import functools
import math

import jax
import jax.numpy as jnp
from jax import lax
from jax.experimental import pallas as pl
from jax.experimental.pallas import tpu as pltpu
from jax.sharding import PartitionSpec as P

ROT = 64
LANES = 128
NORM_EPSILON = 1e-05
MASK_VALUE = -1e30
ROOT_HALF = 0.7071067811865476
DENSITY_SCALE = 0.3989422804014327
F32 = jnp.float32
BF16 = jnp.bfloat16


def contract_rows(left_side, right_side):
    return lax.dot_general(
        left_side, right_side, (((0,), (0,)), ((), ())), preferred_element_type=F32
    )


def contract_cols(left_side, right_side):
    return lax.dot_general(
        left_side, right_side, (((1,), (1,)), ((), ())), preferred_element_type=F32
    )


def matmul(left_side, right_side):
    return jnp.dot(left_side, right_side, preferred_element_type=F32)


def normalize(values):
    centered = values - jnp.mean(values, axis=-1, keepdims=True)
    inverse = lax.rsqrt(jnp.mean(centered * centered, axis=-1, keepdims=True) + NORM_EPSILON)
    return (centered * inverse, inverse)


def sequence_tables(segments):
    places = jnp.arange(segments.shape[1], dtype=jnp.int32)
    same_doc = segments[:, :, None] == segments[:, None, :]
    earlier = places[None, :] < places[:, None]
    position = jnp.sum(jnp.where(same_doc & earlier, 1, 0).astype(jnp.int32), axis=2)
    allowed = same_doc & (places[None, :] <= places[:, None])
    exponent = jnp.arange(ROT // 2, dtype=F32) * (2.0 / ROT)
    frequency = 10000.0 ** (-exponent)
    angles = position.astype(F32)[..., None] * frequency
    cosine, sine = jnp.cos(angles), jnp.sin(angles)
    rest = jnp.zeros(angles.shape[:2] + (LANES - ROT,), F32)
    count = segments.shape[0] * segments.shape[1]
    return (
        jnp.concatenate([cosine, cosine, rest + 1.0], axis=-1).reshape(count, LANES),
        jnp.concatenate([-sine, sine, rest], axis=-1).reshape(count, LANES),
        jnp.where(allowed, 0.0, MASK_VALUE).astype(F32).reshape(count, segments.shape[1]),
    )


class Layout:
    def __init__(self, mesh, heads):
        self.cores = mesh.shape["tensor"]
        self.dp = mesh.shape["dp"]
        self.chips = heads
        self.groups = self.dp // heads
        self.core_heads = heads // self.cores
        self.ring = list(range(0, heads, 2)) + list(range(heads - 1, 0, -2))
        self.slots = []
        for k in range(heads // 2):
            self.slots += [-k % heads, k + 1]

    def place(self):
        dp_index = lax.axis_index("dp")
        self.core = lax.axis_index("tensor")
        self.chip = dp_index // self.groups
        self.group = dp_index % self.groups

    def between_chips(self, block, target_of, sections=None):
        pairs = [
            (chip * self.groups + group, target_of(chip) * self.groups + group)
            for chip in range(self.chips)
            for group in range(self.groups)
        ]
        if sections is None:
            return lax.ppermute(block, "dp", pairs)
        pairs = [
            (section * self.dp + source, section * self.dp + target)
            for section in sections
            for source, target in pairs
        ]
        return lax.ppermute(block, ("section", "dp"), pairs)

    def ring_step(self, block, distance, sections=None):
        size = len(self.ring)

        def target_of(chip):
            return self.ring[(self.ring.index(chip) + distance) % size]

        return self.between_chips(block, target_of, sections)

    def between_groups(self, block, distance):
        pairs = [
            (chip * self.groups + group, chip * self.groups + (group + distance) % self.groups)
            for chip in range(self.chips)
            for group in range(self.groups)
        ]
        return lax.ppermute(block, "dp", pairs)

    def other_core(self, block):
        return lax.ppermute(block, "tensor", [(0, 1), (1, 0)])

    def by_core(self, own, other):
        first = self.core == 0
        return jnp.concatenate(
            [jnp.where(first, own, other), jnp.where(first, other, own)], axis=0
        )

    def gather_groups(self, block, axis):
        if self.groups == 1:
            return block
        size = block.shape[axis]
        shape = list(block.shape)
        shape[axis] = size * self.groups
        total = jnp.zeros(shape, block.dtype)
        for distance in range(self.groups):
            part = self.between_groups(block, distance) if distance else block
            source = (self.group - distance) % self.groups
            total = lax.dynamic_update_slice_in_dim(total, part, source * size, axis)
        return total

    def scatter_groups(self, block, axis):
        if self.groups == 1:
            return block.astype(F32)
        size = block.shape[axis] // self.groups
        total = lax.dynamic_slice_in_dim(block, self.group * size, size, axis).astype(F32)
        for distance in range(1, self.groups):
            target = (self.group + distance) % self.groups
            part = lax.dynamic_slice_in_dim(block, target * size, size, axis)
            total = total + self.between_groups(part.astype(BF16), distance).astype(F32)
        return total

    def gather_chips(self, block):
        held = block[None]
        mask = 1
        while mask < self.chips:
            held = jnp.concatenate(
                [held, self.between_chips(held, lambda chip: chip ^ mask)], axis=0
            )
            mask *= 2
        return held

    def sum_all(self, block):
        block = block + self.other_core(block)
        mask = 1
        while mask < self.chips:
            block = block + self.between_chips(block, lambda chip: chip ^ mask)
            mask *= 2
        total = block
        for distance in range(1, self.groups):
            total = total + self.between_groups(block, distance)
        return total

    def ring_gather(self, block):
        half = self.chips // 2
        held = {0: block}
        for k in range(1, half + 1):
            held[k] = self.ring_step(held[k - 1], -1)
            if k < half:
                held[self.chips - k] = self.ring_step(held[(self.chips - k + 1) % self.chips], 1)
        return held

    def ring_scatter(self, pieces, sections):
        half = self.chips // 2
        total = pieces[0].astype(F32)
        moving = pieces[half]
        for k in range(half - 1, -1, -1):
            arrived = self.ring_step(moving, 1, sections).astype(F32)
            if k == 0:
                total = total + arrived
            else:
                moving = (arrived + pieces[k].astype(F32)).astype(BF16)
        moving = pieces[half + 1]
        for k in range(half + 2, self.chips + 1):
            arrived = self.ring_step(moving, -1, sections).astype(F32)
            if k == self.chips:
                total = total + arrived
            else:
                moving = (arrived + pieces[k].astype(F32)).astype(BF16)
        return total

    def head_turn(self, chip, turn):
        return (chip % self.core_heads + turn) % self.core_heads

    def head_route(self, turn):
        pairs = []
        for core in range(self.cores):
            for chip in range(self.chips):
                target_core = chip // self.core_heads
                target = core * self.core_heads + self.head_turn(chip, turn)
                for group in range(self.groups):
                    pairs.append(
                        (
                            core * self.dp + chip * self.groups + group,
                            target_core * self.dp + target * self.groups + group,
                        )
                    )
        return pairs

    def heads_out(self, take):
        held = None
        for turn in range(self.core_heads):
            block = take(self.head_turn(self.chip, turn))
            block = lax.ppermute(block, ("tensor", "dp"), self.head_route(turn))
            rows, cols = block.shape
            if held is None:
                held = jnp.zeros((self.core_heads * rows, cols), block.dtype)
            slot = (self.chip - turn) % self.core_heads
            held = lax.dynamic_update_slice_in_dim(held, block, slot * rows, 0)
        return self.by_core(held, self.other_core(held))

    def heads_back(self, held, put, blocks):
        rows = held.shape[0] // self.core_heads
        for turn in range(self.core_heads):
            slot = (self.chip - turn) % self.core_heads
            block = lax.dynamic_slice_in_dim(held, slot * rows, rows, 0)
            pairs = [(target, source) for source, target in self.head_route(turn)]
            block = lax.ppermute(block, ("tensor", "dp"), pairs)
            blocks = put(blocks, self.head_turn(self.chip, turn), block)
        return blocks

    def columns_out(self, block):
        rows = block.shape[0]
        width = block.shape[1] // self.chips
        whole = jnp.zeros((rows * self.chips, width), block.dtype)
        for mask in range(self.chips):
            source = self.chip ^ mask
            part = lax.dynamic_slice_in_dim(block, source * width, width, 1)
            if mask:
                part = self.between_chips(part, lambda chip: chip ^ mask)
            whole = lax.dynamic_update_slice_in_dim(whole, part, source * rows, 0)
        return jnp.concatenate([whole, self.other_core(whole)], axis=1)

    def columns_back(self, held):
        rows = held.shape[0] // self.chips
        width = held.shape[1]
        block = jnp.zeros((rows, width * self.chips), BF16)
        for mask in range(self.chips):
            source = self.chip ^ mask
            part = lax.dynamic_slice_in_dim(held, source * rows, rows, 0)
            if mask:
                part = self.between_chips(part, lambda chip: chip ^ mask)
            block = lax.dynamic_update_slice_in_dim(block, part, source * width, 1)
        return block


def turn_head(values, cosine, sine):
    first = values[:, :LANES]
    lane = lax.broadcasted_iota(jnp.int32, first.shape, 1)
    half = ROT // 2
    swapped = jnp.where(
        lane < half, pltpu.roll(first, LANES - half, 1), pltpu.roll(first, half, 1)
    )
    return jnp.concatenate([first * cosine + swapped * sine, values[:, LANES:]], axis=1)


def attend(joined, cosine, sine, mask):
    size = joined.shape[1] // 3
    queries = turn_head(joined[:, :size], cosine, sine).astype(BF16)
    key_rows = turn_head(joined[:, size : 2 * size], cosine, sine).astype(BF16)
    values = joined[:, 2 * size :].astype(BF16)
    scores = contract_cols(queries, key_rows) * (1.0 / math.sqrt(size)) + mask
    powered = jnp.exp(scores - jnp.max(scores, axis=-1, keepdims=True))
    attention = powered / jnp.sum(powered, axis=-1, keepdims=True)
    attended = matmul(attention.astype(BF16), values).astype(BF16)
    return (queries, key_rows, values, attention, attended)


def attend_back(queries, key_rows, values, attention, attended_grad, cosine, sine):
    scale = 1.0 / math.sqrt(queries.shape[1])
    values_grad = contract_rows(attention.astype(BF16), attended_grad)
    attention_grad = contract_cols(attended_grad, values)
    row_dots = jnp.sum(attention_grad * attention, axis=-1, keepdims=True)
    scores_grad = (attention * (attention_grad - row_dots)).astype(BF16)
    queries_grad = turn_head(matmul(scores_grad, key_rows) * scale, cosine, -sine)
    keys_grad = turn_head(contract_rows(scores_grad, queries) * scale, cosine, -sine)
    return jnp.concatenate([queries_grad, keys_grad, values_grad], axis=1).astype(BF16)


def fold_rows(values):
    return jnp.sum(values.reshape(values.shape[0] // 8, 8, values.shape[1]), axis=0)


def forward_kernel(
    n0, n1, wq, bq, wu, bu, wo, wd, cosine, sine, mask, out0, out1, normed, attended, active
):
    length = n0.shape[0]
    normed[:length] = n0[...]
    normed[length:] = n1[...]
    joined = matmul(normed[...], wq[...]) + bq[...]
    for s in range(2):
        rows = slice(s * length, (s + 1) * length)
        attended[rows] = attend(joined[rows], cosine[rows], sine[rows], mask[rows])[4]
    step = min(256, wu.shape[1])
    for at in range(0, wu.shape[1], step):
        hidden = matmul(normed[...], wu[:, at : at + step]) + bu[:, at : at + step]
        active[:, at : at + step] = (
            hidden * (0.5 * (1.0 + lax.erf(hidden * ROOT_HALF)))
        ).astype(BF16)
    for at in range(0, wo.shape[1], step):
        cols = slice(at, at + step)
        total = matmul(attended[...], wo[:, cols]) + matmul(active[...], wd[:, cols])
        out0[:, cols] = total[:length].astype(BF16)
        out1[:, cols] = total[length:].astype(BF16)


def both_kernel(chained, n0, n1, g0, g1, wq, bq, wu, bu, wo, wd, cosine, sine, mask, *refs):
    refs = refs[6:] if chained else refs
    qkv, attention, attended, active, slope, joined_grad, s0, s1, normed, upstream, hidden_grad = (
        refs
    )
    length = n0.shape[0]
    size = wo.shape[0]
    normed[:length] = n0[...]
    normed[length:] = n1[...]
    upstream[:length] = g0[...]
    upstream[length:] = g1[...]
    joined = matmul(normed[...], wq[...]) + bq[...]
    attended_grad = contract_cols(upstream[...], wo[...]).astype(BF16)
    for s in range(2):
        rows = slice(s * length, (s + 1) * length)
        queries, key_rows, values, weights, result = attend(
            joined[rows], cosine[rows], sine[rows], mask[rows]
        )
        qkv[rows, :size] = queries
        qkv[rows, size : 2 * size] = key_rows
        qkv[rows, 2 * size :] = values
        attention[rows] = weights
        attended[rows] = result
        joined_grad[rows] = attend_back(
            queries, key_rows, values, weights, attended_grad[rows], cosine[rows], sine[rows]
        )
    step = min(256, wu.shape[1])
    for at in range(0, wu.shape[1], step):
        cols = slice(at, at + step)
        hidden = matmul(normed[...], wu[:, cols]) + bu[:, cols]
        active_grad = contract_cols(upstream[...], wd[cols])
        normal_cdf = 0.5 * (1.0 + lax.erf(hidden * ROOT_HALF))
        normal_pdf = jnp.exp(-0.5 * hidden * hidden) * DENSITY_SCALE
        active[:, cols] = (hidden * normal_cdf).astype(BF16)
        change = normal_cdf + hidden * normal_pdf
        slope[:, cols] = change.astype(BF16)
        hidden_grad[:, cols] = (active_grad * change).astype(BF16)
    for at in range(0, wq.shape[0], step):
        rows = slice(at, at + step)
        total = contract_cols(joined_grad[...], wq[rows]) + contract_cols(
            hidden_grad[...], wu[rows]
        )
        s0[:, rows] = total[:length].astype(BF16)
        s1[:, rows] = total[length:].astype(BF16)


def backward_kernel(
    chained, n0, n1, g0, g1, wq, wu, wo, wd, cosine, sine, qkv, attention, slope, *refs
):
    refs = refs[2:] if chained else refs
    joined_grad, hidden_grad, norm_sums, joined_sum, hidden_sum, s0, s1, normed, upstream = refs
    length = n0.shape[0]
    size = wo.shape[0]
    normed[:length] = n0[...]
    normed[length:] = n1[...]
    upstream[:length] = g0[...]
    upstream[length:] = g1[...]
    attended_grad = contract_cols(upstream[...], wo[...]).astype(BF16)
    for s in range(2):
        rows = slice(s * length, (s + 1) * length)
        joined_grad[rows] = attend_back(
            qkv[rows, :size],
            qkv[rows, size : 2 * size],
            qkv[rows, 2 * size :],
            attention[rows],
            attended_grad[rows],
            cosine[rows],
            sine[rows],
        )
    joined_sum[...] = fold_rows(joined_grad[...].astype(F32))
    step = min(256, wu.shape[1])
    for at in range(0, wu.shape[1], step):
        cols = slice(at, at + step)
        active_grad = contract_cols(upstream[...], wd[cols])
        grad = (active_grad * slope[:, cols].astype(F32)).astype(BF16)
        hidden_grad[:, cols] = grad
        hidden_sum[:, cols] = fold_rows(grad.astype(F32))
    for at in range(0, wq.shape[0], step):
        rows = slice(at, at + step)
        first = contract_cols(joined_grad[...], wq[rows])
        second = contract_cols(hidden_grad[...], wu[rows])
        part = normed[:, rows].astype(F32)
        norm_sums[0:8, rows] = fold_rows(first * part)
        norm_sums[8:16, rows] = fold_rows(second * part)
        norm_sums[16:24, rows] = fold_rows(first)
        norm_sums[24:32, rows] = fold_rows(second)
        total = first + second
        s0[:, rows] = total[:length].astype(BF16)
        s1[:, rows] = total[length:].astype(BF16)


def whole_spec(array):
    return pl.BlockSpec(
        array.shape, lambda i: (0,) * array.ndim, pipeline_mode=pl.Buffered(buffer_count=1)
    )


def rows_spec(array, count, pair):
    return pl.BlockSpec((count, array.shape[1]), lambda i: (pair, 0))


def call_pair(kernel, whole, by_rows, chain, outs_by_rows, outs_whole, scratch, pair, rows, flops):
    pair_rows = 2 * rows
    out_shape = list(outs_by_rows) + list(outs_whole)
    out_specs = [rows_spec(item, pair_rows, pair) for item in outs_by_rows] + [
        pl.BlockSpec(item.shape, lambda i: (0, 0)) for item in outs_whole
    ]
    operands = list(whole) + list(by_rows)
    in_specs = [whole_spec(item) for item in whole] + [
        rows_spec(item, pair_rows, pair) for item in by_rows
    ]
    aliases = {}
    if chain is not None:
        for at, item in enumerate(chain):
            aliases[len(operands)] = at
            operands.append(item)
            in_specs.append(pl.BlockSpec(memory_space=pl.ANY))
    moved = sum(item.size * item.dtype.itemsize for item in operands[: len(whole)])
    return pl.pallas_call(
        kernel,
        grid=(1,),
        out_shape=out_shape,
        in_specs=in_specs,
        out_specs=out_specs,
        scratch_shapes=scratch,
        input_output_aliases=aliases,
        cost_estimate=pl.CostEstimate(flops=flops, bytes_accessed=moved, transcendentals=0),
        compiler_params=pltpu.CompilerParams(vmem_limit_bytes=40 * 1024 * 1024),
    )(*operands)


def on_device(
    layout,
    tokens,
    segments,
    cotangent,
    norm_gain,
    norm_bias,
    qkv_weight,
    qkv_bias,
    out_weight,
    out_bias,
    up_weight,
    up_bias,
    down_weight,
    down_bias,
):
    layout.place()
    first_section = lax.axis_index("section") == 0
    cores, chips, chip, core = layout.cores, layout.chips, layout.chip, layout.core
    length = segments.shape[1]
    width = tokens.shape[1]
    core_heads, joined_size = qkv_weight.shape[2:]
    head_size = joined_size // 3
    hidden_part = up_weight.shape[2] // chips
    hidden_size = cores * hidden_part
    row_count = chips * length

    def core_rows(block):
        return lax.dynamic_slice_in_dim(block, core * length, length, 0)

    gains = norm_gain[0].astype(F32)
    shifts = norm_bias[0].astype(F32)
    own_tokens = core_rows(tokens).astype(F32)
    own_cotangent = core_rows(cotangent)
    own_normed, _ = normalize(own_tokens)
    gathered = layout.ring_gather(
        jnp.where(first_section, own_normed.astype(BF16), own_cotangent)
    )

    ring = jnp.array(layout.ring, jnp.int32)
    ring_place = jnp.array([layout.ring.index(c) for c in range(chips)], jnp.int32)
    slots = jnp.array(layout.slots, jnp.int32)
    chip_of = ring[(ring_place[chip] + slots) % chips]
    all_segments = layout.gather_chips(segments)
    all_segments = lax.dynamic_index_in_dim(all_segments, core, 1, keepdims=False)
    chosen = (chip_of ^ chip)[:, None] == jnp.arange(chips)[None, :]
    own_segments = jnp.sum(jnp.where(chosen[:, :, None], all_segments[None], 0), axis=1)
    cosine, sine, mask = sequence_tables(own_segments)

    shard = qkv_weight.shape[1]
    at = lax.axis_index("dp") * shard
    gain_rows = lax.dynamic_slice_in_dim(gains, at, shard, 1)
    shift_rows = lax.dynamic_slice_in_dim(shifts, at, shard, 1)
    qkv_scaled = qkv_weight[0].reshape(shard, core_heads * joined_size).astype(F32)
    qkv_scaled = layout.gather_groups((qkv_scaled * gain_rows[0][:, None]).astype(BF16), 0)
    up_scaled = (up_weight[0].astype(F32) * gain_rows[1][:, None]).astype(BF16)
    out_shard = layout.gather_groups(out_weight[0], 1)
    wq = layout.heads_out(
        lambda head: lax.dynamic_slice_in_dim(qkv_scaled, head * joined_size, joined_size, 1)
    )
    wo = layout.heads_out(
        lambda head: lax.dynamic_index_in_dim(out_shard, head, 0, keepdims=False)
    )
    wu = layout.columns_out(layout.gather_groups(up_scaled, 0))
    down_own = layout.gather_groups(down_weight[0], 0)
    wd = jnp.concatenate([down_own, layout.other_core(down_own)], axis=0)

    joined_biases = qkv_bias[0].astype(F32)
    joined_biases = layout.by_core(joined_biases, layout.other_core(joined_biases))
    bq = lax.dynamic_index_in_dim(joined_biases, chip, 0, keepdims=True)
    bu = up_bias[0].astype(F32)[None]
    bu = jnp.concatenate(
        [
            lax.dynamic_slice_in_dim(item, chip * hidden_part, hidden_part, 1)
            for item in (bu, layout.other_core(bu))
        ],
        axis=1,
    )
    ratio = (shifts / gains).astype(BF16)
    bq = bq + matmul(ratio[:1], wq)
    bu = bu + matmul(ratio[1:], wu)
    row_bias = (out_bias[0].astype(F32) + down_bias[0].astype(F32))[None]

    piece = jax.ShapeDtypeStruct((length, width), BF16)
    pair_piece = pltpu.VMEM((2 * length, width), BF16)

    def by_rows(cols, dtype):
        return jax.ShapeDtypeStruct((row_count, cols), dtype)

    matrix_flops = 4 * length * width * (joined_size + head_size + 2 * hidden_size)

    def pair_slots(pair):
        return layout.slots[2 * pair], layout.slots[2 * pair + 1]

    def norm_back(upstream, scaled, normed, inverse):
        return upstream.astype(F32) + inverse * (
            scaled
            - jnp.mean(scaled, axis=-1, keepdims=True)
            - normed * jnp.mean(scaled * normed, axis=-1, keepdims=True)
        )

    pieces = {}
    for pair in range(chips // 2 - 1, -1, -1):
        one, two = pair_slots(pair)
        pieces[one], pieces[two] = call_pair(
            forward_kernel,
            (gathered[one], gathered[two], wq, bq, wu, bu, wo, wd),
            (cosine, sine, mask),
            None,
            (),
            (piece, piece),
            [
                pair_piece,
                pltpu.VMEM((2 * length, head_size), BF16),
                pltpu.VMEM((2 * length, hidden_size), BF16),
            ],
            pair,
            length,
            matrix_flops,
        )
    branch_rows = layout.ring_scatter(pieces, (0,))
    first_out = (own_tokens + branch_rows + row_bias).astype(BF16)

    arrived = lax.ppermute(first_out, "section", [(0, 1)])
    layer_input = jnp.where(first_section, own_tokens, arrived.astype(F32))
    own_normed, own_inverse = normalize(layer_input)
    normed = layout.ring_gather(own_normed.astype(BF16))
    kept_shapes = (
        by_rows(joined_size, BF16),
        by_rows(length, F32),
        by_rows(head_size, BF16),
        by_rows(hidden_size, BF16),
        by_rows(hidden_size, BF16),
        by_rows(joined_size, BF16),
    )
    kept = None
    pieces = {}
    for pair in range(chips // 2):
        one, two = pair_slots(pair)
        *kept, pieces[one], pieces[two] = call_pair(
            functools.partial(both_kernel, kept is not None),
            (normed[one], normed[two], gathered[one], gathered[two], wq, bq, wu, bu, wo, wd),
            (cosine, sine, mask),
            kept,
            kept_shapes,
            (piece, piece),
            [pair_piece, pair_piece, pltpu.VMEM((2 * length, hidden_size), BF16)],
            pair,
            length,
            2 * matrix_flops,
        )
    qkv, attention, attended, active, slope, _ = kept
    scaled_rows = layout.ring_scatter(pieces, (1,))
    second_grad = norm_back(own_cotangent, scaled_rows, own_normed, own_inverse)

    arrived_grad = lax.ppermute(second_grad.astype(BF16), "section", [(1, 0)])
    own_upstream = jnp.where(first_section, arrived_grad, own_cotangent)
    upstream = layout.ring_gather(own_upstream)
    grads = None
    last_pieces = {}
    sums = []
    for pair in range(chips // 2):
        one, two = pair_slots(pair)
        *grads, norm_sums, joined_sum, hidden_sum, last_pieces[one], last_pieces[two] = call_pair(
            functools.partial(backward_kernel, grads is not None),
            (normed[one], normed[two], upstream[one], upstream[two], wq, wu, wo, wd),
            (cosine, sine, qkv, attention, slope),
            grads,
            (by_rows(joined_size, BF16), by_rows(hidden_size, BF16)),
            (
                jax.ShapeDtypeStruct((32, width), F32),
                jax.ShapeDtypeStruct((8, joined_size), F32),
                jax.ShapeDtypeStruct((8, hidden_size), F32),
                piece,
                piece,
            ),
            [pair_piece, pair_piece],
            pair,
            length,
            matrix_flops,
        )
        sums.append((norm_sums, joined_sum, hidden_sum))
    joined_grad, hidden_grad = grads

    normed_rows = jnp.concatenate([normed[slot] for slot in layout.slots], axis=0)
    upstream_rows = jnp.concatenate([upstream[slot] for slot in layout.slots], axis=0)

    def core_sum(own, other):
        return own + layout.other_core(other.astype(BF16)).astype(F32)

    def half(array, which):
        size = array.shape[1] // cores
        return lax.dynamic_slice_in_dim(array, which * size, size, 1)

    out_held = core_sum(
        contract_rows(half(attended, core), upstream_rows),
        contract_rows(half(attended, 1 - core), upstream_rows),
    ).astype(BF16)
    out_blocks = layout.heads_back(
        out_held,
        lambda blocks, head, block: lax.dynamic_update_slice_in_dim(blocks, block[None], head, 0),
        jnp.zeros((core_heads, out_held.shape[0] // core_heads, width), BF16),
    )
    out_weight_grad = layout.scatter_groups(out_blocks, 1)

    hidden_held = core_sum(
        contract_rows(normed_rows, hidden_grad[:, :hidden_part]),
        contract_rows(normed_rows, hidden_grad[:, hidden_part:]),
    ).astype(BF16)
    up_plain = layout.scatter_groups(layout.columns_back(hidden_held), 0)

    joined_held = core_sum(
        contract_rows(half(normed_rows, core), joined_grad),
        contract_rows(half(normed_rows, 1 - core), joined_grad),
    ).astype(BF16)
    joined_blocks = layout.heads_back(
        joined_held,
        lambda blocks, head, block: lax.dynamic_update_slice_in_dim(
            blocks, block, head * joined_size, 1
        ),
        jnp.zeros((joined_held.shape[0] // core_heads, core_heads * joined_size), BF16),
    )
    joined_plain = layout.scatter_groups(joined_blocks, 0)

    down_weight_grad = core_sum(
        contract_rows(active[:, :hidden_part], upstream_rows),
        contract_rows(active[:, hidden_part:], upstream_rows),
    )
    if layout.groups > 1:
        down_weight_grad = layout.scatter_groups(down_weight_grad, 0)

    norm_sums, joined_sum, hidden_sum = (
        functools.reduce(jnp.add, [item[k] for item in sums]) for k in range(3)
    )
    norm_sums = jnp.sum(norm_sums.reshape(2, 2, 8, width), axis=2) / gains
    joined_bias_all = lax.dynamic_update_slice(
        jnp.zeros((chips, joined_size), F32), jnp.sum(joined_sum, axis=0)[None], (chip, 0)
    )
    hidden_sum = jnp.sum(hidden_sum, axis=0)[None, None]
    hidden_bias_all = jnp.zeros((cores, chips, hidden_part), F32)
    hidden_bias_all = lax.dynamic_update_slice(
        hidden_bias_all, hidden_sum[:, :, :hidden_part], (core, chip, 0)
    )
    hidden_bias_all = lax.dynamic_update_slice(
        hidden_bias_all, hidden_sum[:, :, hidden_part:], (1 - core, chip, 0)
    )
    vectors = (
        norm_sums,
        joined_bias_all,
        jnp.sum(own_upstream, axis=0, dtype=F32),
        hidden_bias_all,
    )
    joint = layout.sum_all(jnp.concatenate([item.reshape(-1) for item in vectors]))
    summed, start = [], 0
    for item in vectors:
        summed.append(joint[start : start + item.size].reshape(item.shape))
        start += item.size
    norm_sums, joined_bias_all, out_bias_grad, hidden_bias_all = summed
    joined_bias_grad = lax.dynamic_slice_in_dim(joined_bias_all, core * core_heads, core_heads, 0)
    up_bias_grad = lax.dynamic_index_in_dim(hidden_bias_all, core, 0, keepdims=False).reshape(-1)

    up_weight_grad = up_plain * gain_rows[1][:, None] + shift_rows[1][:, None] * up_bias_grad
    joined_weight_grad = (
        joined_plain * gain_rows[0][:, None]
        + shift_rows[0][:, None] * joined_bias_grad.reshape(-1)
    ).reshape(shard, core_heads, joined_size)

    branch = matmul(attended, wo) + matmul(active, wd)
    pieces = {
        slot: branch[k * length : (k + 1) * length].astype(BF16)
        for k, slot in enumerate(layout.slots)
    }
    branch_rows = layout.ring_scatter(pieces, (1,))
    second_out = (layer_input + branch_rows + row_bias).astype(BF16)
    own_out = jnp.where(first_section, first_out, second_out)
    layer_outputs = layout.by_core(own_out, layout.other_core(own_out))

    scaled_rows = layout.ring_scatter(last_pieces, (0,))
    first_grad = norm_back(own_upstream, scaled_rows, own_normed, own_inverse)
    own_grad = jnp.where(first_section, first_grad, second_grad)
    input_gradients = layout.by_core(own_grad, layout.other_core(own_grad))

    return (
        layer_outputs[None],
        input_gradients[None],
        norm_sums[0][None],
        norm_sums[1][None],
        joined_weight_grad[None],
        joined_bias_grad[None],
        out_weight_grad[None],
        out_bias_grad[None],
        up_weight_grad[None],
        up_bias_grad[None],
        down_weight_grad[None],
        out_bias_grad[None],
    )


def solution(mesh):
    def whole(*arrays):
        layout = Layout(mesh, arrays[5].shape[2])

        def local(*blocks):
            return on_device(layout, *blocks)

        return jax.shard_map(
            local,
            mesh=mesh,
            in_specs=(
                P("dp", None),
                P("dp", None),
                P("dp", None),
                P("section", None, None),
                P("section", None, None),
                P("section", "dp", "tensor", None),
                P("section", "tensor", None),
                P("section", "tensor", "dp", None),
                P("section", None),
                P("section", "dp", "tensor"),
                P("section", "tensor"),
                P("section", ("tensor", "dp"), None),
                P("section", None),
            ),
            out_specs=(
                P("section", "dp", None),
                P("section", "dp", None),
                P("section", None, None),
                P("section", None, None),
                P("section", "dp", "tensor", None),
                P("section", "tensor", None),
                P("section", "tensor", "dp", None),
                P("section", None),
                P("section", "dp", "tensor"),
                P("section", "tensor"),
                P("section", ("tensor", "dp"), None),
                P("section", None),
            ),
            check_vma=False,
        )(*arrays)

    return whole
```

```python
import functools
import math

import jax
import jax.numpy as jnp
from jax import lax
from jax.experimental import pallas as pl
from jax.experimental.layout import Layout as Format
from jax.experimental.layout import with_layout_constraint
from jax.experimental.pallas import tpu as pltpu
from jax.sharding import PartitionSpec as P

ROT = 64
LANES = 128
NORM_EPSILON = 1e-05
MASK_VALUE = -1e30
ROOT_HALF = 0.7071067811865476
DENSITY_SCALE = 0.3989422804014327
F32 = jnp.float32
BF16 = jnp.bfloat16
VMEM_BYTES = 24 * 1024 * 1024


def contract_rows(left_side, right_side):
    return lax.dot_general(
        left_side, right_side, (((0,), (0,)), ((), ())), preferred_element_type=F32
    )


def contract_cols(left_side, right_side):
    return lax.dot_general(
        left_side, right_side, (((1,), (1,)), ((), ())), preferred_element_type=F32
    )


def matmul(left_side, right_side):
    return jnp.dot(left_side, right_side, preferred_element_type=F32)


def normalize(values):
    centered = values - jnp.mean(values, axis=-1, keepdims=True)
    inverse = lax.rsqrt(jnp.mean(centered * centered, axis=-1, keepdims=True) + NORM_EPSILON)
    return (centered * inverse, inverse)


def sequence_tables(segments):
    places = jnp.arange(segments.shape[1], dtype=jnp.int32)
    same_doc = segments[:, :, None] == segments[:, None, :]
    earlier = places[None, :] < places[:, None]
    position = jnp.sum(jnp.where(same_doc & earlier, 1, 0).astype(jnp.int32), axis=2)
    allowed = same_doc & (places[None, :] <= places[:, None])
    exponent = jnp.arange(ROT // 2, dtype=F32) * (2.0 / ROT)
    frequency = 10000.0 ** (-exponent)
    angles = position.astype(F32)[..., None] * frequency
    cosine, sine = jnp.cos(angles), jnp.sin(angles)
    rest = jnp.zeros(angles.shape[:2] + (LANES - ROT,), F32)
    count = segments.shape[0] * segments.shape[1]
    return (
        jnp.concatenate([cosine, cosine, rest + 1.0], axis=-1).reshape(count, LANES),
        jnp.concatenate([-sine, sine, rest], axis=-1).reshape(count, LANES),
        jnp.where(allowed, 0.0, MASK_VALUE).astype(F32).reshape(count, segments.shape[1]),
    )


class Layout:
    def __init__(self, mesh, heads):
        self.cores = mesh.shape["tensor"]
        self.dp = mesh.shape["dp"]
        self.chips = heads
        self.groups = self.dp // heads
        self.core_heads = heads // self.cores
        self.ring = list(range(0, heads, 2)) + list(range(heads - 1, 0, -2))
        self.slots = []
        for k in range(heads // 2):
            self.slots += [-k % heads, k + 1]

    def place(self):
        dp_index = lax.axis_index("dp")
        self.core = lax.axis_index("tensor")
        self.chip = dp_index // self.groups
        self.group = dp_index % self.groups

    def between_chips(self, block, target_of, sections=None):
        pairs = [
            (chip * self.groups + group, target_of(chip) * self.groups + group)
            for chip in range(self.chips)
            for group in range(self.groups)
        ]
        if sections is None:
            return lax.ppermute(block, "dp", pairs)
        pairs = [
            (section * self.dp + source, section * self.dp + target)
            for section in sections
            for source, target in pairs
        ]
        return lax.ppermute(block, ("section", "dp"), pairs)

    def ring_step(self, block, distance, sections=None):
        size = len(self.ring)

        def target_of(chip):
            return self.ring[(self.ring.index(chip) + distance) % size]

        return self.between_chips(block, target_of, sections)

    def between_groups(self, block, distance):
        pairs = [
            (chip * self.groups + group, chip * self.groups + (group + distance) % self.groups)
            for chip in range(self.chips)
            for group in range(self.groups)
        ]
        return lax.ppermute(block, "dp", pairs)

    def other_core(self, block):
        return lax.ppermute(block, "tensor", [(0, 1), (1, 0)])

    def by_core(self, own, other):
        first = self.core == 0
        return jnp.concatenate(
            [jnp.where(first, own, other), jnp.where(first, other, own)], axis=0
        )

    def gather_groups(self, block, axis):
        if self.groups == 1:
            return block
        size = block.shape[axis]
        shape = list(block.shape)
        shape[axis] = size * self.groups
        total = jnp.zeros(shape, block.dtype)
        for distance in range(self.groups):
            part = self.between_groups(block, distance) if distance else block
            source = (self.group - distance) % self.groups
            total = lax.dynamic_update_slice_in_dim(total, part, source * size, axis)
        return total

    def scatter_groups(self, block, axis):
        if self.groups == 1:
            return block.astype(F32)
        size = block.shape[axis] // self.groups
        total = lax.dynamic_slice_in_dim(block, self.group * size, size, axis).astype(F32)
        for distance in range(1, self.groups):
            target = (self.group + distance) % self.groups
            part = lax.dynamic_slice_in_dim(block, target * size, size, axis)
            total = total + self.between_groups(part.astype(BF16), distance).astype(F32)
        return total

    def sum_all(self, block):
        block = block + self.other_core(block)
        mask = 1
        while mask < self.chips:
            block = block + self.between_chips(block, lambda chip: chip ^ mask)
            mask *= 2
        total = block
        for distance in range(1, self.groups):
            total = total + self.between_groups(block, distance)
        return total

    def ring_gather(self, parts, sections=None):
        half = self.chips // 2
        held = [{0: part} for part in parts]
        for step in range(1, half + 1):
            for at, slots in enumerate(held):
                down = half - at % 2
                if step <= down:
                    slots[step] = self.ring_step(slots[step - 1], -1, sections)
                if step <= self.chips - 1 - down:
                    slots[self.chips - step] = self.ring_step(
                        slots[(self.chips - step + 1) % self.chips], 1, sections
                    )
        return {slot: [slots[slot] for slots in held] for slot in range(self.chips)}

    def ring_scatter(self, pieces, sections=None, waits=None):
        half = self.chips // 2
        totals = []
        for at in range(len(pieces[0])):
            parts = [pieces[slot][at] for slot in range(self.chips)]
            up = half - at % 2
            total = parts[0].astype(F32)
            for way, slots in (
                (1, range(up, 0, -1)),
                (-1, range(up + 1, self.chips)),
            ):
                moving = None
                for step, slot in enumerate(slots):
                    if moving is None:
                        moving = parts[slot]
                    else:
                        moving = (moving.astype(F32) + parts[slot].astype(F32)).astype(BF16)
                    if waits and step in waits:
                        moving = ordered(moving, *waits[step])
                    moving = self.ring_step(moving, way, sections)
                total = total + moving.astype(F32)
            totals.append(total)
        return totals

    def head_turn(self, chip, turn):
        return (chip % self.core_heads + turn) % self.core_heads

    def head_route(self, turn):
        pairs = []
        for core in range(self.cores):
            for chip in range(self.chips):
                target_core = chip // self.core_heads
                target = core * self.core_heads + self.head_turn(chip, turn)
                for group in range(self.groups):
                    pairs.append(
                        (
                            core * self.dp + chip * self.groups + group,
                            target_core * self.dp + target * self.groups + group,
                        )
                    )
        return pairs

    def send_head(self, block, turn):
        return lax.ppermute(block, ("tensor", "dp"), self.head_route(turn))

    def return_head(self, block, turn):
        pairs = [(target, source) for source, target in self.head_route(turn)]
        return lax.ppermute(block, ("tensor", "dp"), pairs)

    def swap(self, block, mask):
        return self.between_chips(block, lambda chip: chip ^ mask)


def ordered(block, *earlier):
    return lax.optimization_barrier((block,) + earlier)[0]


class Queue:
    def __init__(self, window, first=()):
        self.window = window
        self.results = [first] * window

    def ready(self, block):
        earlier = self.results[-self.window]
        return ordered(block, *earlier) if earlier else block

    def put(self, *result):
        self.results.append(result)


def turn_head(values, cosine, sine):
    first = values[:, :LANES]
    lane = lax.broadcasted_iota(jnp.int32, first.shape, 1)
    half = ROT // 2
    swapped = jnp.where(
        lane < half, pltpu.roll(first, LANES - half, 1), pltpu.roll(first, half, 1)
    )
    return jnp.concatenate([first * cosine + swapped * sine, values[:, LANES:]], axis=1)


def attend(joined, cosine, sine, mask):
    size = joined.shape[1] // 3
    queries = turn_head(joined[:, :size], cosine, sine).astype(BF16)
    key_rows = turn_head(joined[:, size : 2 * size], cosine, sine).astype(BF16)
    values = joined[:, 2 * size :].astype(BF16)
    scores = contract_cols(queries, key_rows) * (1.0 / math.sqrt(size)) + mask
    powered = jnp.exp(scores - jnp.max(scores, axis=-1, keepdims=True))
    attention = powered / jnp.sum(powered, axis=-1, keepdims=True)
    attended = matmul(attention.astype(BF16), values).astype(BF16)
    return (queries, key_rows, values, attention, attended)


def attend_back(queries, key_rows, values, attention, attended_grad, cosine, sine):
    scale = 1.0 / math.sqrt(queries.shape[1])
    values_grad = contract_rows(attention.astype(BF16), attended_grad)
    attention_grad = contract_cols(attended_grad, values)
    row_dots = jnp.sum(attention_grad * attention, axis=-1, keepdims=True)
    scores_grad = (attention * (attention_grad - row_dots)).astype(BF16)
    queries_grad = turn_head(matmul(scores_grad, key_rows) * scale, cosine, -sine)
    keys_grad = turn_head(contract_rows(scores_grad, queries) * scale, cosine, -sine)
    return jnp.concatenate([queries_grad, keys_grad, values_grad], axis=1).astype(BF16)


def fold_rows(values):
    return jnp.sum(values.reshape(values.shape[0] // 8, 8, values.shape[1]), axis=0)


def store_rows(refs, cols, values):
    rows = values.shape[0] // len(refs)
    for at, ref in enumerate(refs):
        ref[:, cols] = values[at * rows : (at + 1) * rows].astype(BF16)


def steps(size):
    step = min(256, size)
    return [slice(at, at + step) for at in range(0, size, step)]


def load_rows(refs, target, shift=0.0):
    rows = target.shape[0] // len(refs)
    for at, ref in enumerate(refs):
        values = ref[:rows]
        if not isinstance(shift, float):
            values = (values.astype(F32) + shift).astype(BF16)
        target[at * rows : (at + 1) * rows] = values


def split_heads(heads, wo):
    size = wo.shape[0]
    rows = heads.shape[0] // wo.shape[1] * size
    cols = heads.shape[1] - size
    part = size * rows // heads.shape[0]
    for at in range(0, heads.shape[0], rows):
        for k in range(rows // part):
            wo[at // rows * part : (at // rows + 1) * part, k * size : (k + 1) * size] = heads[
                at + k * part : at + (k + 1) * part, cols:
            ]
    return heads.at[:, :cols]


def forward_kernel(count, pieces, *refs):
    blocks, refs = refs[:count], refs[count:]
    heads, wu0, wu1, wd0, wd1, bq, bu, ratio, cosine, sine, mask = refs[:11]
    outs, refs = refs[11 : 11 + pieces], refs[11 + pieces :]
    first_norm, second_norm, attended, active, wo = refs
    wq = split_heads(heads, wo)
    length = mask.shape[1]
    part = wu0.shape[1]
    load_rows(blocks, first_norm, ratio[0:1])
    load_rows(blocks, second_norm, ratio[1:2])
    joined = matmul(first_norm[...], wq[...]) + bq[...]
    for s in range(mask.shape[0] // length):
        rows = slice(s * length, (s + 1) * length)
        attended[rows] = attend(joined[rows], cosine[rows], sine[rows], mask[rows])[4]
    for k, wu in enumerate((wu0, wu1)):
        for cols in steps(part):
            at = slice(k * part + cols.start, k * part + cols.stop)
            hidden = matmul(second_norm[...], wu[:, cols]) + bu[:, at]
            active[:, at] = (hidden * (0.5 * (1.0 + lax.erf(hidden * ROOT_HALF)))).astype(BF16)
    for cols in steps(wo.shape[1]):
        total = (
            matmul(attended[...], wo[:, cols])
            + matmul(active[:, :part], wd0[:, cols])
            + matmul(active[:, part:], wd1[:, cols])
        )
        store_rows(outs, cols, total)


def upstream_kernel(count, *refs):
    grads, refs = refs[:count], refs[count:]
    heads, wd0, wd1, attended_grad, active_grad, upstream, wo = refs
    split_heads(heads, wo)
    part = wd0.shape[0]
    load_rows(grads, upstream)
    attended_grad[...] = contract_cols(upstream[...], wo[...]).astype(BF16)
    for k, wd in enumerate((wd0, wd1)):
        for rows in steps(part):
            at = slice(k * part + rows.start, k * part + rows.stop)
            active_grad[:, at] = contract_cols(upstream[...], wd[rows]).astype(BF16)


def both_kernel(count, pieces, chained, *refs):
    blocks, refs = refs[:count], refs[count:]
    heads, wu0, wu1, bq, bu, ratio, cosine, sine, mask, attended_grad, active_grad = refs[:11]
    refs = refs[11 + chained :]
    first_norm, second_norm, qkv, attention, attended, active, slope = refs[:7]
    outs, (joined_grad, hidden_grad) = refs[7 : 7 + pieces], refs[7 + pieces :]
    length = mask.shape[1]
    size = attended_grad.shape[1]
    wq = heads.at[:, : 3 * size]
    part = wu0.shape[1]
    load_rows(blocks, first_norm, ratio[0:1])
    load_rows(blocks, second_norm, ratio[1:2])
    joined = matmul(first_norm[...], wq[...]) + bq[...]

    def attention_of(s):
        rows = slice(s * length, (s + 1) * length)
        queries, key_rows, values, weights, result = attend(
            joined[rows], cosine[rows], sine[rows], mask[rows]
        )
        qkv[rows, :size] = queries
        qkv[rows, size : 2 * size] = key_rows
        qkv[rows, 2 * size :] = values
        attention[rows] = weights
        attended[rows] = result
        joined_grad[rows] = attend_back(
            queries, key_rows, values, weights, attended_grad[rows], cosine[rows], sine[rows]
        )

    for k, wu in enumerate((wu0, wu1)):
        attention_of(k)
        for cols in steps(part):
            at = slice(k * part + cols.start, k * part + cols.stop)
            hidden = matmul(second_norm[...], wu[:, cols]) + bu[:, at]
            normal_cdf = 0.5 * (1.0 + lax.erf(hidden * ROOT_HALF))
            normal_pdf = jnp.exp(-0.5 * hidden * hidden) * DENSITY_SCALE
            active[:, at] = (hidden * normal_cdf).astype(BF16)
            change = normal_cdf + hidden * normal_pdf
            slope[:, at] = change.astype(BF16)
            hidden_grad[:, at] = (active_grad[:, at].astype(F32) * change).astype(BF16)
    for rows in steps(wq.shape[0]):
        total = (
            contract_cols(joined_grad[...], wq[rows])
            + contract_cols(hidden_grad[:, :part], wu0[rows])
            + contract_cols(hidden_grad[:, part:], wu1[rows])
        )
        store_rows(outs, rows, total)


def backward_kernel(count, pieces, chained, *refs):
    grads, refs = refs[:count], refs[count:]
    second, heads, wu0, wu1, wd0, wd1, cosine, sine = refs[:8]
    first_norm, second_norm, qkv, attention, attended, active, slope = refs[8:15]
    refs = refs[15 + chained :]
    upstream, joined_grad, hidden_grad, norm_sums, joined_sum, hidden_sum = refs[:6]
    outs, wo = refs[6 : 6 + pieces], refs[6 + pieces]
    wq = split_heads(heads, wo)
    length = attention.shape[1]
    size = wo.shape[0]
    part = wu0.shape[1]
    load_rows(grads, upstream)
    attended_grad = contract_cols(upstream[...], wo[...]).astype(BF16)
    for k, wd in enumerate((wd0, wd1)):
        rows = slice(k * length, (k + 1) * length)
        joined_grad[rows] = attend_back(
            qkv[rows, :size],
            qkv[rows, size : 2 * size],
            qkv[rows, 2 * size :],
            attention[rows],
            attended_grad[rows],
            cosine[rows],
            sine[rows],
        )
        for cols in steps(part):
            at = slice(k * part + cols.start, k * part + cols.stop)
            active_grad = contract_cols(upstream[...], wd[cols])
            grad = (active_grad * slope[:, at].astype(F32)).astype(BF16)
            hidden_grad[:, at] = grad
            hidden_sum[:, at] = fold_rows(grad.astype(F32))
    joined_sum[...] = fold_rows(joined_grad[...].astype(F32))
    for rows in steps(wq.shape[0]):
        first = contract_cols(joined_grad[...], wq[rows])
        other = contract_cols(hidden_grad[:, :part], wu0[rows]) + contract_cols(
            hidden_grad[:, part:], wu1[rows]
        )
        norm_sums[0:8, rows] = fold_rows(first * first_norm[:, rows].astype(F32))
        norm_sums[8:16, rows] = fold_rows(other * second_norm[:, rows].astype(F32))
        norm_sums[16:24, rows] = fold_rows(first)
        norm_sums[24:32, rows] = fold_rows(other)
        store_rows(outs, rows, first + other)

    @pl.when(second[0] != 0)
    def _():
        for cols in steps(wq.shape[0]):
            total = (
                matmul(attended[...], wo[:, cols])
                + matmul(active[:, :part], wd0[:, cols])
                + matmul(active[:, part:], wd1[:, cols])
            )
            store_rows(outs, cols, total)


def rows_spec(array, count, pair):
    return pl.BlockSpec((count, array.shape[1]), lambda i: (pair, 0))


def call_rows(
    kernel, whole, by_rows, chain, outs_by_rows, outs_whole, scratch, at, rows, flops
):
    out_shape = list(outs_by_rows) + list(outs_whole)
    out_specs = [rows_spec(item, rows, at) for item in outs_by_rows] + [
        pl.BlockSpec(item.shape, lambda i: (0, 0)) for item in outs_whole
    ]
    operands = [*whole, *by_rows]
    in_specs = [
        pl.BlockSpec(memory_space=pltpu.SMEM if item.ndim == 1 else pltpu.VMEM) for item in whole
    ] + [rows_spec(item, rows, at) for item in by_rows]
    aliases = {}
    for k, item in enumerate(chain or ()):
        aliases[len(operands)] = k
        operands.append(item)
        in_specs.append(pl.BlockSpec(memory_space=pl.ANY))
    return pl.pallas_call(
        kernel,
        grid=(1,),
        out_shape=out_shape,
        in_specs=in_specs,
        out_specs=out_specs,
        scratch_shapes=scratch,
        input_output_aliases=aliases,
        cost_estimate=pl.CostEstimate(flops=flops, bytes_accessed=rows * 8192, transcendentals=0),
        compiler_params=pltpu.CompilerParams(vmem_limit_bytes=VMEM_BYTES),
    )(*operands)


def on_device(
    layout,
    tokens,
    segments,
    cotangent,
    norm_gain,
    norm_bias,
    qkv_weight,
    qkv_bias,
    out_weight,
    out_bias,
    up_weight,
    up_bias,
    down_weight,
    down_bias,
):
    layout.place()
    first_section = lax.axis_index("section") == 0
    cores, chips, chip, core = layout.cores, layout.chips, layout.chip, layout.core
    length = segments.shape[1]
    width = tokens.shape[1]
    core_heads, joined_size = qkv_weight.shape[2:]
    head_size = joined_size // 3
    hidden_part = up_weight.shape[2] // chips
    hidden_size = cores * hidden_part
    row_count = chips * length

    def core_rows(block):
        return lax.dynamic_slice_in_dim(block, core * length, length, 0)

    def parts_of(rows, count=2):
        size = rows.shape[0] // count
        return [rows[k * size : (k + 1) * size] for k in range(count)]

    gains = norm_gain[0].astype(F32)
    shifts = norm_bias[0].astype(F32)
    own_tokens = core_rows(tokens).astype(F32)
    own_cotangent = core_rows(cotangent)
    own_normed, _ = normalize(own_tokens)

    own_segments = lax.dynamic_index_in_dim(segments, core, 0, keepdims=True).astype(BF16)
    own_segments = jnp.pad(own_segments, ((0, 15), (0, width - length)))
    first_block = jnp.where(first_section, own_normed.astype(BF16), own_cotangent)
    first_block = jnp.concatenate([first_block, own_segments], axis=0)
    gathered = layout.ring_gather([first_block])
    all_segments = jnp.concatenate(
        [gathered[slot][0][length : length + 1, :length] for slot in layout.slots], axis=0
    )
    cosine, sine, mask = sequence_tables(all_segments.astype(jnp.int32))

    shard = qkv_weight.shape[1]
    at = lax.axis_index("dp") * shard
    gain_rows = lax.dynamic_slice_in_dim(gains, at, shard, 1)
    qkv_scaled = qkv_weight[0].reshape(shard, core_heads * joined_size).astype(F32)
    qkv_scaled = layout.gather_groups((qkv_scaled * gain_rows[0][:, None]).astype(BF16), 0)
    up_scaled = (up_weight[0].astype(F32) * gain_rows[1][:, None]).astype(BF16)
    up_scaled = layout.gather_groups(up_scaled, 0)
    out_shard = layout.gather_groups(out_weight[0], 1)
    wd0 = layout.gather_groups(down_weight[0], 0)
    wd1 = layout.other_core(wd0)
    block_rows = qkv_scaled.shape[0]

    ratio = shifts / gains
    biases = jnp.concatenate([qkv_bias[0].reshape(-1), up_bias[0]]).astype(F32)[None]
    both = jnp.concatenate([biases, layout.other_core(biases)], axis=0)
    joined_biases = both[:, : core_heads * joined_size]
    joined_biases = jnp.where(
        chip // core_heads == core, joined_biases[0], joined_biases[1]
    ).reshape(core_heads, joined_size)
    bq = lax.dynamic_index_in_dim(joined_biases, chip % core_heads, 0, keepdims=True)
    bu = lax.dynamic_slice_in_dim(
        both, core_heads * joined_size + chip * hidden_part, hidden_part, 1
    ).reshape(1, hidden_size)

    hd_rows = out_shard.shape[1]
    head_blocks = []
    for turn in range(core_heads):
        head = layout.head_turn(chip, turn)
        out_part = lax.dynamic_index_in_dim(out_shard, head, 0, keepdims=False)
        out_part = out_part.reshape(hd_rows, width // head_size, head_size).transpose(1, 0, 2)
        head_blocks.append(
            jnp.concatenate(
                [
                    lax.dynamic_slice_in_dim(qkv_scaled, head * joined_size, joined_size, 1),
                    out_part.reshape(block_rows, head_size),
                ],
                axis=1,
            )
        )
    up_blocks = [
        lax.dynamic_slice_in_dim(up_scaled, (chip ^ up_mask) * hidden_part, hidden_part, 1)
        for up_mask in range(chips)
    ]
    queue = Queue(3)
    heads = jnp.zeros((core_heads * block_rows, joined_size + head_size), BF16)
    for turn, block in enumerate(head_blocks):
        if turn == 2:
            block = ordered(block, *up_blocks)
        block = layout.send_head(queue.ready(block), turn)
        slot = (chip - turn) % core_heads
        heads = lax.dynamic_update_slice_in_dim(heads, block, slot * block_rows, 0)
        queue.put(heads)
    wu0 = jnp.zeros((chips * block_rows, hidden_part), BF16)
    wu0 = lax.dynamic_update_slice_in_dim(wu0, up_blocks[0], chip * block_rows, 0)
    for up_mask in range(chips - 1, 0, -1):
        source = chip ^ up_mask
        block = queue.ready(up_blocks[up_mask])
        if up_mask == 1:
            block = ordered(block, cosine, sine, mask, bq, bu)
        block = layout.swap(block, up_mask)
        wu0 = lax.dynamic_update_slice_in_dim(wu0, block, source * block_rows, 0)
        queue.put(wu0)
    wu1 = layout.other_core(wu0)
    heads = layout.by_core(heads, layout.other_core(ordered(heads, up_blocks[1])))

    row_bias = (out_bias[0].astype(F32) + down_bias[0].astype(F32))[None]

    part_rows = length // 2
    piece = jax.ShapeDtypeStruct((part_rows, width), BF16)

    def by_rows(cols, dtype):
        return jax.ShapeDtypeStruct((row_count, cols), dtype)

    matrix_flops = 4 * length * width * (joined_size + head_size + 2 * hidden_size)

    def pair_blocks(blocks, pair):
        return blocks[layout.slots[2 * pair]] + blocks[layout.slots[2 * pair + 1]]

    def put_pieces(pieces, pair, blocks):
        pieces[layout.slots[2 * pair]] = blocks[:2]
        pieces[layout.slots[2 * pair + 1]] = blocks[2:]

    def norm_back(upstream, scaled, normed, inverse):
        return upstream.astype(F32) + inverse * (
            scaled
            - jnp.mean(scaled, axis=-1, keepdims=True)
            - normed * jnp.mean(scaled * normed, axis=-1, keepdims=True)
        )

    cotangent_blocks = [block for slot in layout.slots for block in gathered[slot]]
    attended_grad, active_grad = call_rows(
        functools.partial(upstream_kernel, len(cotangent_blocks)),
        (*cotangent_blocks, heads, wd0, wd1),
        (),
        None,
        (),
        [by_rows(head_size, BF16), by_rows(hidden_size, BF16)],
        [pltpu.VMEM((row_count, width), BF16), pltpu.VMEM((head_size, width), BF16)],
        0,
        row_count,
        2 * row_count * width * (head_size + hidden_size),
    )

    matrices = (heads, wu0, wu1, wd0, wd1)
    pieces = {}
    for at in (1, 0):
        slots = layout.slots[at * chips // 2 : (at + 1) * chips // 2]
        blocks = [block for slot in slots for block in gathered[slot]]
        rows = row_count // 2
        results = call_rows(
            functools.partial(forward_kernel, len(blocks), 2 * len(slots)),
            (*blocks, *matrices, bq, bu, ratio),
            (cosine, sine, mask),
            None,
            (),
            [piece] * (2 * len(slots)),
            [
                pltpu.VMEM((rows, width), BF16),
                pltpu.VMEM((rows, width), BF16),
                pltpu.VMEM((rows, head_size), BF16),
                pltpu.VMEM((rows, hidden_size), BF16),
                pltpu.VMEM((head_size, width), BF16),
            ],
            at,
            rows,
            2 * matrix_flops,
        )
        for k, slot in enumerate(slots):
            pieces[slot] = results[2 * k : 2 * k + 2]
    branch_rows = layout.ring_scatter(pieces)
    first_out = [
        (rows + branch + row_bias).astype(BF16)
        for rows, branch in zip(parts_of(own_tokens), branch_rows)
    ]

    layer_input = [
        jnp.where(first_section, rows, lax.ppermute(sent, "section", [(0, 1)]).astype(F32))
        for rows, sent in zip(parts_of(own_tokens), first_out)
    ]
    own_normed = [normalize(rows) for rows in layer_input]
    normed_blocks = layout.ring_gather([rows.astype(BF16) for rows, _ in own_normed])
    kept_shapes = (
        by_rows(width, BF16),
        by_rows(width, BF16),
        by_rows(joined_size, BF16),
        by_rows(length, F32),
        by_rows(head_size, BF16),
        by_rows(hidden_size, BF16),
        by_rows(hidden_size, BF16),
    )
    kept = None
    pieces = {}
    for pair in range(chips // 2):
        blocks = pair_blocks(normed_blocks, pair)
        results = call_rows(
            functools.partial(both_kernel, len(blocks), 4, len(kept_shapes) if kept else 0),
            (*blocks, heads, wu0, wu1, bq, bu, ratio),
            (cosine, sine, mask, attended_grad, active_grad),
            kept,
            kept_shapes,
            [piece] * 4,
            [
                pltpu.VMEM((2 * length, joined_size), BF16),
                pltpu.VMEM((2 * length, hidden_size), BF16),
            ],
            pair,
            2 * length,
            2 * matrix_flops,
        )
        kept = results[: len(kept_shapes)]
        put_pieces(pieces, pair, results[len(kept_shapes) :])
    first_norm, second_norm, qkv, attention, attended, active, slope = kept
    scaled_rows = layout.ring_scatter(pieces)
    second_grad = [
        norm_back(given, scaled, *norm)
        for given, scaled, norm in zip(parts_of(own_cotangent), scaled_rows, own_normed)
    ]

    arrived_grad = [
        lax.ppermute(rows.astype(BF16), "section", [(1, 0)]) for rows in second_grad
    ]
    own_upstream = [
        jnp.where(first_section, arrived, given)
        for arrived, given in zip(arrived_grad, parts_of(own_cotangent))
    ]
    upstream_blocks = layout.ring_gather(own_upstream)
    second_section = jnp.where(first_section, 0, 1).astype(jnp.int32).reshape(1)
    grad_shapes = (by_rows(width, BF16), by_rows(joined_size, BF16), by_rows(hidden_size, BF16))
    grads = None
    last_pieces = {}
    sums = []
    for pair in range(chips // 2):
        blocks = pair_blocks(upstream_blocks, pair)
        results = call_rows(
            functools.partial(
                backward_kernel, len(blocks), 4, len(grad_shapes) if grads else 0
            ),
            (*blocks, second_section, *matrices),
            (cosine, sine, first_norm, second_norm, qkv, attention, attended, active, slope),
            grads,
            grad_shapes,
            [
                jax.ShapeDtypeStruct((32, width), F32),
                jax.ShapeDtypeStruct((8, joined_size), F32),
                jax.ShapeDtypeStruct((8, hidden_size), F32),
            ]
            + [piece] * 4,
            [pltpu.VMEM((head_size, width), BF16)],
            pair,
            2 * length,
            matrix_flops,
        )
        grads = results[: len(grad_shapes)]
        sums.append(results[len(grad_shapes) : len(grad_shapes) + 3])
        for k in range(2):
            last_pieces[layout.slots[2 * pair + k]] = results[2 * k - 4 : 2 * k - 2 or None]
    upstream, joined_grad, hidden_grad = grads

    def half_of(array, which):
        size = array.shape[1] // cores
        return lax.dynamic_slice_in_dim(array, which * size, size, 1)

    row_major = Format(major_to_minor=(0, 1))

    def weight_grad(left_side, right_side):
        return with_layout_constraint(contract_rows(left_side, right_side), row_major)

    joined_given = weight_grad(half_of(first_norm, 1 - core), joined_grad).astype(BF16)
    out_given = weight_grad(half_of(attended, 1 - core), upstream).astype(BF16)
    hidden_given = weight_grad(second_norm, hidden_grad[:, hidden_part:]).astype(BF16)
    down_given = weight_grad(active[:, hidden_part:], upstream).astype(BF16)
    given = (joined_given, out_given, hidden_given, down_given)
    joined_taken, out_taken, hidden_taken, down_taken = (
        layout.other_core(item) for item in given
    )

    def core_sum(own, taken):
        return (own + taken.astype(F32)).astype(BF16)

    late_grad, late_attended = ordered(joined_grad, *given), ordered(attended, *given)
    joined_held = core_sum(weight_grad(half_of(first_norm, core), late_grad), joined_taken)
    out_held = core_sum(weight_grad(half_of(late_attended, core), upstream), out_taken)
    late_grad = ordered(hidden_grad, joined_held, out_held)
    hidden_held = core_sum(weight_grad(second_norm, late_grad[:, :hidden_part]), hidden_taken)

    own_given = jnp.concatenate(own_upstream, axis=0)
    norm_sums, joined_sum, hidden_sum = (
        functools.reduce(jnp.add, [item[k] for item in sums]) for k in range(3)
    )
    norm_sums = jnp.sum(norm_sums.reshape(2, 2, 8, width), axis=2)
    norm_sums = jnp.stack([norm_sums[0] - ratio * norm_sums[1], norm_sums[1]]) / gains
    joined_bias_all = lax.dynamic_update_slice(
        jnp.zeros((chips, joined_size), F32), jnp.sum(joined_sum, axis=0)[None], (chip, 0)
    )
    hidden_sum = jnp.sum(hidden_sum, axis=0)[None, None]
    hidden_bias_all = jnp.zeros((cores, chips, hidden_part), F32)
    hidden_bias_all = lax.dynamic_update_slice(
        hidden_bias_all, hidden_sum[:, :, :hidden_part], (core, chip, 0)
    )
    hidden_bias_all = lax.dynamic_update_slice(
        hidden_bias_all, hidden_sum[:, :, hidden_part:], (1 - core, chip, 0)
    )
    vectors = (
        norm_sums,
        joined_bias_all,
        jnp.sum(own_given, axis=0, dtype=F32),
        hidden_bias_all,
    )
    joint = layout.sum_all(
        ordered(jnp.concatenate([item.reshape(-1) for item in vectors]), *given)
    )
    summed, start = [], 0
    for item in vectors:
        summed.append(joint[start : start + item.size].reshape(item.shape))
        start += item.size
    norm_sums, joined_bias_all, out_bias_grad, hidden_bias_all = summed
    joined_bias_grad = lax.dynamic_slice_in_dim(joined_bias_all, core * core_heads, core_heads, 0)
    up_bias_grad = lax.dynamic_index_in_dim(hidden_bias_all, core, 0, keepdims=False).reshape(-1)

    (last_rows,) = layout.ring_scatter(
        {slot: [jnp.concatenate(parts, axis=0)] for slot, parts in last_pieces.items()},
        None,
        {1: (joined_held, out_held)},
    )
    last_normed, last_inverse = (
        jnp.concatenate([norm[k] for norm in own_normed], axis=0) for k in range(2)
    )
    first_grad = norm_back(own_given, last_rows, last_normed, last_inverse)
    own_grad = jnp.where(first_section, first_grad, jnp.concatenate(second_grad, axis=0))
    input_gradients = layout.by_core(own_grad, layout.other_core(own_grad))
    second_out = (jnp.concatenate(layer_input, axis=0) + last_rows + row_bias).astype(BF16)
    own_out = jnp.where(first_section, jnp.concatenate(first_out, axis=0), second_out)
    layer_outputs = layout.by_core(own_out, layout.other_core(own_out))

    up_weight_grad = jnp.zeros((shard, chips * hidden_part), F32)
    qkv_grad = jnp.zeros((shard, core_heads * joined_size), F32)
    out_weight_grad = jnp.zeros((core_heads, head_size // layout.dp, width), F32)
    head_blocks = []
    out_rows = out_held.shape[0] // core_heads
    for turn in range(core_heads):
        slot = (chip - turn) % core_heads
        out_part = lax.dynamic_slice_in_dim(out_held, slot * out_rows, out_rows, 0)
        out_part = out_part.reshape(out_rows, width // head_size, head_size).transpose(1, 0, 2)
        head_blocks.append(
            jnp.concatenate(
                [
                    lax.dynamic_slice_in_dim(joined_held, slot * block_rows, block_rows, 0),
                    out_part.reshape(block_rows, head_size),
                ],
                axis=1,
            )
        )
    queue = Queue(3)
    for turn, block in enumerate(head_blocks):
        head = layout.head_turn(chip, turn)
        if turn == 1:
            block = ordered(block, hidden_held, *head_blocks)
        block = layout.return_head(queue.ready(block), turn)
        out_block = block[:, joined_size:].reshape(width // head_size, out_rows, head_size)
        out_block = out_block.transpose(1, 0, 2).reshape(out_rows, width)
        out_block = layout.scatter_groups(out_block, 0)
        block = layout.scatter_groups(block[:, :joined_size], 0) * gain_rows[0][:, None]
        qkv_grad = lax.dynamic_update_slice_in_dim(qkv_grad, block, head * joined_size, 1)
        out_weight_grad = lax.dynamic_update_slice_in_dim(
            out_weight_grad, out_block[None], head, 0
        )
        queue.put(qkv_grad, out_weight_grad)
    joined_weight_grad = qkv_grad.reshape(shard, core_heads, joined_size)

    late_active = ordered(active, hidden_held)
    down_weight_grad = weight_grad(late_active[:, :hidden_part], upstream) + down_taken.astype(F32)
    if layout.groups > 1:
        down_weight_grad = layout.scatter_groups(down_weight_grad, 0)

    for up_mask in range(chips - 1, -1, -1):
        source = chip ^ up_mask
        block = lax.dynamic_slice_in_dim(hidden_held, source * block_rows, block_rows, 0)
        if up_mask:
            block = queue.ready(block)
            if up_mask == 3:
                block = ordered(block, down_weight_grad, joint)
            if up_mask == 1:
                block = ordered(block, last_rows, joined_weight_grad)
            block = layout.swap(block, up_mask)
        block = layout.scatter_groups(block, 0) * gain_rows[1][:, None]
        up_weight_grad = lax.dynamic_update_slice_in_dim(
            up_weight_grad, block, source * hidden_part, 1
        )
        queue.put(up_weight_grad)

    return (
        layer_outputs[None],
        input_gradients[None],
        norm_sums[0][None],
        norm_sums[1][None],
        joined_weight_grad[None],
        joined_bias_grad[None],
        out_weight_grad[None],
        out_bias_grad[None],
        up_weight_grad[None],
        up_bias_grad[None],
        down_weight_grad[None],
        out_bias_grad[None],
    )


def solution(mesh):
    def whole(*arrays):
        layout = Layout(mesh, arrays[5].shape[2])

        def local(*blocks):
            return on_device(layout, *blocks)

        return jax.shard_map(
            local,
            mesh=mesh,
            in_specs=(
                P("dp", None),
                P("dp", None),
                P("dp", None),
                P("section", None, None),
                P("section", None, None),
                P("section", "dp", "tensor", None),
                P("section", "tensor", None),
                P("section", "tensor", "dp", None),
                P("section", None),
                P("section", "dp", "tensor"),
                P("section", "tensor"),
                P("section", ("tensor", "dp"), None),
                P("section", None),
            ),
            out_specs=(
                P("section", "dp", None),
                P("section", "dp", None),
                P("section", None, None),
                P("section", None, None),
                P("section", "dp", "tensor", None),
                P("section", "tensor", None),
                P("section", "tensor", "dp", None),
                P("section", None),
                P("section", "dp", "tensor"),
                P("section", "tensor"),
                P("section", ("tensor", "dp"), None),
                P("section", None),
            ),
            check_vma=False,
        )(*arrays)

    return whole
```

```python
import functools
import math

import jax
import jax.numpy as jnp
from jax import lax
from jax.experimental import pallas as pl
from jax.experimental.layout import Layout as Format
from jax.experimental.layout import with_layout_constraint
from jax.experimental.pallas import tpu as pltpu
from jax.sharding import PartitionSpec as P

ROT = 64
LANES = 128
NORM_EPSILON = 1e-05
MASK_VALUE = -1e30
ROOT_HALF = 0.7071067811865476
DENSITY_SCALE = 0.3989422804014327
F32 = jnp.float32
BF16 = jnp.bfloat16
VMEM_BYTES = 24 * 1024 * 1024


def contract_rows(left_side, right_side):
    return lax.dot_general(
        left_side, right_side, (((0,), (0,)), ((), ())), preferred_element_type=F32
    )


def contract_cols(left_side, right_side):
    return lax.dot_general(
        left_side, right_side, (((1,), (1,)), ((), ())), preferred_element_type=F32
    )


def matmul(left_side, right_side):
    return jnp.dot(left_side, right_side, preferred_element_type=F32)


def normalize(values):
    centered = values - jnp.mean(values, axis=-1, keepdims=True)
    inverse = lax.rsqrt(jnp.mean(centered * centered, axis=-1, keepdims=True) + NORM_EPSILON)
    return (centered * inverse, inverse)


def sequence_tables(segments):
    places = jnp.arange(segments.shape[1], dtype=jnp.int32)
    same_doc = segments[:, :, None] == segments[:, None, :]
    earlier = places[None, :] < places[:, None]
    position = jnp.sum(jnp.where(same_doc & earlier, 1, 0).astype(jnp.int32), axis=2)
    allowed = same_doc & (places[None, :] <= places[:, None])
    exponent = jnp.arange(ROT // 2, dtype=F32) * (2.0 / ROT)
    frequency = 10000.0 ** (-exponent)
    angles = position.astype(F32)[..., None] * frequency
    cosine, sine = jnp.cos(angles), jnp.sin(angles)
    rest = jnp.zeros(angles.shape[:2] + (LANES - ROT,), F32)
    count = segments.shape[0] * segments.shape[1]
    return (
        jnp.concatenate([cosine, cosine, rest + 1.0], axis=-1).reshape(count, LANES),
        jnp.concatenate([-sine, sine, rest], axis=-1).reshape(count, LANES),
        jnp.where(allowed, 0.0, MASK_VALUE).astype(F32).reshape(count, segments.shape[1]),
    )


class Layout:
    def __init__(self, mesh, heads):
        self.cores = mesh.shape["tensor"]
        self.dp = mesh.shape["dp"]
        self.chips = heads
        self.groups = self.dp // heads
        self.core_heads = heads // self.cores
        self.ring = list(range(0, heads, 2)) + list(range(heads - 1, 0, -2))
        self.slots = []
        for k in range(heads // 2):
            self.slots += [-k % heads, k + 1]

    def place(self):
        dp_index = lax.axis_index("dp")
        self.core = lax.axis_index("tensor")
        self.chip = dp_index // self.groups
        self.group = dp_index % self.groups

    def between_chips(self, block, target_of, sections=None):
        pairs = [
            (chip * self.groups + group, target_of(chip) * self.groups + group)
            for chip in range(self.chips)
            for group in range(self.groups)
        ]
        if sections is None:
            return lax.ppermute(block, "dp", pairs)
        pairs = [
            (section * self.dp + source, section * self.dp + target)
            for section in sections
            for source, target in pairs
        ]
        return lax.ppermute(block, ("section", "dp"), pairs)

    def ring_step(self, block, distance, sections=None):
        size = len(self.ring)

        def target_of(chip):
            return self.ring[(self.ring.index(chip) + distance) % size]

        return self.between_chips(block, target_of, sections)

    def between_groups(self, block, distance):
        pairs = [
            (chip * self.groups + group, chip * self.groups + (group + distance) % self.groups)
            for chip in range(self.chips)
            for group in range(self.groups)
        ]
        return lax.ppermute(block, "dp", pairs)

    def other_core(self, block):
        return lax.ppermute(block, "tensor", [(0, 1), (1, 0)])

    def by_core(self, own, other):
        first = self.core == 0
        return jnp.concatenate(
            [jnp.where(first, own, other), jnp.where(first, other, own)], axis=0
        )

    def gather_groups(self, block, axis):
        if self.groups == 1:
            return block
        size = block.shape[axis]
        shape = list(block.shape)
        shape[axis] = size * self.groups
        total = jnp.zeros(shape, block.dtype)
        for distance in range(self.groups):
            part = self.between_groups(block, distance) if distance else block
            source = (self.group - distance) % self.groups
            total = lax.dynamic_update_slice_in_dim(total, part, source * size, axis)
        return total

    def scatter_groups(self, block, axis):
        if self.groups == 1:
            return block.astype(F32)
        size = block.shape[axis] // self.groups
        total = lax.dynamic_slice_in_dim(block, self.group * size, size, axis).astype(F32)
        for distance in range(1, self.groups):
            target = (self.group + distance) % self.groups
            part = lax.dynamic_slice_in_dim(block, target * size, size, axis)
            total = total + self.between_groups(part.astype(BF16), distance).astype(F32)
        return total

    def sum_steps(self, block):
        held = [block + self.other_core(block)]
        mask = 1
        while mask < self.chips:
            held.append(held[-1] + self.between_chips(held[-1], lambda chip: chip ^ mask))
            mask *= 2
        if self.groups > 1:
            total = held[-1]
            for distance in range(1, self.groups):
                total = total + self.between_groups(held[-1], distance)
            held.append(total)
        return held

    def ring_gather(self, parts, sections=None):
        half = self.chips // 2
        held = [{0: part} for part in parts]
        for step in range(1, half + 1):
            for at, slots in enumerate(held):
                down = half - at % 2
                if step <= down:
                    slots[step] = self.ring_step(slots[step - 1], -1, sections)
                if step <= self.chips - 1 - down:
                    slots[self.chips - step] = self.ring_step(
                        slots[(self.chips - step + 1) % self.chips], 1, sections
                    )
        return {slot: [slots[slot] for slots in held] for slot in range(self.chips)}

    def ring_scatter(self, pieces, sections=None, waits=None):
        half = self.chips // 2
        totals = []
        for at in range(len(pieces[0])):
            parts = [pieces[slot][at] for slot in range(self.chips)]
            up = half - at % 2
            total = parts[0].astype(F32)
            for way, slots in (
                (1, range(up, 0, -1)),
                (-1, range(up + 1, self.chips)),
            ):
                moving = None
                for step, slot in enumerate(slots):
                    if moving is None:
                        moving = parts[slot]
                    else:
                        moving = (moving.astype(F32) + parts[slot].astype(F32)).astype(BF16)
                    if waits and step in waits:
                        moving = ordered(moving, *waits[step])
                    moving = self.ring_step(moving, way, sections)
                total = total + moving.astype(F32)
            totals.append(total)
        return totals

    def head_turn(self, chip, turn):
        return (chip % self.core_heads + turn) % self.core_heads

    def head_route(self, turn):
        pairs = []
        for core in range(self.cores):
            for chip in range(self.chips):
                target_core = chip // self.core_heads
                target = core * self.core_heads + self.head_turn(chip, turn)
                for group in range(self.groups):
                    pairs.append(
                        (
                            core * self.dp + chip * self.groups + group,
                            target_core * self.dp + target * self.groups + group,
                        )
                    )
        return pairs

    def send_head(self, block, turn):
        return lax.ppermute(block, ("tensor", "dp"), self.head_route(turn))

    def return_head(self, block, turn):
        pairs = [(target, source) for source, target in self.head_route(turn)]
        return lax.ppermute(block, ("tensor", "dp"), pairs)

    def swap(self, block, mask):
        return self.between_chips(block, lambda chip: chip ^ mask)


def message_order(chips, core_heads):
    near = [("up", mask) for mask in range(chips // 2 - 1, 0, -1)]
    far = [("up", mask) for mask in range(chips - 1, chips // 2 - 1, -1)]
    heads = [("head", turn) for turn in range(core_heads)]
    order = []
    for k, head in enumerate(heads):
        order += [head] + near[k : k + 1]
    return order + near[len(heads) :] + far


def ordered(block, *earlier):
    return lax.optimization_barrier((block,) + earlier)[0]


class Queue:
    def __init__(self, window, first=()):
        self.window = window
        self.results = [first] * window

    def ready(self, block):
        earlier = self.results[-self.window]
        return ordered(block, *earlier) if earlier else block

    def put(self, *result):
        self.results.append(result)


def turn_head(values, cosine, sine):
    first = values[:, :LANES]
    lane = lax.broadcasted_iota(jnp.int32, first.shape, 1)
    half = ROT // 2
    swapped = jnp.where(
        lane < half, pltpu.roll(first, LANES - half, 1), pltpu.roll(first, half, 1)
    )
    return jnp.concatenate([first * cosine + swapped * sine, values[:, LANES:]], axis=1)


def attend(joined, cosine, sine, mask):
    size = joined.shape[1] // 3
    queries = turn_head(joined[:, :size], cosine, sine).astype(BF16)
    key_rows = turn_head(joined[:, size : 2 * size], cosine, sine).astype(BF16)
    values = joined[:, 2 * size :].astype(BF16)
    scores = contract_cols(queries, key_rows) * (1.0 / math.sqrt(size)) + mask
    powered = jnp.exp(scores - jnp.max(scores, axis=-1, keepdims=True))
    attention = powered / jnp.sum(powered, axis=-1, keepdims=True)
    attended = matmul(attention.astype(BF16), values).astype(BF16)
    return (queries, key_rows, values, attention, attended)


def attend_back(queries, key_rows, values, attention, attended_grad, cosine, sine):
    scale = 1.0 / math.sqrt(queries.shape[1])
    values_grad = contract_rows(attention.astype(BF16), attended_grad)
    attention_grad = contract_cols(attended_grad, values)
    row_dots = jnp.sum(attention_grad * attention, axis=-1, keepdims=True)
    scores_grad = (attention * (attention_grad - row_dots)).astype(BF16)
    queries_grad = turn_head(matmul(scores_grad, key_rows) * scale, cosine, -sine)
    keys_grad = turn_head(contract_rows(scores_grad, queries) * scale, cosine, -sine)
    return jnp.concatenate([queries_grad, keys_grad, values_grad], axis=1).astype(BF16)


def fold_rows(values):
    return jnp.sum(values.reshape(values.shape[0] // 8, 8, values.shape[1]), axis=0)


def store_rows(refs, cols, values):
    rows = values.shape[0] // len(refs)
    for at, ref in enumerate(refs):
        ref[:, cols] = values[at * rows : (at + 1) * rows].astype(BF16)


def steps(size):
    step = min(256, size)
    return [slice(at, at + step) for at in range(0, size, step)]


def load_rows(refs, target, shift=0.0):
    rows = target.shape[0] // len(refs)
    for at, ref in enumerate(refs):
        values = ref[:rows]
        if not isinstance(shift, float):
            values = (values.astype(F32) + shift).astype(BF16)
        target[at * rows : (at + 1) * rows] = values


def split_heads(heads, wo):
    size = wo.shape[0]
    rows = heads.shape[0] // wo.shape[1] * size
    cols = heads.shape[1] - size
    part = size * rows // heads.shape[0]
    for at in range(0, heads.shape[0], rows):
        for k in range(rows // part):
            wo[at // rows * part : (at // rows + 1) * part, k * size : (k + 1) * size] = heads[
                at + k * part : at + (k + 1) * part, cols:
            ]
    return heads.at[:, :cols]


def forward_kernel(count, pieces, *refs):
    blocks, refs = refs[:count], refs[count:]
    heads, wu0, wu1, wd0, wd1, bq, bu, ratio, cosine, sine, mask = refs[:11]
    outs, refs = refs[11 : 11 + pieces], refs[11 + pieces :]
    first_norm, second_norm, attended, active, wo = refs
    wq = split_heads(heads, wo)
    length = mask.shape[1]
    part = wu0.shape[1]
    load_rows(blocks, first_norm, ratio[0:1])
    load_rows(blocks, second_norm, ratio[1:2])
    joined = matmul(first_norm[...], wq[...]) + bq[...]
    for s in range(mask.shape[0] // length):
        rows = slice(s * length, (s + 1) * length)
        attended[rows] = attend(joined[rows], cosine[rows], sine[rows], mask[rows])[4]
    for k, wu in enumerate((wu0, wu1)):
        for cols in steps(part):
            at = slice(k * part + cols.start, k * part + cols.stop)
            hidden = matmul(second_norm[...], wu[:, cols]) + bu[:, at]
            active[:, at] = (hidden * (0.5 * (1.0 + lax.erf(hidden * ROOT_HALF)))).astype(BF16)
    for cols in steps(wo.shape[1]):
        total = (
            matmul(attended[...], wo[:, cols])
            + matmul(active[:, :part], wd0[:, cols])
            + matmul(active[:, part:], wd1[:, cols])
        )
        store_rows(outs, cols, total)


def upstream_kernel(count, *refs):
    grads, refs = refs[:count], refs[count:]
    heads, wd0, wd1, attended_grad, active_grad, upstream, wo = refs
    split_heads(heads, wo)
    part = wd0.shape[0]
    load_rows(grads, upstream)
    attended_grad[...] = contract_cols(upstream[...], wo[...]).astype(BF16)
    for k, wd in enumerate((wd0, wd1)):
        for rows in steps(part):
            at = slice(k * part + rows.start, k * part + rows.stop)
            active_grad[:, at] = contract_cols(upstream[...], wd[rows]).astype(BF16)


def both_kernel(count, pieces, chained, *refs):
    blocks, refs = refs[:count], refs[count:]
    heads, wu0, wu1, bq, bu, ratio, cosine, sine, mask, attended_grad, active_grad = refs[:11]
    refs = refs[11 + chained :]
    first_norm, second_norm, qkv, attention, attended, active, slope = refs[:7]
    outs, (joined_grad, hidden_grad) = refs[7 : 7 + pieces], refs[7 + pieces :]
    length = mask.shape[1]
    size = attended_grad.shape[1]
    wq = heads.at[:, : 3 * size]
    part = wu0.shape[1]
    load_rows(blocks, first_norm, ratio[0:1])
    load_rows(blocks, second_norm, ratio[1:2])
    joined = matmul(first_norm[...], wq[...]) + bq[...]

    def attention_of(s):
        rows = slice(s * length, (s + 1) * length)
        queries, key_rows, values, weights, result = attend(
            joined[rows], cosine[rows], sine[rows], mask[rows]
        )
        qkv[rows, :size] = queries
        qkv[rows, size : 2 * size] = key_rows
        qkv[rows, 2 * size :] = values
        attention[rows] = weights
        attended[rows] = result
        joined_grad[rows] = attend_back(
            queries, key_rows, values, weights, attended_grad[rows], cosine[rows], sine[rows]
        )

    for k, wu in enumerate((wu0, wu1)):
        attention_of(k)
        for cols in steps(part):
            at = slice(k * part + cols.start, k * part + cols.stop)
            hidden = matmul(second_norm[...], wu[:, cols]) + bu[:, at]
            normal_cdf = 0.5 * (1.0 + lax.erf(hidden * ROOT_HALF))
            normal_pdf = jnp.exp(-0.5 * hidden * hidden) * DENSITY_SCALE
            active[:, at] = (hidden * normal_cdf).astype(BF16)
            change = normal_cdf + hidden * normal_pdf
            slope[:, at] = change.astype(BF16)
            hidden_grad[:, at] = (active_grad[:, at].astype(F32) * change).astype(BF16)
    for rows in steps(wq.shape[0]):
        total = (
            contract_cols(joined_grad[...], wq[rows])
            + contract_cols(hidden_grad[:, :part], wu0[rows])
            + contract_cols(hidden_grad[:, part:], wu1[rows])
        )
        store_rows(outs, rows, total)


def backward_kernel(count, pieces, chained, *refs):
    grads, refs = refs[:count], refs[count:]
    second, heads, wu0, wu1, wd0, wd1, cosine, sine = refs[:8]
    first_norm, second_norm, qkv, attention, attended, active, slope = refs[8:15]
    refs = refs[15 + chained :]
    upstream, joined_grad, hidden_grad, norm_sums, joined_sum, hidden_sum = refs[:6]
    outs, wo = refs[6 : 6 + pieces], refs[6 + pieces]
    wq = split_heads(heads, wo)
    length = attention.shape[1]
    size = wo.shape[0]
    part = wu0.shape[1]
    load_rows(grads, upstream)
    attended_grad = contract_cols(upstream[...], wo[...]).astype(BF16)
    for k, wd in enumerate((wd0, wd1)):
        rows = slice(k * length, (k + 1) * length)
        joined_grad[rows] = attend_back(
            qkv[rows, :size],
            qkv[rows, size : 2 * size],
            qkv[rows, 2 * size :],
            attention[rows],
            attended_grad[rows],
            cosine[rows],
            sine[rows],
        )
        for cols in steps(part):
            at = slice(k * part + cols.start, k * part + cols.stop)
            active_grad = contract_cols(upstream[...], wd[cols])
            grad = (active_grad * slope[:, at].astype(F32)).astype(BF16)
            hidden_grad[:, at] = grad
            hidden_sum[:, at] = fold_rows(grad.astype(F32))
    joined_sum[...] = fold_rows(joined_grad[...].astype(F32))
    for rows in steps(wq.shape[0]):
        first = contract_cols(joined_grad[...], wq[rows])
        other = contract_cols(hidden_grad[:, :part], wu0[rows]) + contract_cols(
            hidden_grad[:, part:], wu1[rows]
        )
        norm_sums[0:8, rows] = fold_rows(first * first_norm[:, rows].astype(F32))
        norm_sums[8:16, rows] = fold_rows(other * second_norm[:, rows].astype(F32))
        norm_sums[16:24, rows] = fold_rows(first)
        norm_sums[24:32, rows] = fold_rows(other)
        store_rows(outs, rows, first + other)

    @pl.when(second[0] != 0)
    def _():
        for cols in steps(wq.shape[0]):
            total = (
                matmul(attended[...], wo[:, cols])
                + matmul(active[:, :part], wd0[:, cols])
                + matmul(active[:, part:], wd1[:, cols])
            )
            store_rows(outs, cols, total)


def sums_kernel(pairs, *refs):
    where, parts, (given, sums) = refs[0], refs[1 : 1 + 3 * pairs], refs[1 + 3 * pairs :]
    norm_sums, joined_sum, hidden_sum = (
        functools.reduce(jnp.add, [parts[3 * pair + k][...] for pair in range(pairs)])
        for k in range(3)
    )
    rows, width = sums.shape[0], given.shape[1]
    size = joined_sum.shape[1]
    chip, core = where[0], where[1]
    upstream = jnp.sum(given[...].astype(F32), axis=0, keepdims=True)
    for k in range(4):
        sums[k : k + 1, :width] = jnp.sum(norm_sums[8 * k : 8 * k + 8], axis=0, keepdims=True)
    sums[4:5, :width] = upstream
    sums[5:rows, :width] = jnp.zeros((rows - 5, width), F32)
    mine = lax.broadcasted_iota(jnp.int32, (rows, 1), 0) == chip
    joined = jnp.sum(joined_sum, axis=0, keepdims=True)
    sums[:, width : width + size] = jnp.where(mine, joined, 0.0)
    hidden = jnp.sum(hidden_sum, axis=0, keepdims=True)
    half = hidden.shape[1] // 2
    own, other = hidden[:, :half], hidden[:, half:]
    hidden = jnp.concatenate(
        [jnp.where(core == 0, own, other), jnp.where(core == 0, other, own)], axis=1
    )
    sums[:, width + size :] = jnp.where(mine, hidden, 0.0)


def heads_kernel(count, *refs):
    which, blocks, refs = refs[0], refs[1 : 1 + count], refs[1 + count :]
    gain, qkv_grad, out_grad, held, signals = refs
    copies = [
        pltpu.make_async_copy(block, held.at[which[k]], signals.at[k])
        for k, block in enumerate(blocks)
    ]
    for copy in copies:
        copy.start()
    for copy in copies:
        copy.wait()
    size = qkv_grad.shape[2]
    rows, width = out_grad.shape[1:]
    part = held.shape[2] - size
    for head in range(count):
        qkv_grad[:, head] = held[head, :, :size].astype(F32) * gain[...]
        for k in range(width // part):
            out_grad[head, :, k * part : (k + 1) * part] = held[
                head, k * rows : (k + 1) * rows, size:
            ].astype(F32)


def up_kernel(count, chained, *refs):
    which, blocks, refs = refs[0], refs[1 : 1 + count], refs[1 + count :]
    gain, refs = refs[0], refs[1 + chained :]
    up_grad, held, signals = refs
    size = blocks[0].shape[1]
    copies = []
    for k, block in enumerate(blocks):
        held[k] = block[...].astype(F32) * gain[...]
        place = pl.multiple_of(which[k] * size, size)
        copies.append(
            pltpu.make_async_copy(held.at[k], up_grad.at[:, pl.ds(place, size)], signals.at[k])
        )
        copies[-1].start()
    for copy in copies:
        copy.wait()


def rows_spec(array, count, pair):
    return pl.BlockSpec((count, array.shape[1]), lambda i: (pair, 0))


def call_rows(
    kernel, whole, by_rows, chain, outs_by_rows, outs_whole, scratch, at, rows, flops
):
    out_shape = list(outs_by_rows) + list(outs_whole)
    out_specs = [rows_spec(item, rows, at) for item in outs_by_rows] + [
        pl.BlockSpec(item.shape, lambda i: (0, 0)) for item in outs_whole
    ]
    operands = [*whole, *by_rows]
    in_specs = [
        pl.BlockSpec(memory_space=pltpu.SMEM if item.ndim == 1 else pltpu.VMEM) for item in whole
    ] + [rows_spec(item, rows, at) for item in by_rows]
    aliases = {}
    for k, item in enumerate(chain or ()):
        aliases[len(operands)] = k
        operands.append(item)
        in_specs.append(pl.BlockSpec(memory_space=pl.ANY))
    return pl.pallas_call(
        kernel,
        grid=(1,),
        out_shape=out_shape,
        in_specs=in_specs,
        out_specs=out_specs,
        scratch_shapes=scratch,
        input_output_aliases=aliases,
        cost_estimate=pl.CostEstimate(flops=flops, bytes_accessed=rows * 8192, transcendentals=0),
        compiler_params=pltpu.CompilerParams(vmem_limit_bytes=VMEM_BYTES),
    )(*operands)


def call_whole(kernel, operands, outs, scratch, outside=(), aliases=None):
    spaces = [
        pltpu.SMEM if item.dtype == jnp.int32 else pl.ANY if k in outside else pltpu.VMEM
        for k, item in enumerate([*operands, *outs])
    ]
    specs = [pl.BlockSpec(memory_space=space) for space in spaces]
    return pl.pallas_call(
        kernel,
        out_shape=outs,
        in_specs=specs[: len(operands)],
        out_specs=specs[len(operands) :],
        scratch_shapes=scratch,
        input_output_aliases=aliases or {},
        compiler_params=pltpu.CompilerParams(vmem_limit_bytes=VMEM_BYTES),
    )(*operands)


def on_device(
    layout,
    tokens,
    segments,
    cotangent,
    norm_gain,
    norm_bias,
    qkv_weight,
    qkv_bias,
    out_weight,
    out_bias,
    up_weight,
    up_bias,
    down_weight,
    down_bias,
):
    layout.place()
    first_section = lax.axis_index("section") == 0
    cores, chips, chip, core = layout.cores, layout.chips, layout.chip, layout.core
    length = segments.shape[1]
    width = tokens.shape[1]
    core_heads, joined_size = qkv_weight.shape[2:]
    head_size = joined_size // 3
    hidden_part = up_weight.shape[2] // chips
    hidden_size = cores * hidden_part
    row_count = chips * length

    def core_rows(block):
        return lax.dynamic_slice_in_dim(block, core * length, length, 0)

    def parts_of(rows, count=2):
        size = rows.shape[0] // count
        return [rows[k * size : (k + 1) * size] for k in range(count)]

    gains = norm_gain[0].astype(F32)
    shifts = norm_bias[0].astype(F32)
    own_tokens = core_rows(tokens).astype(F32)
    own_cotangent = core_rows(cotangent)
    own_normed, _ = normalize(own_tokens)

    own_segments = lax.dynamic_index_in_dim(segments, core, 0, keepdims=True).astype(BF16)
    own_segments = jnp.pad(own_segments, ((0, 15), (0, width - length)))
    first_block = jnp.where(first_section, own_normed.astype(BF16), own_cotangent)
    first_block = jnp.concatenate([first_block, own_segments], axis=0)
    gathered = layout.ring_gather([first_block])
    all_segments = jnp.concatenate(
        [gathered[slot][0][length : length + 1, :length] for slot in layout.slots], axis=0
    )
    cosine, sine, mask = sequence_tables(all_segments.astype(jnp.int32))

    shard = qkv_weight.shape[1]
    at = lax.axis_index("dp") * shard
    gain_rows = lax.dynamic_slice_in_dim(gains, at, shard, 1)
    qkv_scaled = qkv_weight[0].reshape(shard, core_heads * joined_size).astype(F32)
    qkv_scaled = layout.gather_groups((qkv_scaled * gain_rows[0][:, None]).astype(BF16), 0)
    up_scaled = (up_weight[0].astype(F32) * gain_rows[1][:, None]).astype(BF16)
    up_scaled = layout.gather_groups(up_scaled, 0)
    out_shard = layout.gather_groups(out_weight[0], 1)
    wd0 = layout.gather_groups(down_weight[0], 0)
    wd1 = layout.other_core(wd0)
    block_rows = qkv_scaled.shape[0]

    ratio = shifts / gains
    biases = jnp.concatenate([qkv_bias[0].reshape(-1), up_bias[0]]).astype(F32)[None]
    both = jnp.concatenate([biases, layout.other_core(biases)], axis=0)
    joined_biases = both[:, : core_heads * joined_size]
    joined_biases = jnp.where(
        chip // core_heads == core, joined_biases[0], joined_biases[1]
    ).reshape(core_heads, joined_size)
    bq = lax.dynamic_index_in_dim(joined_biases, chip % core_heads, 0, keepdims=True)
    bu = lax.dynamic_slice_in_dim(
        both, core_heads * joined_size + chip * hidden_part, hidden_part, 1
    ).reshape(1, hidden_size)

    hd_rows = out_shard.shape[1]
    head_blocks = []
    for turn in range(core_heads):
        head = layout.head_turn(chip, turn)
        out_part = lax.dynamic_index_in_dim(out_shard, head, 0, keepdims=False)
        out_part = out_part.reshape(hd_rows, width // head_size, head_size).transpose(1, 0, 2)
        head_blocks.append(
            jnp.concatenate(
                [
                    lax.dynamic_slice_in_dim(qkv_scaled, head * joined_size, joined_size, 1),
                    out_part.reshape(block_rows, head_size),
                ],
                axis=1,
            )
        )
    up_blocks = [
        lax.dynamic_slice_in_dim(up_scaled, (chip ^ up_mask) * hidden_part, hidden_part, 1)
        for up_mask in range(chips)
    ]
    queue = Queue(3)
    order = message_order(chips, core_heads)
    heads = jnp.zeros((core_heads * block_rows, joined_size + head_size), BF16)
    wu0 = jnp.zeros((chips * block_rows, hidden_part), BF16)
    wu0 = lax.dynamic_update_slice_in_dim(wu0, up_blocks[0], chip * block_rows, 0)
    for k, (kind, which) in enumerate(order):
        block = head_blocks[which] if kind == "head" else up_blocks[which]
        if k == 1:
            block = ordered(block, *head_blocks)
        if k == 3:
            block = ordered(block, *up_blocks)
        if k == len(order) - 1:
            block = ordered(block, cosine, sine, mask, bq, bu)
        block = queue.ready(block)
        if kind == "head":
            block = layout.send_head(block, which)
            slot = (chip - which) % core_heads
            heads = lax.dynamic_update_slice_in_dim(heads, block, slot * block_rows, 0)
        else:
            block = layout.swap(block, which)
            wu0 = lax.dynamic_update_slice_in_dim(wu0, block, (chip ^ which) * block_rows, 0)
        queue.put(block)
    wu1 = layout.other_core(wu0)
    heads = layout.by_core(heads, layout.other_core(heads))

    row_bias = (out_bias[0].astype(F32) + down_bias[0].astype(F32))[None]

    part_rows = length // 2
    piece = jax.ShapeDtypeStruct((part_rows, width), BF16)
    whole_piece = jax.ShapeDtypeStruct((length, width), BF16)

    def by_rows(cols, dtype):
        return jax.ShapeDtypeStruct((row_count, cols), dtype)

    matrix_flops = 4 * length * width * (joined_size + head_size + 2 * hidden_size)

    def pair_blocks(blocks, pair):
        return blocks[layout.slots[2 * pair]] + blocks[layout.slots[2 * pair + 1]]

    def put_pieces(pieces, pair, blocks):
        pieces[layout.slots[2 * pair]] = blocks[:2]
        pieces[layout.slots[2 * pair + 1]] = blocks[2:]

    def norm_back(upstream, scaled, normed, inverse):
        return upstream.astype(F32) + inverse * (
            scaled
            - jnp.mean(scaled, axis=-1, keepdims=True)
            - normed * jnp.mean(scaled * normed, axis=-1, keepdims=True)
        )

    cotangent_blocks = [block for slot in layout.slots for block in gathered[slot]]
    attended_grad, active_grad = call_rows(
        functools.partial(upstream_kernel, len(cotangent_blocks)),
        (*cotangent_blocks, heads, wd0, wd1),
        (),
        None,
        (),
        [by_rows(head_size, BF16), by_rows(hidden_size, BF16)],
        [pltpu.VMEM((row_count, width), BF16), pltpu.VMEM((head_size, width), BF16)],
        0,
        row_count,
        2 * row_count * width * (head_size + hidden_size),
    )

    matrices = (heads, wu0, wu1, wd0, wd1)
    pieces = {}
    for at in (1, 0):
        slots = layout.slots[at * chips // 2 : (at + 1) * chips // 2]
        blocks = [block for slot in slots for block in gathered[slot]]
        rows = row_count // 2
        results = call_rows(
            functools.partial(forward_kernel, len(blocks), 2 * len(slots)),
            (*blocks, *matrices, bq, bu, ratio),
            (cosine, sine, mask),
            None,
            (),
            [piece] * (2 * len(slots)),
            [
                pltpu.VMEM((rows, width), BF16),
                pltpu.VMEM((rows, width), BF16),
                pltpu.VMEM((rows, head_size), BF16),
                pltpu.VMEM((rows, hidden_size), BF16),
                pltpu.VMEM((head_size, width), BF16),
            ],
            at,
            rows,
            2 * matrix_flops,
        )
        for k, slot in enumerate(slots):
            pieces[slot] = results[2 * k : 2 * k + 2]
    branch_rows = layout.ring_scatter(pieces)
    first_out = [
        (rows + branch + row_bias).astype(BF16)
        for rows, branch in zip(parts_of(own_tokens), branch_rows)
    ]

    layer_input = [
        jnp.where(first_section, rows, lax.ppermute(sent, "section", [(0, 1)]).astype(F32))
        for rows, sent in zip(parts_of(own_tokens), first_out)
    ]
    own_normed = [normalize(rows) for rows in layer_input]
    normed_blocks = layout.ring_gather([rows.astype(BF16) for rows, _ in own_normed])
    kept_shapes = (
        by_rows(width, BF16),
        by_rows(width, BF16),
        by_rows(joined_size, BF16),
        by_rows(length, F32),
        by_rows(head_size, BF16),
        by_rows(hidden_size, BF16),
        by_rows(hidden_size, BF16),
    )
    kept = None
    pieces = {}
    for pair in range(chips // 2):
        blocks = pair_blocks(normed_blocks, pair)
        results = call_rows(
            functools.partial(both_kernel, len(blocks), 4, len(kept_shapes) if kept else 0),
            (*blocks, heads, wu0, wu1, bq, bu, ratio),
            (cosine, sine, mask, attended_grad, active_grad),
            kept,
            kept_shapes,
            [piece] * 4,
            [
                pltpu.VMEM((2 * length, joined_size), BF16),
                pltpu.VMEM((2 * length, hidden_size), BF16),
            ],
            pair,
            2 * length,
            2 * matrix_flops,
        )
        kept = results[: len(kept_shapes)]
        put_pieces(pieces, pair, results[len(kept_shapes) :])
    first_norm, second_norm, qkv, attention, attended, active, slope = kept
    scaled_rows = layout.ring_scatter(pieces)
    second_grad = [
        norm_back(given, scaled, *norm)
        for given, scaled, norm in zip(parts_of(own_cotangent), scaled_rows, own_normed)
    ]

    arrived_grad = [
        lax.ppermute(rows.astype(BF16), "section", [(1, 0)]) for rows in second_grad
    ]
    own_upstream = [
        jnp.where(first_section, arrived, given)
        for arrived, given in zip(arrived_grad, parts_of(own_cotangent))
    ]
    upstream_blocks = layout.ring_gather(own_upstream)
    second_section = jnp.where(first_section, 0, 1).astype(jnp.int32).reshape(1)
    grad_shapes = (by_rows(width, BF16), by_rows(joined_size, BF16), by_rows(hidden_size, BF16))
    grads = None
    last_pieces = {}
    sums = []
    for pair in range(chips // 2):
        blocks = pair_blocks(upstream_blocks, pair)
        results = call_rows(
            functools.partial(
                backward_kernel, len(blocks), 2, len(grad_shapes) if grads else 0
            ),
            (*blocks, second_section, *matrices),
            (cosine, sine, first_norm, second_norm, qkv, attention, attended, active, slope),
            grads,
            grad_shapes,
            [
                jax.ShapeDtypeStruct((32, width), F32),
                jax.ShapeDtypeStruct((8, joined_size), F32),
                jax.ShapeDtypeStruct((8, hidden_size), F32),
            ]
            + [whole_piece] * 2,
            [pltpu.VMEM((head_size, width), BF16)],
            pair,
            2 * length,
            matrix_flops,
        )
        grads = results[: len(grad_shapes)]
        sums.append(results[len(grad_shapes) : len(grad_shapes) + 3])
        for k in range(2):
            last_pieces[layout.slots[2 * pair + k]] = [results[k - 2]]
    upstream, joined_grad, hidden_grad = grads

    own_given = jnp.concatenate(own_upstream, axis=0)
    (local_sums,) = call_whole(
        functools.partial(sums_kernel, len(sums)),
        [jnp.stack([chip, core]), *[item for pair in sums for item in pair], own_given],
        [jax.ShapeDtypeStruct((chips, width + joined_size + hidden_size), F32)],
        [],
    )
    joint = layout.sum_steps(local_sums)

    def half_of(array, which):
        size = array.shape[1] // cores
        return lax.dynamic_slice_in_dim(array, which * size, size, 1)

    row_major = Format(major_to_minor=(0, 1))

    def weight_grad(left_side, right_side):
        return with_layout_constraint(contract_rows(left_side, right_side), row_major)

    joined_given = weight_grad(half_of(first_norm, 1 - core), joined_grad).astype(BF16)
    out_given = weight_grad(half_of(attended, 1 - core), upstream).astype(BF16)
    hidden_given = weight_grad(second_norm, hidden_grad[:, hidden_part:]).astype(BF16)
    joined_taken, out_taken, hidden_taken = (
        layout.other_core(item) for item in (joined_given, out_given, hidden_given)
    )

    def core_sum(own, taken):
        return (own + taken.astype(F32)).astype(BF16)

    late_grad, late_attended = (
        ordered(item, joint[0], joined_given, out_given, hidden_given)
        for item in (joined_grad, attended)
    )
    joined_held = core_sum(weight_grad(half_of(first_norm, core), late_grad), joined_taken)
    out_held = core_sum(weight_grad(half_of(late_attended, core), upstream), out_taken)
    late_grad = ordered(hidden_grad, joined_held, out_held)
    hidden_held = core_sum(weight_grad(second_norm, late_grad[:, :hidden_part]), hidden_taken)
    late_active = ordered(active, hidden_held)
    down_taken = layout.other_core(
        weight_grad(late_active[:, hidden_part:], upstream).astype(BF16)
    )

    whole_sums = joint[-1]
    norm_sums = whole_sums[:4, :width].reshape(2, 2, width)
    norm_sums = jnp.stack([norm_sums[0] - ratio * norm_sums[1], norm_sums[1]]) / gains
    out_bias_grad = whole_sums[4, :width]
    joined_bias_grad = lax.dynamic_slice_in_dim(
        whole_sums[:, width : width + joined_size], core * core_heads, core_heads, 0
    )
    up_bias_grad = lax.dynamic_slice_in_dim(
        whole_sums[:, width + joined_size :], core * hidden_part, hidden_part, 1
    ).reshape(-1)

    (last_rows,) = layout.ring_scatter(last_pieces, None, {1: (joined_held, out_held)})
    last_normed, last_inverse = (
        jnp.concatenate([norm[k] for norm in own_normed], axis=0) for k in range(2)
    )
    first_grad = norm_back(own_given, last_rows, last_normed, last_inverse)
    own_grad = jnp.where(first_section, first_grad, jnp.concatenate(second_grad, axis=0))
    input_gradients = layout.by_core(own_grad, layout.other_core(own_grad))
    second_out = (jnp.concatenate(layer_input, axis=0) + last_rows + row_bias).astype(BF16)
    own_out = jnp.where(first_section, jnp.concatenate(first_out, axis=0), second_out)
    layer_outputs = layout.by_core(own_out, layout.other_core(own_out))

    out_rows = out_held.shape[0] // core_heads
    share_rows = out_rows // layout.groups
    head_blocks = []
    for turn in range(core_heads):
        slot = (chip - turn) % core_heads
        out_part = lax.dynamic_slice_in_dim(out_held, slot * out_rows, out_rows, 0)
        out_part = out_part.reshape(layout.groups, share_rows, width // head_size, head_size)
        head_blocks.append(
            jnp.concatenate(
                [
                    lax.dynamic_slice_in_dim(joined_held, slot * block_rows, block_rows, 0),
                    out_part.transpose(0, 2, 1, 3).reshape(block_rows, head_size),
                ],
                axis=1,
            )
        )
    queue = Queue(3)
    gain_cols = gain_rows[:, :, None]
    blocks = {
        ("up", 0): lax.dynamic_slice_in_dim(hidden_held, chip * block_rows, block_rows, 0)
    }
    up_weight_grad = None
    for k, (kind, which) in enumerate(order):
        if kind == "head":
            block = head_blocks[which]
        else:
            block = lax.dynamic_slice_in_dim(
                hidden_held, (chip ^ which) * block_rows, block_rows, 0
            )
        if k == 0:
            block = ordered(block, joint[1], *head_blocks)
        if k == 2:
            block = ordered(block, joint[2])
        if k == 4:
            block = ordered(block, joint[-1])
        if k == len(order) - 3:
            block = ordered(block, down_weight_grad)
        if k == len(order) - 1:
            block = ordered(block, last_rows, joined_weight_grad)
        block = queue.ready(block)
        block = layout.return_head(block, which) if kind == "head" else layout.swap(block, which)
        queue.put(block)
        blocks[kind, which] = block
        if kind == "head" and which == core_heads - 1:
            heads_in = [blocks["head", turn] for turn in range(core_heads)]
            if layout.groups > 1:
                heads_in = [layout.scatter_groups(item, 0) for item in heads_in]
            joined_weight_grad, out_weight_grad = call_whole(
                functools.partial(heads_kernel, core_heads),
                [
                    jnp.stack([layout.head_turn(chip, turn) for turn in range(core_heads)]),
                    *heads_in,
                    gain_cols[0],
                ],
                [
                    jax.ShapeDtypeStruct((shard, core_heads, joined_size), F32),
                    jax.ShapeDtypeStruct((core_heads, share_rows, width), F32),
                ],
                [
                    pltpu.VMEM((core_heads, *heads_in[0].shape), heads_in[0].dtype),
                    pltpu.SemaphoreType.DMA((core_heads,)),
                ],
                range(1, 1 + core_heads),
            )
            down_weight_grad = weight_grad(
                late_active[:, :hidden_part], upstream
            ) + down_taken.astype(F32)
            if layout.groups > 1:
                down_weight_grad = layout.scatter_groups(down_weight_grad, 0)
        if k in (len(order) - 3, len(order) - 1):
            masks = [mask for mask in range(chips) if ("up", mask) in blocks]
            columns = [blocks.pop(("up", mask)) for mask in masks]
            if layout.groups > 1:
                columns = [layout.scatter_groups(item, 0) for item in columns]
            chain = [] if up_weight_grad is None else [up_weight_grad]
            (up_weight_grad,) = call_whole(
                functools.partial(up_kernel, len(columns), len(chain)),
                [jnp.stack([chip ^ mask for mask in masks]), *columns, gain_cols[1], *chain],
                [jax.ShapeDtypeStruct((shard, chips * hidden_part), F32)],
                [
                    pltpu.VMEM((len(columns), *columns[0].shape), F32),
                    pltpu.SemaphoreType.DMA((len(columns),)),
                ],
                range(len(columns) + 2, len(columns) + 3 + len(chain)),
                {len(columns) + 2: 0} if chain else None,
            )

    return (
        layer_outputs[None],
        input_gradients[None],
        norm_sums[0][None],
        norm_sums[1][None],
        joined_weight_grad[None],
        joined_bias_grad[None],
        out_weight_grad[None],
        out_bias_grad[None],
        up_weight_grad[None],
        up_bias_grad[None],
        down_weight_grad[None],
        out_bias_grad[None],
    )


def solution(mesh):
    def whole(*arrays):
        layout = Layout(mesh, arrays[5].shape[2])

        def local(*blocks):
            return on_device(layout, *blocks)

        return jax.shard_map(
            local,
            mesh=mesh,
            in_specs=(
                P("dp", None),
                P("dp", None),
                P("dp", None),
                P("section", None, None),
                P("section", None, None),
                P("section", "dp", "tensor", None),
                P("section", "tensor", None),
                P("section", "tensor", "dp", None),
                P("section", None),
                P("section", "dp", "tensor"),
                P("section", "tensor"),
                P("section", ("tensor", "dp"), None),
                P("section", None),
            ),
            out_specs=(
                P("section", "dp", None),
                P("section", "dp", None),
                P("section", None, None),
                P("section", None, None),
                P("section", "dp", "tensor", None),
                P("section", "tensor", None),
                P("section", "tensor", "dp", None),
                P("section", None),
                P("section", "dp", "tensor"),
                P("section", "tensor"),
                P("section", ("tensor", "dp"), None),
                P("section", None),
            ),
            check_vma=False,
        )(*arrays)

    return whole
```

```python
import functools
import math

import jax
import jax.numpy as jnp
from jax import lax
from jax.experimental import pallas as pl
from jax.experimental.layout import Layout as Format
from jax.experimental.layout import with_layout_constraint
from jax.experimental.pallas import tpu as pltpu
from jax.sharding import PartitionSpec as P

ROT = 64
LANES = 128
NORM_EPSILON = 1e-05
MASK_VALUE = -1e30
ROOT_HALF = 0.7071067811865476
DENSITY_SCALE = 0.3989422804014327
F32 = jnp.float32
BF16 = jnp.bfloat16
VMEM_BYTES = 24 * 1024 * 1024


def contract_rows(left_side, right_side):
    return lax.dot_general(
        left_side, right_side, (((0,), (0,)), ((), ())), preferred_element_type=F32
    )


def contract_cols(left_side, right_side):
    return lax.dot_general(
        left_side, right_side, (((1,), (1,)), ((), ())), preferred_element_type=F32
    )


def matmul(left_side, right_side):
    return jnp.dot(left_side, right_side, preferred_element_type=F32)


def normalize(values):
    centered = values - jnp.mean(values, axis=-1, keepdims=True)
    inverse = lax.rsqrt(jnp.mean(centered * centered, axis=-1, keepdims=True) + NORM_EPSILON)
    return (centered * inverse, inverse)


def sequence_tables(segments):
    places = jnp.arange(segments.shape[1], dtype=jnp.int32)
    same_doc = segments[:, :, None] == segments[:, None, :]
    earlier = places[None, :] < places[:, None]
    position = jnp.sum(jnp.where(same_doc & earlier, 1, 0).astype(jnp.int32), axis=2)
    allowed = same_doc & (places[None, :] <= places[:, None])
    exponent = jnp.arange(ROT // 2, dtype=F32) * (2.0 / ROT)
    frequency = 10000.0 ** (-exponent)
    angles = position.astype(F32)[..., None] * frequency
    cosine, sine = jnp.cos(angles), jnp.sin(angles)
    rest = jnp.zeros(angles.shape[:2] + (LANES - ROT,), F32)
    count = segments.shape[0] * segments.shape[1]
    return (
        jnp.concatenate([cosine, cosine, rest + 1.0], axis=-1).reshape(count, LANES),
        jnp.concatenate([-sine, sine, rest], axis=-1).reshape(count, LANES),
        jnp.where(allowed, 0.0, MASK_VALUE).astype(F32).reshape(count, segments.shape[1]),
    )


class Layout:
    def __init__(self, mesh, heads):
        self.cores = mesh.shape["tensor"]
        self.dp = mesh.shape["dp"]
        self.chips = heads
        self.groups = self.dp // heads
        self.core_heads = heads // self.cores
        self.ring = list(range(0, heads, 2)) + list(range(heads - 1, 0, -2))
        self.slots = []
        for k in range(heads // 2):
            self.slots += [-k % heads, k + 1]

    def place(self):
        dp_index = lax.axis_index("dp")
        self.core = lax.axis_index("tensor")
        self.chip = dp_index // self.groups
        self.group = dp_index % self.groups

    def between_chips(self, block, target_of, sections=None):
        pairs = [
            (chip * self.groups + group, target_of(chip) * self.groups + group)
            for chip in range(self.chips)
            for group in range(self.groups)
        ]
        if sections is None:
            return lax.ppermute(block, "dp", pairs)
        pairs = [
            (section * self.dp + source, section * self.dp + target)
            for section in sections
            for source, target in pairs
        ]
        return lax.ppermute(block, ("section", "dp"), pairs)

    def ring_step(self, block, distance, sections=None):
        size = len(self.ring)

        def target_of(chip):
            return self.ring[(self.ring.index(chip) + distance) % size]

        return self.between_chips(block, target_of, sections)

    def between_groups(self, block, distance):
        pairs = [
            (chip * self.groups + group, chip * self.groups + (group + distance) % self.groups)
            for chip in range(self.chips)
            for group in range(self.groups)
        ]
        return lax.ppermute(block, "dp", pairs)

    def other_core(self, block):
        return lax.ppermute(block, "tensor", [(0, 1), (1, 0)])

    def by_core(self, own, other):
        first = self.core == 0
        return jnp.concatenate(
            [jnp.where(first, own, other), jnp.where(first, other, own)], axis=0
        )

    def gather_groups(self, block, axis):
        if self.groups == 1:
            return block
        size = block.shape[axis]
        shape = list(block.shape)
        shape[axis] = size * self.groups
        total = jnp.zeros(shape, block.dtype)
        for distance in range(self.groups):
            part = self.between_groups(block, distance) if distance else block
            source = (self.group - distance) % self.groups
            total = lax.dynamic_update_slice_in_dim(total, part, source * size, axis)
        return total

    def scatter_groups(self, block, axis):
        if self.groups == 1:
            return block.astype(F32)
        size = block.shape[axis] // self.groups
        total = lax.dynamic_slice_in_dim(block, self.group * size, size, axis).astype(F32)
        for distance in range(1, self.groups):
            target = (self.group + distance) % self.groups
            part = lax.dynamic_slice_in_dim(block, target * size, size, axis)
            total = total + self.between_groups(part.astype(BF16), distance).astype(F32)
        return total

    def sum_steps(self, block):
        held = [block + self.other_core(block)]
        mask = 1
        while mask < self.chips:
            held.append(held[-1] + self.between_chips(held[-1], lambda chip: chip ^ mask))
            mask *= 2
        if self.groups > 1:
            total = held[-1]
            for distance in range(1, self.groups):
                total = total + self.between_groups(held[-1], distance)
            held.append(total)
        return held

    def ring_gather(self, parts, sections=None):
        half = self.chips // 2
        held = [{0: part} for part in parts]
        for step in range(1, half + 1):
            for at, slots in enumerate(held):
                down = half - at % 2
                if step <= down:
                    slots[step] = self.ring_step(slots[step - 1], -1, sections)
                if step <= self.chips - 1 - down:
                    slots[self.chips - step] = self.ring_step(
                        slots[(self.chips - step + 1) % self.chips], 1, sections
                    )
        return {slot: [slots[slot] for slots in held] for slot in range(self.chips)}

    def ring_scatter(self, pieces, sections=None, waits=None):
        half = self.chips // 2
        totals = []
        for at in range(len(pieces[0])):
            parts = [pieces[slot][at] for slot in range(self.chips)]
            up = half - at % 2
            total = parts[0].astype(F32)
            for way, slots in (
                (1, range(up, 0, -1)),
                (-1, range(up + 1, self.chips)),
            ):
                moving = None
                for step, slot in enumerate(slots):
                    if moving is None:
                        moving = parts[slot]
                    else:
                        moving = (moving.astype(F32) + parts[slot].astype(F32)).astype(BF16)
                    if waits and step in waits:
                        moving = ordered(moving, *waits[step])
                    moving = self.ring_step(moving, way, sections)
                total = total + moving.astype(F32)
            totals.append(total)
        return totals

    def head_turn(self, chip, turn):
        return (chip % self.core_heads) ^ turn

    def head_route(self, turn):
        pairs = []
        for core in range(self.cores):
            for chip in range(self.chips):
                target_core = chip // self.core_heads
                target = core * self.core_heads + self.head_turn(chip, turn)
                for group in range(self.groups):
                    pairs.append(
                        (
                            core * self.dp + chip * self.groups + group,
                            target_core * self.dp + target * self.groups + group,
                        )
                    )
        return pairs

    def send_head(self, block, turn):
        return lax.ppermute(block, ("tensor", "dp"), self.head_route(turn))

    def return_head(self, block, turn):
        pairs = [(target, source) for source, target in self.head_route(turn)]
        return lax.ppermute(block, ("tensor", "dp"), pairs)

    def swap(self, block, mask):
        return self.between_chips(block, lambda chip: chip ^ mask)


def message_order(chips, core_heads):
    near = [("up", mask) for mask in range(chips // 2 - 1, 0, -1)]
    far = [("up", mask) for mask in range(chips - 1, chips // 2 - 1, -1)]
    heads = [("head", turn) for turn in range(core_heads)]
    order = []
    for k, head in enumerate(heads):
        order += [head] + near[k : k + 1]
    return order + near[len(heads) :] + far


def ordered(block, *earlier):
    return lax.optimization_barrier((block,) + earlier)[0]


class Queue:
    def __init__(self, window, first=()):
        self.window = window
        self.results = [first] * window

    def ready(self, block):
        earlier = self.results[-self.window]
        return ordered(block, *earlier) if earlier else block

    def put(self, *result):
        self.results.append(result)


def turn_head(values, cosine, sine):
    first = values[:, :LANES]
    lane = lax.broadcasted_iota(jnp.int32, first.shape, 1)
    half = ROT // 2
    swapped = jnp.where(
        lane < half, pltpu.roll(first, LANES - half, 1), pltpu.roll(first, half, 1)
    )
    return jnp.concatenate([first * cosine + swapped * sine, values[:, LANES:]], axis=1)


def attend(joined, cosine, sine, mask):
    size = joined.shape[1] // 3
    queries = turn_head(joined[:, :size], cosine, sine).astype(BF16)
    key_rows = turn_head(joined[:, size : 2 * size], cosine, sine).astype(BF16)
    values = joined[:, 2 * size :].astype(BF16)
    scores = contract_cols(queries, key_rows) * (1.0 / math.sqrt(size)) + mask
    powered = jnp.exp(scores - jnp.max(scores, axis=-1, keepdims=True))
    attention = powered / jnp.sum(powered, axis=-1, keepdims=True)
    attended = matmul(attention.astype(BF16), values).astype(BF16)
    return (queries, key_rows, values, attention, attended)


def attend_back(queries, key_rows, values, attention, attended_grad, cosine, sine):
    scale = 1.0 / math.sqrt(queries.shape[1])
    values_grad = contract_rows(attention.astype(BF16), attended_grad)
    attention_grad = contract_cols(attended_grad, values)
    row_dots = jnp.sum(attention_grad * attention, axis=-1, keepdims=True)
    scores_grad = (attention * (attention_grad - row_dots)).astype(BF16)
    queries_grad = turn_head(matmul(scores_grad, key_rows) * scale, cosine, -sine)
    keys_grad = turn_head(contract_rows(scores_grad, queries) * scale, cosine, -sine)
    return jnp.concatenate([queries_grad, keys_grad, values_grad], axis=1).astype(BF16)


def fold_rows(values):
    return jnp.sum(values.reshape(values.shape[0] // 8, 8, values.shape[1]), axis=0)


def store_rows(refs, cols, values):
    rows = values.shape[0] // len(refs)
    for at, ref in enumerate(refs):
        ref[:, cols] = values[at * rows : (at + 1) * rows].astype(BF16)


def steps(size):
    step = min(256, size)
    return [slice(at, at + step) for at in range(0, size, step)]


def load_rows(refs, target, shift=0.0):
    rows = target.shape[0] // len(refs)
    for at, ref in enumerate(refs):
        values = ref[:rows]
        if not isinstance(shift, float):
            values = (values.astype(F32) + shift).astype(BF16)
        target[at * rows : (at + 1) * rows] = values


def split_heads(heads, wo):
    size = wo.shape[0]
    rows = heads.shape[0] // wo.shape[1] * size
    cols = heads.shape[1] - size
    part = size * rows // heads.shape[0]
    for at in range(0, heads.shape[0], rows):
        for k in range(rows // part):
            wo[at // rows * part : (at // rows + 1) * part, k * size : (k + 1) * size] = heads[
                at + k * part : at + (k + 1) * part, cols:
            ]
    return heads.at[:, :cols]


def forward_kernel(count, pieces, *refs):
    blocks, refs = refs[:count], refs[count:]
    heads, wu, wd, bq, bu, ratio, cosine, sine, mask = refs[:9]
    outs, refs = refs[9 : 9 + pieces], refs[9 + pieces :]
    first_norm, second_norm, attended, active, wo = refs
    wq = split_heads(heads, wo)
    length = mask.shape[1]
    load_rows(blocks, first_norm, ratio[0:1])
    load_rows(blocks, second_norm, ratio[1:2])
    joined = matmul(first_norm[...], wq[...]) + bq[...]
    for s in range(mask.shape[0] // length):
        rows = slice(s * length, (s + 1) * length)
        attended[rows] = attend(joined[rows], cosine[rows], sine[rows], mask[rows])[4]
    for cols in steps(wu.shape[1]):
        hidden = matmul(second_norm[...], wu[:, cols]) + bu[:, cols]
        active[:, cols] = (hidden * (0.5 * (1.0 + lax.erf(hidden * ROOT_HALF)))).astype(BF16)
    for cols in steps(wo.shape[1]):
        total = matmul(attended[...], wo[:, cols]) + matmul(active[...], wd[:, cols])
        store_rows(outs, cols, total)


def upstream_kernel(count, *refs):
    grads, refs = refs[:count], refs[count:]
    heads, wd, attended_grad, active_grad, upstream, wo = refs
    split_heads(heads, wo)
    load_rows(grads, upstream)
    attended_grad[...] = contract_cols(upstream[...], wo[...]).astype(BF16)
    for rows in steps(wd.shape[0]):
        active_grad[:, rows] = contract_cols(upstream[...], wd[rows]).astype(BF16)


def both_kernel(count, pieces, chained, *refs):
    blocks, refs = refs[:count], refs[count:]
    heads, wu, bq, bu, ratio, cosine, sine, mask, attended_grad, active_grad = refs[:10]
    refs = refs[10 + chained :]
    first_norm, second_norm, qkv, attention, attended, active, slope = refs[:7]
    outs, (joined_grad, hidden_grad) = refs[7 : 7 + pieces], refs[7 + pieces :]
    length = mask.shape[1]
    size = attended_grad.shape[1]
    wq = heads.at[:, : 3 * size]
    part = wu.shape[1] // 2
    load_rows(blocks, first_norm, ratio[0:1])
    load_rows(blocks, second_norm, ratio[1:2])
    joined = matmul(first_norm[...], wq[...]) + bq[...]

    def attention_of(s):
        rows = slice(s * length, (s + 1) * length)
        queries, key_rows, values, weights, result = attend(
            joined[rows], cosine[rows], sine[rows], mask[rows]
        )
        qkv[rows, :size] = queries
        qkv[rows, size : 2 * size] = key_rows
        qkv[rows, 2 * size :] = values
        attention[rows] = weights
        attended[rows] = result
        joined_grad[rows] = attend_back(
            queries, key_rows, values, weights, attended_grad[rows], cosine[rows], sine[rows]
        )

    for k in range(2):
        attention_of(k)
        for cols in steps(part):
            at = slice(k * part + cols.start, k * part + cols.stop)
            hidden = matmul(second_norm[...], wu[:, at]) + bu[:, at]
            normal_cdf = 0.5 * (1.0 + lax.erf(hidden * ROOT_HALF))
            normal_pdf = jnp.exp(-0.5 * hidden * hidden) * DENSITY_SCALE
            active[:, at] = (hidden * normal_cdf).astype(BF16)
            change = normal_cdf + hidden * normal_pdf
            slope[:, at] = change.astype(BF16)
            hidden_grad[:, at] = (active_grad[:, at].astype(F32) * change).astype(BF16)
    for rows in steps(wq.shape[0]):
        total = contract_cols(joined_grad[...], wq[rows]) + contract_cols(
            hidden_grad[...], wu[rows]
        )
        store_rows(outs, rows, total)


def backward_kernel(count, pieces, chained, *refs):
    grads, refs = refs[:count], refs[count:]
    second, heads, wu, wd, cosine, sine = refs[:6]
    first_norm, second_norm, qkv, attention, attended, active, slope = refs[6:13]
    refs = refs[13 + chained :]
    upstream, joined_grad, hidden_grad, norm_sums, joined_sum, hidden_sum = refs[:6]
    outs, wo = refs[6 : 6 + pieces], refs[6 + pieces]
    wq = split_heads(heads, wo)
    length = attention.shape[1]
    size = wo.shape[0]
    part = wu.shape[1] // 2
    load_rows(grads, upstream)
    attended_grad = contract_cols(upstream[...], wo[...]).astype(BF16)
    for k in range(2):
        rows = slice(k * length, (k + 1) * length)
        joined_grad[rows] = attend_back(
            qkv[rows, :size],
            qkv[rows, size : 2 * size],
            qkv[rows, 2 * size :],
            attention[rows],
            attended_grad[rows],
            cosine[rows],
            sine[rows],
        )
        for cols in steps(part):
            at = slice(k * part + cols.start, k * part + cols.stop)
            active_grad = contract_cols(upstream[...], wd[at])
            grad = (active_grad * slope[:, at].astype(F32)).astype(BF16)
            hidden_grad[:, at] = grad
            hidden_sum[:, at] = fold_rows(grad.astype(F32))
    joined_sum[...] = fold_rows(joined_grad[...].astype(F32))
    for rows in steps(wq.shape[0]):
        first = contract_cols(joined_grad[...], wq[rows])
        other = contract_cols(hidden_grad[...], wu[rows])
        norm_sums[0:8, rows] = fold_rows(first * first_norm[:, rows].astype(F32))
        norm_sums[8:16, rows] = fold_rows(other * second_norm[:, rows].astype(F32))
        norm_sums[16:24, rows] = fold_rows(first)
        norm_sums[24:32, rows] = fold_rows(other)
        store_rows(outs, rows, first + other)

    @pl.when(second[0] != 0)
    def _():
        for cols in steps(wq.shape[0]):
            total = matmul(attended[...], wo[:, cols]) + matmul(active[...], wd[:, cols])
            store_rows(outs, cols, total)


def sums_kernel(pairs, *refs):
    where, parts, (given, sums) = refs[0], refs[1 : 1 + 3 * pairs], refs[1 + 3 * pairs :]
    norm_sums, joined_sum, hidden_sum = (
        functools.reduce(jnp.add, [parts[3 * pair + k][...] for pair in range(pairs)])
        for k in range(3)
    )
    rows, width = sums.shape[0], given.shape[1]
    size = joined_sum.shape[1]
    chip, core = where[0], where[1]
    upstream = jnp.sum(given[...].astype(F32), axis=0, keepdims=True)
    for k in range(4):
        sums[k : k + 1, :width] = jnp.sum(norm_sums[8 * k : 8 * k + 8], axis=0, keepdims=True)
    sums[4:5, :width] = upstream
    sums[5:rows, :width] = jnp.zeros((rows - 5, width), F32)
    mine = lax.broadcasted_iota(jnp.int32, (rows, 1), 0) == chip
    joined = jnp.sum(joined_sum, axis=0, keepdims=True)
    sums[:, width : width + size] = jnp.where(mine, joined, 0.0)
    hidden = jnp.sum(hidden_sum, axis=0, keepdims=True)
    half = hidden.shape[1] // 2
    own, other = hidden[:, :half], hidden[:, half:]
    hidden = jnp.concatenate(
        [jnp.where(core == 0, own, other), jnp.where(core == 0, other, own)], axis=1
    )
    sums[:, width + size :] = jnp.where(mine, hidden, 0.0)


def heads_kernel(count, *refs):
    which, blocks, refs = refs[0], refs[1 : 1 + count], refs[1 + count :]
    gain, qkv_grad, out_grad, held, signals = refs
    copies = [
        pltpu.make_async_copy(block, held.at[which[k]], signals.at[k])
        for k, block in enumerate(blocks)
    ]
    for copy in copies:
        copy.start()
    for copy in copies:
        copy.wait()
    size = qkv_grad.shape[2]
    rows, width = out_grad.shape[1:]
    part = held.shape[2] - size
    for head in range(count):
        qkv_grad[:, head] = held[head, :, :size].astype(F32) * gain[...]
        for k in range(width // part):
            out_grad[head, :, k * part : (k + 1) * part] = held[
                head, k * rows : (k + 1) * rows, size:
            ].astype(F32)


def up_kernel(count, chained, *refs):
    which, blocks, refs = refs[0], refs[1 : 1 + count], refs[1 + count :]
    gain, refs = refs[0], refs[1 + chained :]
    up_grad, held, signals = refs
    size = blocks[0].shape[1]
    copies = []
    for k, block in enumerate(blocks):
        held[k] = block[...].astype(F32) * gain[...]
        place = pl.multiple_of(which[k] * size, size)
        copies.append(
            pltpu.make_async_copy(held.at[k], up_grad.at[:, pl.ds(place, size)], signals.at[k])
        )
        copies[-1].start()
    for copy in copies:
        copy.wait()


def rows_spec(array, count, pair):
    return pl.BlockSpec((count, array.shape[1]), lambda i: (pair, 0))


def call_rows(
    kernel, whole, by_rows, chain, outs_by_rows, outs_whole, scratch, at, rows, flops
):
    out_shape = list(outs_by_rows) + list(outs_whole)
    out_specs = [rows_spec(item, rows, at) for item in outs_by_rows] + [
        pl.BlockSpec(item.shape, lambda i: (0, 0)) for item in outs_whole
    ]
    operands = [*whole, *by_rows]
    in_specs = [
        pl.BlockSpec(memory_space=pltpu.SMEM if item.ndim == 1 else pltpu.VMEM) for item in whole
    ] + [rows_spec(item, rows, at) for item in by_rows]
    aliases = {}
    for k, item in enumerate(chain or ()):
        aliases[len(operands)] = k
        operands.append(item)
        in_specs.append(pl.BlockSpec(memory_space=pl.ANY))
    return pl.pallas_call(
        kernel,
        grid=(1,),
        out_shape=out_shape,
        in_specs=in_specs,
        out_specs=out_specs,
        scratch_shapes=scratch,
        input_output_aliases=aliases,
        cost_estimate=pl.CostEstimate(flops=flops, bytes_accessed=rows * 8192, transcendentals=0),
        compiler_params=pltpu.CompilerParams(vmem_limit_bytes=VMEM_BYTES),
    )(*operands)


def call_whole(kernel, operands, outs, scratch, outside=(), aliases=None):
    spaces = [
        pltpu.SMEM if item.dtype == jnp.int32 else pl.ANY if k in outside else pltpu.VMEM
        for k, item in enumerate([*operands, *outs])
    ]
    specs = [pl.BlockSpec(memory_space=space) for space in spaces]
    return pl.pallas_call(
        kernel,
        out_shape=outs,
        in_specs=specs[: len(operands)],
        out_specs=specs[len(operands) :],
        scratch_shapes=scratch,
        input_output_aliases=aliases or {},
        compiler_params=pltpu.CompilerParams(vmem_limit_bytes=VMEM_BYTES),
    )(*operands)


def on_device(
    layout,
    tokens,
    segments,
    cotangent,
    norm_gain,
    norm_bias,
    qkv_weight,
    qkv_bias,
    out_weight,
    out_bias,
    up_weight,
    up_bias,
    down_weight,
    down_bias,
):
    layout.place()
    first_section = lax.axis_index("section") == 0
    cores, chips, chip, core = layout.cores, layout.chips, layout.chip, layout.core
    length = segments.shape[1]
    width = tokens.shape[1]
    core_heads, joined_size = qkv_weight.shape[2:]
    head_size = joined_size // 3
    hidden_part = up_weight.shape[2] // chips
    hidden_size = cores * hidden_part
    row_count = chips * length

    def core_rows(block):
        return lax.dynamic_slice_in_dim(block, core * length, length, 0)

    def parts_of(rows, count=2):
        size = rows.shape[0] // count
        return [rows[k * size : (k + 1) * size] for k in range(count)]

    gains = norm_gain[0].astype(F32)
    shifts = norm_bias[0].astype(F32)
    own_tokens = core_rows(tokens).astype(F32)
    own_cotangent = core_rows(cotangent)
    own_normed, _ = normalize(own_tokens)

    own_segments = lax.dynamic_index_in_dim(segments, core, 0, keepdims=True).astype(BF16)
    own_segments = jnp.pad(own_segments, ((0, 15), (0, width - length)))
    first_block = jnp.where(first_section, own_normed.astype(BF16), own_cotangent)
    first_block = jnp.concatenate([first_block, own_segments], axis=0)
    gathered = layout.ring_gather([first_block])
    all_segments = jnp.concatenate(
        [gathered[slot][0][length : length + 1, :length] for slot in layout.slots], axis=0
    )
    cosine, sine, mask = sequence_tables(all_segments.astype(jnp.int32))

    shard = qkv_weight.shape[1]
    at = lax.axis_index("dp") * shard
    gain_rows = lax.dynamic_slice_in_dim(gains, at, shard, 1)
    qkv_scaled = qkv_weight[0].reshape(shard, core_heads * joined_size).astype(F32)
    qkv_scaled = layout.gather_groups((qkv_scaled * gain_rows[0][:, None]).astype(BF16), 0)
    up_scaled = (up_weight[0].astype(F32) * gain_rows[1][:, None]).astype(BF16)
    up_scaled = layout.gather_groups(up_scaled, 0)
    out_shard = layout.gather_groups(out_weight[0], 1)
    wd0 = layout.gather_groups(down_weight[0], 0)
    wd = jnp.concatenate([wd0, layout.other_core(wd0)], axis=0)
    block_rows = qkv_scaled.shape[0]

    ratio = shifts / gains
    biases = jnp.concatenate([qkv_bias[0].reshape(-1), up_bias[0]]).astype(F32)[None]
    both = jnp.concatenate([biases, layout.other_core(biases)], axis=0)
    joined_biases = both[:, : core_heads * joined_size]
    joined_biases = jnp.where(
        chip // core_heads == core, joined_biases[0], joined_biases[1]
    ).reshape(core_heads, joined_size)
    bq = lax.dynamic_index_in_dim(joined_biases, chip % core_heads, 0, keepdims=True)
    bu = lax.dynamic_slice_in_dim(
        both, core_heads * joined_size + chip * hidden_part, hidden_part, 1
    ).reshape(1, hidden_size)

    hd_rows = out_shard.shape[1]
    head_blocks = []
    for turn in range(core_heads):
        head = layout.head_turn(chip, turn)
        out_part = lax.dynamic_index_in_dim(out_shard, head, 0, keepdims=False)
        out_part = out_part.reshape(hd_rows, width // head_size, head_size).transpose(1, 0, 2)
        head_blocks.append(
            jnp.concatenate(
                [
                    lax.dynamic_slice_in_dim(qkv_scaled, head * joined_size, joined_size, 1),
                    out_part.reshape(block_rows, head_size),
                ],
                axis=1,
            )
        )
    up_blocks = [
        lax.dynamic_slice_in_dim(up_scaled, (chip ^ up_mask) * hidden_part, hidden_part, 1)
        for up_mask in range(chips)
    ]
    queue = Queue(3)
    order = message_order(chips, core_heads)
    heads = jnp.zeros((core_heads * block_rows, joined_size + head_size), BF16)
    wu0 = jnp.zeros((chips * block_rows, hidden_part), BF16)
    wu0 = lax.dynamic_update_slice_in_dim(wu0, up_blocks[0], chip * block_rows, 0)
    for k, (kind, which) in enumerate(order):
        block = head_blocks[which] if kind == "head" else up_blocks[which]
        if k == 1:
            block = ordered(block, *head_blocks)
        if k == 3:
            block = ordered(block, *up_blocks)
        if k == len(order) - 1:
            block = ordered(block, cosine, sine, mask, bq, bu, wd)
        block = queue.ready(block)
        if kind == "head":
            block = layout.send_head(block, which)
            slot = layout.head_turn(chip, which)
            heads = lax.dynamic_update_slice_in_dim(heads, block, slot * block_rows, 0)
        else:
            block = layout.swap(block, which)
            wu0 = lax.dynamic_update_slice_in_dim(wu0, block, (chip ^ which) * block_rows, 0)
        queue.put(block)
    wu = jnp.concatenate([wu0, layout.other_core(wu0)], axis=1)
    heads = layout.by_core(heads, layout.other_core(heads))

    row_bias = (out_bias[0].astype(F32) + down_bias[0].astype(F32))[None]

    part_rows = length // 2
    piece = jax.ShapeDtypeStruct((part_rows, width), BF16)
    whole_piece = jax.ShapeDtypeStruct((length, width), BF16)

    def by_rows(cols, dtype):
        return jax.ShapeDtypeStruct((row_count, cols), dtype)

    matrix_flops = 4 * length * width * (joined_size + head_size + 2 * hidden_size)

    def pair_blocks(blocks, pair):
        return blocks[layout.slots[2 * pair]] + blocks[layout.slots[2 * pair + 1]]

    def put_pieces(pieces, pair, blocks):
        pieces[layout.slots[2 * pair]] = blocks[:2]
        pieces[layout.slots[2 * pair + 1]] = blocks[2:]

    def norm_back(upstream, scaled, normed, inverse):
        return upstream.astype(F32) + inverse * (
            scaled
            - jnp.mean(scaled, axis=-1, keepdims=True)
            - normed * jnp.mean(scaled * normed, axis=-1, keepdims=True)
        )

    cotangent_blocks = [block for slot in layout.slots for block in gathered[slot]]
    attended_grad, active_grad = call_rows(
        functools.partial(upstream_kernel, len(cotangent_blocks)),
        (*cotangent_blocks, heads, wd),
        (),
        None,
        (),
        [by_rows(head_size, BF16), by_rows(hidden_size, BF16)],
        [pltpu.VMEM((row_count, width), BF16), pltpu.VMEM((head_size, width), BF16)],
        0,
        row_count,
        2 * row_count * width * (head_size + hidden_size),
    )

    matrices = (heads, wu, wd)
    pieces = {}
    for at in (1, 0):
        slots = layout.slots[at * chips // 2 : (at + 1) * chips // 2]
        blocks = [block for slot in slots for block in gathered[slot]]
        rows = row_count // 2
        results = call_rows(
            functools.partial(forward_kernel, len(blocks), 2 * len(slots)),
            (*blocks, *matrices, bq, bu, ratio),
            (cosine, sine, mask),
            None,
            (),
            [piece] * (2 * len(slots)),
            [
                pltpu.VMEM((rows, width), BF16),
                pltpu.VMEM((rows, width), BF16),
                pltpu.VMEM((rows, head_size), BF16),
                pltpu.VMEM((rows, hidden_size), BF16),
                pltpu.VMEM((head_size, width), BF16),
            ],
            at,
            rows,
            2 * matrix_flops,
        )
        for k, slot in enumerate(slots):
            pieces[slot] = results[2 * k : 2 * k + 2]
    branch_rows = layout.ring_scatter(pieces)
    first_out = [
        (rows + branch + row_bias).astype(BF16)
        for rows, branch in zip(parts_of(own_tokens), branch_rows)
    ]

    layer_input = [
        jnp.where(first_section, rows, lax.ppermute(sent, "section", [(0, 1), (1, 0)]).astype(F32))
        for rows, sent in zip(parts_of(own_tokens), first_out)
    ]
    own_normed = [normalize(rows) for rows in layer_input]
    normed_blocks = layout.ring_gather([rows.astype(BF16) for rows, _ in own_normed])
    kept_shapes = (
        by_rows(width, BF16),
        by_rows(width, BF16),
        by_rows(joined_size, BF16),
        by_rows(length, F32),
        by_rows(head_size, BF16),
        by_rows(hidden_size, BF16),
        by_rows(hidden_size, BF16),
    )
    kept = None
    pieces = {}
    for pair in range(chips // 2):
        blocks = pair_blocks(normed_blocks, pair)
        results = call_rows(
            functools.partial(both_kernel, len(blocks), 4, len(kept_shapes) if kept else 0),
            (*blocks, heads, wu, bq, bu, ratio),
            (cosine, sine, mask, attended_grad, active_grad),
            kept,
            kept_shapes,
            [piece] * 4,
            [
                pltpu.VMEM((2 * length, joined_size), BF16),
                pltpu.VMEM((2 * length, hidden_size), BF16),
            ],
            pair,
            2 * length,
            2 * matrix_flops,
        )
        kept = results[: len(kept_shapes)]
        put_pieces(pieces, pair, results[len(kept_shapes) :])
    first_norm, second_norm, qkv, attention, attended, active, slope = kept
    scaled_rows = layout.ring_scatter(pieces)
    second_grad = [
        norm_back(given, scaled, *norm)
        for given, scaled, norm in zip(parts_of(own_cotangent), scaled_rows, own_normed)
    ]

    arrived_grad = [
        lax.ppermute(rows.astype(BF16), "section", [(0, 1), (1, 0)]) for rows in second_grad
    ]
    own_upstream = [
        jnp.where(first_section, arrived, given)
        for arrived, given in zip(arrived_grad, parts_of(own_cotangent))
    ]
    upstream_blocks = layout.ring_gather(own_upstream)
    second_section = jnp.where(first_section, 0, 1).astype(jnp.int32).reshape(1)
    grad_shapes = (by_rows(width, BF16), by_rows(joined_size, BF16), by_rows(hidden_size, BF16))
    grads = None
    last_pieces = {}
    sums = []
    for pair in range(chips // 2):
        blocks = pair_blocks(upstream_blocks, pair)
        results = call_rows(
            functools.partial(
                backward_kernel, len(blocks), 2, len(grad_shapes) if grads else 0
            ),
            (*blocks, second_section, *matrices),
            (cosine, sine, first_norm, second_norm, qkv, attention, attended, active, slope),
            grads,
            grad_shapes,
            [
                jax.ShapeDtypeStruct((32, width), F32),
                jax.ShapeDtypeStruct((8, joined_size), F32),
                jax.ShapeDtypeStruct((8, hidden_size), F32),
            ]
            + [whole_piece] * 2,
            [pltpu.VMEM((head_size, width), BF16)],
            pair,
            2 * length,
            matrix_flops,
        )
        grads = results[: len(grad_shapes)]
        sums.append(results[len(grad_shapes) : len(grad_shapes) + 3])
        for k in range(2):
            last_pieces[layout.slots[2 * pair + k]] = [results[k - 2]]
    upstream, joined_grad, hidden_grad = grads

    own_given = jnp.concatenate(own_upstream, axis=0)
    (local_sums,) = call_whole(
        functools.partial(sums_kernel, len(sums)),
        [jnp.stack([chip, core]), *[item for pair in sums for item in pair], own_given],
        [jax.ShapeDtypeStruct((chips, width + joined_size + hidden_size), F32)],
        [],
    )
    joint = layout.sum_steps(local_sums)

    def half_of(array, which):
        size = array.shape[1] // cores
        return lax.dynamic_slice_in_dim(array, which * size, size, 1)

    row_major = Format(major_to_minor=(0, 1))

    def weight_grad(left_side, right_side):
        return with_layout_constraint(contract_rows(left_side, right_side), row_major)

    joined_given = weight_grad(half_of(first_norm, 1 - core), joined_grad).astype(BF16)
    out_given = weight_grad(half_of(attended, 1 - core), upstream).astype(BF16)
    hidden_given = weight_grad(second_norm, hidden_grad[:, hidden_part:]).astype(BF16)
    joined_taken, out_taken, hidden_taken = (
        layout.other_core(item) for item in (joined_given, out_given, hidden_given)
    )

    def core_sum(own, taken):
        return (own + taken.astype(F32)).astype(BF16)

    late_grad, late_attended = (
        ordered(item, joint[0], joined_given, out_given, hidden_given)
        for item in (joined_grad, attended)
    )
    joined_held = core_sum(weight_grad(half_of(first_norm, core), late_grad), joined_taken)
    out_held = core_sum(weight_grad(half_of(late_attended, core), upstream), out_taken)
    late_grad = ordered(hidden_grad, joined_held, out_held)
    hidden_held = core_sum(weight_grad(second_norm, late_grad[:, :hidden_part]), hidden_taken)
    late_active = ordered(active, hidden_held)
    down_taken = layout.other_core(
        weight_grad(late_active[:, hidden_part:], upstream).astype(BF16)
    )

    whole_sums = joint[-1]
    norm_sums = whole_sums[:4, :width].reshape(2, 2, width)
    norm_sums = jnp.stack([norm_sums[0] - ratio * norm_sums[1], norm_sums[1]]) / gains
    out_bias_grad = whole_sums[4, :width]
    joined_bias_grad = lax.dynamic_slice_in_dim(
        whole_sums[:, width : width + joined_size], core * core_heads, core_heads, 0
    )
    up_bias_grad = lax.dynamic_slice_in_dim(
        whole_sums[:, width + joined_size :], core * hidden_part, hidden_part, 1
    ).reshape(-1)

    (last_rows,) = layout.ring_scatter(last_pieces, None, {1: (joined_held, out_held)})
    last_normed, last_inverse = (
        jnp.concatenate([norm[k] for norm in own_normed], axis=0) for k in range(2)
    )
    first_grad = norm_back(own_given, last_rows, last_normed, last_inverse)
    own_grad = jnp.where(first_section, first_grad, jnp.concatenate(second_grad, axis=0))
    input_gradients = layout.by_core(own_grad, layout.other_core(own_grad))
    second_out = (jnp.concatenate(layer_input, axis=0) + last_rows + row_bias).astype(BF16)
    own_out = jnp.where(first_section, jnp.concatenate(first_out, axis=0), second_out)
    layer_outputs = layout.by_core(own_out, layout.other_core(own_out))

    out_rows = out_held.shape[0] // core_heads
    share_rows = out_rows // layout.groups
    head_blocks = []
    for turn in range(core_heads):
        slot = layout.head_turn(chip, turn)
        out_part = lax.dynamic_slice_in_dim(out_held, slot * out_rows, out_rows, 0)
        out_part = out_part.reshape(layout.groups, share_rows, width // head_size, head_size)
        head_blocks.append(
            jnp.concatenate(
                [
                    lax.dynamic_slice_in_dim(joined_held, slot * block_rows, block_rows, 0),
                    out_part.transpose(0, 2, 1, 3).reshape(block_rows, head_size),
                ],
                axis=1,
            )
        )
    queue = Queue(3)
    gain_cols = gain_rows[:, :, None]
    blocks = {
        ("up", 0): lax.dynamic_slice_in_dim(hidden_held, chip * block_rows, block_rows, 0)
    }
    up_weight_grad = None
    for k, (kind, which) in enumerate(order):
        if kind == "head":
            block = head_blocks[which]
        else:
            block = lax.dynamic_slice_in_dim(
                hidden_held, (chip ^ which) * block_rows, block_rows, 0
            )
        if k == 0:
            block = ordered(block, joint[1], *head_blocks)
        if k == 2:
            block = ordered(block, joint[2])
        if k == 4:
            block = ordered(block, joint[-1])
        if k == len(order) - 3:
            block = ordered(block, down_weight_grad)
        if k == len(order) - 1:
            block = ordered(block, last_rows, joined_weight_grad)
        block = queue.ready(block)
        block = layout.return_head(block, which) if kind == "head" else layout.swap(block, which)
        queue.put(block)
        blocks[kind, which] = block
        if kind == "head" and which == core_heads - 1:
            heads_in = [blocks["head", turn] for turn in range(core_heads)]
            if layout.groups > 1:
                heads_in = [layout.scatter_groups(item, 0) for item in heads_in]
            joined_weight_grad, out_weight_grad = call_whole(
                functools.partial(heads_kernel, core_heads),
                [
                    jnp.stack([layout.head_turn(chip, turn) for turn in range(core_heads)]),
                    *heads_in,
                    gain_cols[0],
                ],
                [
                    jax.ShapeDtypeStruct((shard, core_heads, joined_size), F32),
                    jax.ShapeDtypeStruct((core_heads, share_rows, width), F32),
                ],
                [
                    pltpu.VMEM((core_heads, *heads_in[0].shape), heads_in[0].dtype),
                    pltpu.SemaphoreType.DMA((core_heads,)),
                ],
                range(1, 1 + core_heads),
            )
            down_weight_grad = weight_grad(
                late_active[:, :hidden_part], upstream
            ) + down_taken.astype(F32)
            if layout.groups > 1:
                down_weight_grad = layout.scatter_groups(down_weight_grad, 0)
        if k in (len(order) - 3, len(order) - 1):
            masks = [mask for mask in range(chips) if ("up", mask) in blocks]
            columns = [blocks.pop(("up", mask)) for mask in masks]
            if layout.groups > 1:
                columns = [layout.scatter_groups(item, 0) for item in columns]
            chain = [] if up_weight_grad is None else [up_weight_grad]
            (up_weight_grad,) = call_whole(
                functools.partial(up_kernel, len(columns), len(chain)),
                [jnp.stack([chip ^ mask for mask in masks]), *columns, gain_cols[1], *chain],
                [jax.ShapeDtypeStruct((shard, chips * hidden_part), F32)],
                [
                    pltpu.VMEM((len(columns), *columns[0].shape), F32),
                    pltpu.SemaphoreType.DMA((len(columns),)),
                ],
                range(len(columns) + 2, len(columns) + 3 + len(chain)),
                {len(columns) + 2: 0} if chain else None,
            )

    return (
        layer_outputs[None],
        input_gradients[None],
        norm_sums[0][None],
        norm_sums[1][None],
        joined_weight_grad[None],
        joined_bias_grad[None],
        out_weight_grad[None],
        out_bias_grad[None],
        up_weight_grad[None],
        up_bias_grad[None],
        down_weight_grad[None],
        out_bias_grad[None],
    )


def solution(mesh):
    def whole(*arrays):
        layout = Layout(mesh, arrays[5].shape[2])

        def local(*blocks):
            return on_device(layout, *blocks)

        return jax.shard_map(
            local,
            mesh=mesh,
            in_specs=(
                P("dp", None),
                P("dp", None),
                P("dp", None),
                P("section", None, None),
                P("section", None, None),
                P("section", "dp", "tensor", None),
                P("section", "tensor", None),
                P("section", "tensor", "dp", None),
                P("section", None),
                P("section", "dp", "tensor"),
                P("section", "tensor"),
                P("section", ("tensor", "dp"), None),
                P("section", None),
            ),
            out_specs=(
                P("section", "dp", None),
                P("section", "dp", None),
                P("section", None, None),
                P("section", None, None),
                P("section", "dp", "tensor", None),
                P("section", "tensor", None),
                P("section", "tensor", "dp", None),
                P("section", None),
                P("section", "dp", "tensor"),
                P("section", "tensor"),
                P("section", ("tensor", "dp"), None),
                P("section", None),
            ),
            check_vma=False,
        )(*arrays)

    return whole
```

```python
import functools
import math

import jax
import jax.numpy as jnp
from jax import lax
from jax.experimental import pallas as pl
from jax.experimental.layout import Layout as Format
from jax.experimental.layout import with_layout_constraint
from jax.experimental.pallas import tpu as pltpu
from jax.sharding import PartitionSpec as P

ROT = 64
LANES = 128
NORM_EPSILON = 1e-05
MASK_VALUE = -1e30
ROOT_HALF = 0.7071067811865476
DENSITY_SCALE = 0.3989422804014327
F32 = jnp.float32
BF16 = jnp.bfloat16
VMEM_BYTES = 24 * 1024 * 1024


def contract_rows(left_side, right_side):
    return lax.dot_general(
        left_side, right_side, (((0,), (0,)), ((), ())), preferred_element_type=F32
    )


def contract_cols(left_side, right_side):
    return lax.dot_general(
        left_side, right_side, (((1,), (1,)), ((), ())), preferred_element_type=F32
    )


def matmul(left_side, right_side):
    return jnp.dot(left_side, right_side, preferred_element_type=F32)


def normalize(values):
    centered = values - jnp.mean(values, axis=-1, keepdims=True)
    inverse = lax.rsqrt(jnp.mean(centered * centered, axis=-1, keepdims=True) + NORM_EPSILON)
    return (centered * inverse, inverse)


def sequence_tables(segments):
    places = jnp.arange(segments.shape[1], dtype=jnp.int32)
    same_doc = segments[:, :, None] == segments[:, None, :]
    earlier = places[None, :] < places[:, None]
    position = jnp.sum(jnp.where(same_doc & earlier, 1, 0).astype(jnp.int32), axis=2)
    allowed = same_doc & (places[None, :] <= places[:, None])
    exponent = jnp.arange(ROT // 2, dtype=F32) * (2.0 / ROT)
    frequency = 10000.0 ** (-exponent)
    angles = position.astype(F32)[..., None] * frequency
    cosine, sine = jnp.cos(angles), jnp.sin(angles)
    rest = jnp.zeros(angles.shape[:2] + (LANES - ROT,), F32)
    count = segments.shape[0] * segments.shape[1]
    return (
        jnp.concatenate([cosine, cosine, rest + 1.0], axis=-1).reshape(count, LANES),
        jnp.concatenate([-sine, sine, rest], axis=-1).reshape(count, LANES),
        jnp.where(allowed, 0.0, MASK_VALUE).astype(F32).reshape(count, segments.shape[1]),
    )


class Layout:
    def __init__(self, mesh, heads):
        self.cores = mesh.shape["tensor"]
        self.dp = mesh.shape["dp"]
        self.chips = heads
        self.groups = self.dp // heads
        self.core_heads = heads // self.cores
        self.ring = list(range(0, heads, 2)) + list(range(heads - 1, 0, -2))
        self.slots = []
        for k in range(heads // 2):
            self.slots += [-k % heads, k + 1]

    def place(self):
        dp_index = lax.axis_index("dp")
        self.core = lax.axis_index("tensor")
        self.chip = dp_index // self.groups
        self.group = dp_index % self.groups

    def between_chips(self, block, target_of, sections=None):
        pairs = [
            (chip * self.groups + group, target_of(chip) * self.groups + group)
            for chip in range(self.chips)
            for group in range(self.groups)
        ]
        if sections is None:
            return lax.ppermute(block, "dp", pairs)
        pairs = [
            (section * self.dp + source, section * self.dp + target)
            for section in sections
            for source, target in pairs
        ]
        return lax.ppermute(block, ("section", "dp"), pairs)

    def ring_step(self, block, distance, sections=None):
        size = len(self.ring)

        def target_of(chip):
            return self.ring[(self.ring.index(chip) + distance) % size]

        return self.between_chips(block, target_of, sections)

    def between_groups(self, block, distance):
        pairs = [
            (chip * self.groups + group, chip * self.groups + (group + distance) % self.groups)
            for chip in range(self.chips)
            for group in range(self.groups)
        ]
        return lax.ppermute(block, "dp", pairs)

    def other_core(self, block):
        return lax.ppermute(block, "tensor", [(0, 1), (1, 0)])

    def by_core(self, own, other):
        first = self.core == 0
        return jnp.concatenate(
            [jnp.where(first, own, other), jnp.where(first, other, own)], axis=0
        )

    def gather_groups(self, block, axis):
        if self.groups == 1:
            return block
        size = block.shape[axis]
        shape = list(block.shape)
        shape[axis] = size * self.groups
        total = jnp.zeros(shape, block.dtype)
        for distance in range(self.groups):
            part = self.between_groups(block, distance) if distance else block
            source = (self.group - distance) % self.groups
            total = lax.dynamic_update_slice_in_dim(total, part, source * size, axis)
        return total

    def scatter_groups(self, block, axis):
        if self.groups == 1:
            return block.astype(F32)
        size = block.shape[axis] // self.groups
        total = lax.dynamic_slice_in_dim(block, self.group * size, size, axis).astype(F32)
        for distance in range(1, self.groups):
            target = (self.group + distance) % self.groups
            part = lax.dynamic_slice_in_dim(block, target * size, size, axis)
            total = total + self.between_groups(part.astype(BF16), distance).astype(F32)
        return total

    def sum_steps(self, block):
        held = [block + self.other_core(block)]
        mask = 1
        while mask < self.chips:
            held.append(held[-1] + self.between_chips(held[-1], lambda chip: chip ^ mask))
            mask *= 2
        if self.groups > 1:
            total = held[-1]
            for distance in range(1, self.groups):
                total = total + self.between_groups(held[-1], distance)
            held.append(total)
        return held

    def ring_gather(self, parts, sections=None):
        half = self.chips // 2
        held = [{0: part} for part in parts]
        for step in range(1, half + 1):
            for at, slots in enumerate(held):
                down = half - at % 2
                if step <= down:
                    slots[step] = self.ring_step(slots[step - 1], -1, sections)
                if step <= self.chips - 1 - down:
                    slots[self.chips - step] = self.ring_step(
                        slots[(self.chips - step + 1) % self.chips], 1, sections
                    )
        return {slot: [slots[slot] for slots in held] for slot in range(self.chips)}

    def ring_scatter(self, pieces, sections=None, waits=None):
        half = self.chips // 2
        totals = []
        for at in range(len(pieces[0])):
            parts = [pieces[slot][at] for slot in range(self.chips)]
            up = half - at % 2
            total = parts[0].astype(F32)
            for way, slots in (
                (1, range(up, 0, -1)),
                (-1, range(up + 1, self.chips)),
            ):
                moving = None
                for step, slot in enumerate(slots):
                    if moving is None:
                        moving = parts[slot]
                    else:
                        moving = (moving.astype(F32) + parts[slot].astype(F32)).astype(BF16)
                    if waits and step in waits:
                        moving = ordered(moving, *waits[step])
                    moving = self.ring_step(moving, way, sections)
                total = total + moving.astype(F32)
            totals.append(total)
        return totals

    def head_turn(self, chip, turn):
        return (chip % self.core_heads) ^ turn

    def head_route(self, turn):
        pairs = []
        for core in range(self.cores):
            for chip in range(self.chips):
                target_core = chip // self.core_heads
                target = core * self.core_heads + self.head_turn(chip, turn)
                for group in range(self.groups):
                    pairs.append(
                        (
                            core * self.dp + chip * self.groups + group,
                            target_core * self.dp + target * self.groups + group,
                        )
                    )
        return pairs

    def send_head(self, block, turn):
        return lax.ppermute(block, ("tensor", "dp"), self.head_route(turn))

    def return_head(self, block, turn):
        pairs = [(target, source) for source, target in self.head_route(turn)]
        return lax.ppermute(block, ("tensor", "dp"), pairs)

    def swap(self, block, mask):
        return self.between_chips(block, lambda chip: chip ^ mask)


def message_orders(chips, core_heads):
    near = [("up", mask) for mask in range(chips // 2 - 1, 0, -1)]
    far = [("up", mask) for mask in range(chips - 1, chips // 2 - 1, -1)]
    heads = [("head", turn) for turn in range(core_heads)]
    out = heads[:1]
    for k, head in enumerate(heads[1:]):
        out += [head] + near[k : k + 1]
    out += near[len(heads) - 1 :] + far
    mixed = [item for pair in zip(near, far) for item in pair][: len(heads)]
    back = [item for pair in zip(heads, mixed) for item in pair]
    rest = [item for item in far if item not in back]
    back += rest[:-1] + [item for item in near if item not in back] + rest[-1:]
    return (out, back)


def ordered(block, *earlier):
    return lax.optimization_barrier((block,) + earlier)[0]


class Queue:
    def __init__(self, window, first=()):
        self.window = window
        self.results = [first] * window

    def ready(self, block):
        earlier = self.results[-self.window]
        return ordered(block, *earlier) if earlier else block

    def put(self, *result):
        self.results.append(result)


def turn_head(values, cosine, sine):
    first = values[:, :LANES]
    lane = lax.broadcasted_iota(jnp.int32, first.shape, 1)
    half = ROT // 2
    swapped = jnp.where(
        lane < half, pltpu.roll(first, LANES - half, 1), pltpu.roll(first, half, 1)
    )
    return jnp.concatenate([first * cosine + swapped * sine, values[:, LANES:]], axis=1)


def attend(joined, cosine, sine, mask):
    size = joined.shape[1] // 3
    queries = turn_head(joined[:, :size], cosine, sine).astype(BF16)
    key_rows = turn_head(joined[:, size : 2 * size], cosine, sine).astype(BF16)
    values = joined[:, 2 * size :].astype(BF16)
    scores = contract_cols(queries, key_rows) * (1.0 / math.sqrt(size)) + mask
    powered = jnp.exp(scores - jnp.max(scores, axis=-1, keepdims=True))
    attention = powered / jnp.sum(powered, axis=-1, keepdims=True)
    attended = matmul(attention.astype(BF16), values).astype(BF16)
    return (queries, key_rows, values, attention, attended)


def attend_back(queries, key_rows, values, attention, attended_grad, cosine, sine):
    scale = 1.0 / math.sqrt(queries.shape[1])
    values_grad = contract_rows(attention.astype(BF16), attended_grad)
    attention_grad = contract_cols(attended_grad, values)
    row_dots = jnp.sum(attention_grad * attention, axis=-1, keepdims=True)
    scores_grad = (attention * (attention_grad - row_dots)).astype(BF16)
    queries_grad = turn_head(matmul(scores_grad, key_rows) * scale, cosine, -sine)
    keys_grad = turn_head(contract_rows(scores_grad, queries) * scale, cosine, -sine)
    return jnp.concatenate([queries_grad, keys_grad, values_grad], axis=1).astype(BF16)


def fold_rows(values):
    return jnp.sum(values.reshape(values.shape[0] // 8, 8, values.shape[1]), axis=0)


def store_rows(refs, cols, values):
    rows = values.shape[0] // len(refs)
    for at, ref in enumerate(refs):
        ref[:, cols] = values[at * rows : (at + 1) * rows].astype(BF16)


def steps(size):
    step = min(256, size)
    return [slice(at, at + step) for at in range(0, size, step)]


def load_rows(refs, target, shift=0.0):
    rows = target.shape[0] // len(refs)
    for at, ref in enumerate(refs):
        values = ref[:rows]
        if not isinstance(shift, float):
            values = (values.astype(F32) + shift).astype(BF16)
        target[at * rows : (at + 1) * rows] = values


def split_heads(heads, wo):
    size = wo.shape[0]
    rows = heads.shape[0] // wo.shape[1] * size
    cols = heads.shape[1] - size
    part = size * rows // heads.shape[0]
    for at in range(0, heads.shape[0], rows):
        for k in range(rows // part):
            wo[at // rows * part : (at // rows + 1) * part, k * size : (k + 1) * size] = heads[
                at + k * part : at + (k + 1) * part, cols:
            ]
    return heads.at[:, :cols]


def forward_kernel(count, pieces, *refs):
    blocks, refs = refs[:count], refs[count:]
    heads, wu, wd, bq, bu, ratio, cosine, sine, mask = refs[:9]
    outs, refs = refs[9 : 9 + pieces], refs[9 + pieces :]
    first_norm, second_norm, attended, active, wo = refs
    wq = split_heads(heads, wo)
    length = mask.shape[1]
    load_rows(blocks, first_norm, ratio[0:1])
    load_rows(blocks, second_norm, ratio[1:2])
    joined = matmul(first_norm[...], wq[...]) + bq[...]
    for s in range(mask.shape[0] // length):
        rows = slice(s * length, (s + 1) * length)
        attended[rows] = attend(joined[rows], cosine[rows], sine[rows], mask[rows])[4]
    for cols in steps(wu.shape[1]):
        hidden = matmul(second_norm[...], wu[:, cols]) + bu[:, cols]
        active[:, cols] = (hidden * (0.5 * (1.0 + lax.erf(hidden * ROOT_HALF)))).astype(BF16)
    for cols in steps(wo.shape[1]):
        total = matmul(attended[...], wo[:, cols]) + matmul(active[...], wd[:, cols])
        store_rows(outs, cols, total)


def upstream_kernel(count, *refs):
    grads, refs = refs[:count], refs[count:]
    heads, wd, attended_grad, active_grad, upstream, wo = refs
    split_heads(heads, wo)
    load_rows(grads, upstream)
    attended_grad[...] = contract_cols(upstream[...], wo[...]).astype(BF16)
    for rows in steps(wd.shape[0]):
        active_grad[:, rows] = contract_cols(upstream[...], wd[rows]).astype(BF16)


def both_kernel(count, pieces, chained, *refs):
    blocks, refs = refs[:count], refs[count:]
    heads, wu, bq, bu, ratio, cosine, sine, mask, attended_grad, active_grad = refs[:10]
    refs = refs[10 + chained :]
    first_norm, second_norm, qkv, attention, attended, active, slope = refs[:7]
    outs, (joined_grad, hidden_grad) = refs[7 : 7 + pieces], refs[7 + pieces :]
    length = mask.shape[1]
    size = attended_grad.shape[1]
    wq = heads.at[:, : 3 * size]
    part = wu.shape[1] // 2
    load_rows(blocks, first_norm, ratio[0:1])
    load_rows(blocks, second_norm, ratio[1:2])
    joined = matmul(first_norm[...], wq[...]) + bq[...]

    def attention_of(s):
        rows = slice(s * length, (s + 1) * length)
        queries, key_rows, values, weights, result = attend(
            joined[rows], cosine[rows], sine[rows], mask[rows]
        )
        qkv[rows, :size] = queries
        qkv[rows, size : 2 * size] = key_rows
        qkv[rows, 2 * size :] = values
        attention[rows] = weights
        attended[rows] = result
        joined_grad[rows] = attend_back(
            queries, key_rows, values, weights, attended_grad[rows], cosine[rows], sine[rows]
        )

    for k in range(2):
        attention_of(k)
        for cols in steps(part):
            at = slice(k * part + cols.start, k * part + cols.stop)
            hidden = matmul(second_norm[...], wu[:, at]) + bu[:, at]
            normal_cdf = 0.5 * (1.0 + lax.erf(hidden * ROOT_HALF))
            normal_pdf = jnp.exp(-0.5 * hidden * hidden) * DENSITY_SCALE
            active[:, at] = (hidden * normal_cdf).astype(BF16)
            change = normal_cdf + hidden * normal_pdf
            slope[:, at] = change.astype(BF16)
            hidden_grad[:, at] = (active_grad[:, at].astype(F32) * change).astype(BF16)
    for rows in steps(wq.shape[0]):
        total = contract_cols(joined_grad[...], wq[rows]) + contract_cols(
            hidden_grad[...], wu[rows]
        )
        store_rows(outs, rows, total)


def backward_kernel(count, chained, *refs):
    grads, refs = refs[:count], refs[count:]
    heads, wd, cosine, sine, qkv, attention, slope = refs[:7]
    upstream, joined_grad, hidden_grad, joined_sum, hidden_sum, wo = refs[7 + chained :]
    split_heads(heads, wo)
    length = attention.shape[1]
    size = wo.shape[0]
    part = wd.shape[0] // 2
    load_rows(grads, upstream)
    attended_grad = contract_cols(upstream[...], wo[...]).astype(BF16)
    for k in range(2):
        rows = slice(k * length, (k + 1) * length)
        joined_grad[rows] = attend_back(
            qkv[rows, :size],
            qkv[rows, size : 2 * size],
            qkv[rows, 2 * size :],
            attention[rows],
            attended_grad[rows],
            cosine[rows],
            sine[rows],
        )
        for cols in steps(part):
            at = slice(k * part + cols.start, k * part + cols.stop)
            active_grad = contract_cols(upstream[...], wd[at])
            grad = (active_grad * slope[:, at].astype(F32)).astype(BF16)
            hidden_grad[:, at] = grad
            hidden_sum[:, at] = fold_rows(grad.astype(F32))
    joined_sum[...] = fold_rows(joined_grad[...].astype(F32))


def scaled_kernel(second, heads, wu, wd, *refs):
    first_norm, second_norm, attended, active, joined_grad, hidden_grad = refs[:6]
    out, norm_sums, wo = refs[6:]
    wq = split_heads(heads, wo)

    @pl.when(pl.program_id(0) == 0)
    def _():
        norm_sums[...] = jnp.zeros_like(norm_sums)

    for cols in steps(wq.shape[0]):
        first = contract_cols(joined_grad[...], wq[cols])
        other = contract_cols(hidden_grad[...], wu[cols])
        norm_sums[0:8, cols] += fold_rows(first * first_norm[:, cols].astype(F32))
        norm_sums[8:16, cols] += fold_rows(other * second_norm[:, cols].astype(F32))
        norm_sums[16:24, cols] += fold_rows(first)
        norm_sums[24:32, cols] += fold_rows(other)
        out[:, cols] = (first + other).astype(BF16)

    @pl.when(second[0] != 0)
    def _():
        for cols in steps(wq.shape[0]):
            total = matmul(attended[...], wo[:, cols]) + matmul(active[...], wd[:, cols])
            out[:, cols] = total.astype(BF16)


def sums_kernel(pairs, *refs):
    where, norm_sums, parts = refs[0], refs[1], refs[2 : 2 + 2 * pairs]
    given, sums = refs[2 + 2 * pairs :]
    joined_sum, hidden_sum = (
        functools.reduce(jnp.add, [parts[2 * pair + k][...] for pair in range(pairs)])
        for k in range(2)
    )
    rows, width = sums.shape[0], given.shape[1]
    size = joined_sum.shape[1]
    chip, core = where[0], where[1]
    upstream = jnp.sum(given[...].astype(F32), axis=0, keepdims=True)
    for k in range(4):
        sums[k : k + 1, :width] = jnp.sum(norm_sums[8 * k : 8 * k + 8], axis=0, keepdims=True)
    sums[4:5, :width] = upstream
    sums[5:rows, :width] = jnp.zeros((rows - 5, width), F32)
    mine = lax.broadcasted_iota(jnp.int32, (rows, 1), 0) == chip
    joined = jnp.sum(joined_sum, axis=0, keepdims=True)
    sums[:, width : width + size] = jnp.where(mine, joined, 0.0)
    hidden = jnp.sum(hidden_sum, axis=0, keepdims=True)
    half = hidden.shape[1] // 2
    own, other = hidden[:, :half], hidden[:, half:]
    hidden = jnp.concatenate(
        [jnp.where(core == 0, own, other), jnp.where(core == 0, other, own)], axis=1
    )
    sums[:, width + size :] = jnp.where(mine, hidden, 0.0)


def heads_kernel(count, *refs):
    which, blocks, refs = refs[0], refs[1 : 1 + count], refs[1 + count :]
    gain, qkv_grad, out_grad, held, signals = refs
    copies = [
        pltpu.make_async_copy(block, held.at[which[k]], signals.at[k])
        for k, block in enumerate(blocks)
    ]
    for copy in copies:
        copy.start()
    for copy in copies:
        copy.wait()
    size = qkv_grad.shape[2]
    rows, width = out_grad.shape[1:]
    part = held.shape[2] - size
    for head in range(count):
        qkv_grad[:, head] = held[head, :, :size].astype(F32) * gain[...]
        for k in range(width // part):
            out_grad[head, :, k * part : (k + 1) * part] = held[
                head, k * rows : (k + 1) * rows, size:
            ].astype(F32)


def up_kernel(count, chained, *refs):
    which, blocks, refs = refs[0], refs[1 : 1 + count], refs[1 + count :]
    gain, refs = refs[0], refs[1 + chained :]
    up_grad, held, signals = refs
    size = blocks[0].shape[1]
    copies = []
    for k, block in enumerate(blocks):
        held[k] = block[...].astype(F32) * gain[...]
        place = pl.multiple_of(which[k] * size, size)
        copies.append(
            pltpu.make_async_copy(held.at[k], up_grad.at[:, pl.ds(place, size)], signals.at[k])
        )
        copies[-1].start()
    for copy in copies:
        copy.wait()


def rows_spec(array, count, pair):
    return pl.BlockSpec((count, array.shape[1]), lambda i: (pair, 0))


def call_rows(
    kernel, whole, by_rows, chain, outs_by_rows, outs_whole, scratch, at, rows, flops
):
    out_shape = list(outs_by_rows) + list(outs_whole)
    out_specs = [rows_spec(item, rows, at) for item in outs_by_rows] + [
        pl.BlockSpec(item.shape, lambda i: (0, 0)) for item in outs_whole
    ]
    operands = [*whole, *by_rows]
    in_specs = [
        pl.BlockSpec(memory_space=pltpu.SMEM if item.ndim == 1 else pltpu.VMEM) for item in whole
    ] + [rows_spec(item, rows, at) for item in by_rows]
    aliases = {}
    for k, item in enumerate(chain or ()):
        aliases[len(operands)] = k
        operands.append(item)
        in_specs.append(pl.BlockSpec(memory_space=pl.ANY))
    return pl.pallas_call(
        kernel,
        grid=(1,),
        out_shape=out_shape,
        in_specs=in_specs,
        out_specs=out_specs,
        scratch_shapes=scratch,
        input_output_aliases=aliases,
        cost_estimate=pl.CostEstimate(flops=flops, bytes_accessed=rows * 8192, transcendentals=0),
        compiler_params=pltpu.CompilerParams(vmem_limit_bytes=VMEM_BYTES),
    )(*operands)


def call_whole(kernel, operands, outs, scratch, outside=(), aliases=None):
    spaces = [
        pltpu.SMEM if item.dtype == jnp.int32 else pl.ANY if k in outside else pltpu.VMEM
        for k, item in enumerate([*operands, *outs])
    ]
    specs = [pl.BlockSpec(memory_space=space) for space in spaces]
    return pl.pallas_call(
        kernel,
        out_shape=outs,
        in_specs=specs[: len(operands)],
        out_specs=specs[len(operands) :],
        scratch_shapes=scratch,
        input_output_aliases=aliases or {},
        compiler_params=pltpu.CompilerParams(vmem_limit_bytes=VMEM_BYTES),
    )(*operands)


def on_device(
    layout,
    tokens,
    segments,
    cotangent,
    norm_gain,
    norm_bias,
    qkv_weight,
    qkv_bias,
    out_weight,
    out_bias,
    up_weight,
    up_bias,
    down_weight,
    down_bias,
):
    layout.place()
    first_section = lax.axis_index("section") == 0
    cores, chips, chip, core = layout.cores, layout.chips, layout.chip, layout.core
    length = segments.shape[1]
    width = tokens.shape[1]
    core_heads, joined_size = qkv_weight.shape[2:]
    head_size = joined_size // 3
    hidden_part = up_weight.shape[2] // chips
    hidden_size = cores * hidden_part
    row_count = chips * length

    def core_rows(block):
        return lax.dynamic_slice_in_dim(block, core * length, length, 0)

    def parts_of(rows, count=2):
        size = rows.shape[0] // count
        return [rows[k * size : (k + 1) * size] for k in range(count)]

    gains = norm_gain[0].astype(F32)
    shifts = norm_bias[0].astype(F32)
    own_tokens = core_rows(tokens).astype(F32)
    own_cotangent = core_rows(cotangent)
    own_normed, _ = normalize(own_tokens)

    own_segments = lax.dynamic_index_in_dim(segments, core, 0, keepdims=True).astype(BF16)
    own_segments = jnp.pad(own_segments, ((0, 15), (0, width - length)))
    first_block = jnp.where(first_section, own_normed.astype(BF16), own_cotangent)
    first_block = jnp.concatenate([first_block, own_segments], axis=0)
    gathered = layout.ring_gather([first_block])
    all_segments = jnp.concatenate(
        [gathered[slot][0][length : length + 1, :length] for slot in layout.slots], axis=0
    )
    cosine, sine, mask = sequence_tables(all_segments.astype(jnp.int32))

    shard = qkv_weight.shape[1]
    at = lax.axis_index("dp") * shard
    gain_rows = lax.dynamic_slice_in_dim(gains, at, shard, 1)
    qkv_scaled = qkv_weight[0].reshape(shard, core_heads * joined_size).astype(F32)
    qkv_scaled = layout.gather_groups((qkv_scaled * gain_rows[0][:, None]).astype(BF16), 0)
    up_scaled = (up_weight[0].astype(F32) * gain_rows[1][:, None]).astype(BF16)
    up_scaled = layout.gather_groups(up_scaled, 0)
    out_shard = layout.gather_groups(out_weight[0], 1)
    wd0 = layout.gather_groups(down_weight[0], 0)
    wd = jnp.concatenate([wd0, layout.other_core(wd0)], axis=0)
    block_rows = qkv_scaled.shape[0]

    ratio = shifts / gains
    biases = jnp.concatenate([qkv_bias[0].reshape(-1), up_bias[0]]).astype(F32)[None]
    both = jnp.concatenate([biases, layout.other_core(biases)], axis=0)
    joined_biases = both[:, : core_heads * joined_size]
    joined_biases = jnp.where(
        chip // core_heads == core, joined_biases[0], joined_biases[1]
    ).reshape(core_heads, joined_size)
    bq = lax.dynamic_index_in_dim(joined_biases, chip % core_heads, 0, keepdims=True)
    bu = lax.dynamic_slice_in_dim(
        both, core_heads * joined_size + chip * hidden_part, hidden_part, 1
    ).reshape(1, hidden_size)

    hd_rows = out_shard.shape[1]
    head_blocks = []
    for turn in range(core_heads):
        head = layout.head_turn(chip, turn)
        out_part = lax.dynamic_index_in_dim(out_shard, head, 0, keepdims=False)
        out_part = out_part.reshape(hd_rows, width // head_size, head_size).transpose(1, 0, 2)
        head_blocks.append(
            jnp.concatenate(
                [
                    lax.dynamic_slice_in_dim(qkv_scaled, head * joined_size, joined_size, 1),
                    out_part.reshape(block_rows, head_size),
                ],
                axis=1,
            )
        )
    up_blocks = [
        lax.dynamic_slice_in_dim(up_scaled, (chip ^ up_mask) * hidden_part, hidden_part, 1)
        for up_mask in range(chips)
    ]
    queue = Queue(3)
    order, back_order = message_orders(chips, core_heads)
    heads = jnp.zeros((core_heads * block_rows, joined_size + head_size), BF16)
    wu0 = jnp.zeros((chips * block_rows, hidden_part), BF16)
    wu0 = lax.dynamic_update_slice_in_dim(wu0, up_blocks[0], chip * block_rows, 0)
    for k, (kind, which) in enumerate(order):
        block = head_blocks[which] if kind == "head" else up_blocks[which]
        if k == 1:
            block = ordered(block, *head_blocks)
        if k == 3:
            block = ordered(block, *up_blocks)
        if k == len(order) - 1:
            block = ordered(block, cosine, sine, mask, bq, bu, wd)
        block = queue.ready(block)
        if kind == "head":
            block = layout.send_head(block, which)
            slot = layout.head_turn(chip, which)
            heads = lax.dynamic_update_slice_in_dim(heads, block, slot * block_rows, 0)
        else:
            block = layout.swap(block, which)
            wu0 = lax.dynamic_update_slice_in_dim(wu0, block, (chip ^ which) * block_rows, 0)
        queue.put(block)
    wu = jnp.concatenate([wu0, layout.other_core(wu0)], axis=1)
    heads = layout.by_core(heads, layout.other_core(heads))

    row_bias = (out_bias[0].astype(F32) + down_bias[0].astype(F32))[None]

    part_rows = length // 2
    piece = jax.ShapeDtypeStruct((part_rows, width), BF16)

    def by_rows(cols, dtype):
        return jax.ShapeDtypeStruct((row_count, cols), dtype)

    matrix_flops = 4 * length * width * (joined_size + head_size + 2 * hidden_size)

    def pair_blocks(blocks, pair):
        return blocks[layout.slots[2 * pair]] + blocks[layout.slots[2 * pair + 1]]

    def put_pieces(pieces, pair, blocks):
        pieces[layout.slots[2 * pair]] = blocks[:2]
        pieces[layout.slots[2 * pair + 1]] = blocks[2:]

    def norm_back(upstream, scaled, normed, inverse):
        return upstream.astype(F32) + inverse * (
            scaled
            - jnp.mean(scaled, axis=-1, keepdims=True)
            - normed * jnp.mean(scaled * normed, axis=-1, keepdims=True)
        )

    cotangent_blocks = [block for slot in layout.slots for block in gathered[slot]]
    attended_grad, active_grad = call_rows(
        functools.partial(upstream_kernel, len(cotangent_blocks)),
        (*cotangent_blocks, heads, wd),
        (),
        None,
        (),
        [by_rows(head_size, BF16), by_rows(hidden_size, BF16)],
        [pltpu.VMEM((row_count, width), BF16), pltpu.VMEM((head_size, width), BF16)],
        0,
        row_count,
        2 * row_count * width * (head_size + hidden_size),
    )

    matrices = (heads, wu, wd)
    pieces = {}
    for at in (1, 0):
        slots = layout.slots[at * chips // 2 : (at + 1) * chips // 2]
        blocks = [block for slot in slots for block in gathered[slot]]
        rows = row_count // 2
        results = call_rows(
            functools.partial(forward_kernel, len(blocks), 2 * len(slots)),
            (*blocks, *matrices, bq, bu, ratio),
            (cosine, sine, mask),
            None,
            (),
            [piece] * (2 * len(slots)),
            [
                pltpu.VMEM((rows, width), BF16),
                pltpu.VMEM((rows, width), BF16),
                pltpu.VMEM((rows, head_size), BF16),
                pltpu.VMEM((rows, hidden_size), BF16),
                pltpu.VMEM((head_size, width), BF16),
            ],
            at,
            rows,
            2 * matrix_flops,
        )
        for k, slot in enumerate(slots):
            pieces[slot] = results[2 * k : 2 * k + 2]
    branch_rows = layout.ring_scatter(pieces)
    first_out = [
        (rows + branch + row_bias).astype(BF16)
        for rows, branch in zip(parts_of(own_tokens), branch_rows)
    ]

    layer_input = [
        jnp.where(first_section, rows, lax.ppermute(sent, "section", [(0, 1), (1, 0)]).astype(F32))
        for rows, sent in zip(parts_of(own_tokens), first_out)
    ]
    own_normed = [normalize(rows) for rows in layer_input]
    normed_blocks = layout.ring_gather([rows.astype(BF16) for rows, _ in own_normed])
    kept_shapes = (
        by_rows(width, BF16),
        by_rows(width, BF16),
        by_rows(joined_size, BF16),
        by_rows(length, F32),
        by_rows(head_size, BF16),
        by_rows(hidden_size, BF16),
        by_rows(hidden_size, BF16),
    )
    kept = None
    pieces = {}
    for pair in range(chips // 2):
        blocks = pair_blocks(normed_blocks, pair)
        results = call_rows(
            functools.partial(both_kernel, len(blocks), 4, len(kept_shapes) if kept else 0),
            (*blocks, heads, wu, bq, bu, ratio),
            (cosine, sine, mask, attended_grad, active_grad),
            kept,
            kept_shapes,
            [piece] * 4,
            [
                pltpu.VMEM((2 * length, joined_size), BF16),
                pltpu.VMEM((2 * length, hidden_size), BF16),
            ],
            pair,
            2 * length,
            2 * matrix_flops,
        )
        kept = results[: len(kept_shapes)]
        put_pieces(pieces, pair, results[len(kept_shapes) :])
    first_norm, second_norm, qkv, attention, attended, active, slope = kept
    scaled_rows = layout.ring_scatter(pieces)
    second_grad = [
        norm_back(given, scaled, *norm)
        for given, scaled, norm in zip(parts_of(own_cotangent), scaled_rows, own_normed)
    ]

    arrived_grad = [
        lax.ppermute(rows.astype(BF16), "section", [(0, 1), (1, 0)]) for rows in second_grad
    ]
    own_upstream = [
        jnp.where(first_section, arrived, given)
        for arrived, given in zip(arrived_grad, parts_of(own_cotangent))
    ]
    upstream_blocks = layout.ring_gather(own_upstream)
    second_section = jnp.where(first_section, 0, 1).astype(jnp.int32).reshape(1)
    grad_shapes = (by_rows(width, BF16), by_rows(joined_size, BF16), by_rows(hidden_size, BF16))
    grads = None
    sums = []
    for pair in range(chips // 2):
        blocks = pair_blocks(upstream_blocks, pair)
        results = call_rows(
            functools.partial(
                backward_kernel, len(blocks), len(grad_shapes) if grads else 0
            ),
            (*blocks, heads, wd),
            (cosine, sine, qkv, attention, slope),
            grads,
            grad_shapes,
            [
                jax.ShapeDtypeStruct((8, joined_size), F32),
                jax.ShapeDtypeStruct((8, hidden_size), F32),
            ],
            [pltpu.VMEM((head_size, width), BF16)],
            pair,
            2 * length,
            matrix_flops // 2,
        )
        grads = results[: len(grad_shapes)]
        sums.append(results[len(grad_shapes) :])
    upstream, joined_grad, hidden_grad = grads

    def half_of(array, which):
        size = array.shape[1] // cores
        return lax.dynamic_slice_in_dim(array, which * size, size, 1)

    row_major = Format(major_to_minor=(0, 1))

    def weight_grad(left_side, right_side):
        return with_layout_constraint(contract_rows(left_side, right_side), row_major)

    joined_given = weight_grad(half_of(first_norm, 1 - core), joined_grad).astype(BF16)
    out_given = weight_grad(half_of(attended, 1 - core), upstream).astype(BF16)
    hidden_given = weight_grad(second_norm, hidden_grad[:, hidden_part:]).astype(BF16)
    joined_taken, out_taken, hidden_taken = (
        layout.other_core(item) for item in (joined_given, out_given, hidden_given)
    )

    def core_sum(own, taken):
        return (own + taken.astype(F32)).astype(BF16)

    late_grad, late_attended = (
        ordered(item, joined_given, out_given, hidden_given) for item in (joined_grad, attended)
    )
    joined_held = core_sum(weight_grad(half_of(first_norm, core), late_grad), joined_taken)
    out_held = core_sum(weight_grad(half_of(late_attended, core), upstream), out_taken)
    late_grad = ordered(hidden_grad, joined_held, out_held)
    hidden_held = core_sum(weight_grad(second_norm, late_grad[:, :hidden_part]), hidden_taken)
    late_active = ordered(active, hidden_held)
    down_taken = layout.other_core(
        weight_grad(late_active[:, hidden_part:], upstream).astype(BF16)
    )

    late_grad = ordered(joined_grad, joined_held, out_held, hidden_held)
    pair_rows = 2 * length

    def by_pair(item):
        return pl.BlockSpec((pair_rows, item.shape[1]), lambda i: (i, 0))

    row_items = (first_norm, second_norm, attended, active, late_grad, hidden_grad)
    last_rows, norm_parts = pl.pallas_call(
        scaled_kernel,
        grid=(row_count // pair_rows,),
        out_shape=[by_rows(width, BF16), jax.ShapeDtypeStruct((32, width), F32)],
        in_specs=[pl.BlockSpec(memory_space=pltpu.SMEM)]
        + [pl.BlockSpec(memory_space=pltpu.VMEM)] * 3
        + [by_pair(item) for item in row_items],
        out_specs=[
            by_pair(by_rows(width, BF16)),
            pl.BlockSpec((32, width), lambda i: (0, 0)),
        ],
        scratch_shapes=[pltpu.VMEM((head_size, width), BF16)],
        cost_estimate=pl.CostEstimate(
            flops=2 * matrix_flops, bytes_accessed=row_count * 8192, transcendentals=0
        ),
        compiler_params=pltpu.CompilerParams(vmem_limit_bytes=VMEM_BYTES),
    )(second_section, heads, wu, wd, *row_items)
    last_pieces = {
        slot: [last_rows[k * length : (k + 1) * length]] for k, slot in enumerate(layout.slots)
    }

    own_given = jnp.concatenate(own_upstream, axis=0)
    (local_sums,) = call_whole(
        functools.partial(sums_kernel, len(sums)),
        [
            jnp.stack([chip, core]),
            norm_parts,
            *[item for pair in sums for item in pair],
            own_given,
        ],
        [jax.ShapeDtypeStruct((chips, width + joined_size + hidden_size), F32)],
        [],
    )
    joint = layout.sum_steps(local_sums)

    whole_sums = joint[-1]
    norm_sums = whole_sums[:4, :width].reshape(2, 2, width)
    norm_sums = jnp.stack([norm_sums[0] - ratio * norm_sums[1], norm_sums[1]]) / gains
    out_bias_grad = whole_sums[4, :width]
    joined_bias_grad = lax.dynamic_slice_in_dim(
        whole_sums[:, width : width + joined_size], core * core_heads, core_heads, 0
    )
    up_bias_grad = lax.dynamic_slice_in_dim(
        whole_sums[:, width + joined_size :], core * hidden_part, hidden_part, 1
    ).reshape(-1)

    (last_rows,) = layout.ring_scatter(last_pieces)
    last_normed, last_inverse = (
        jnp.concatenate([norm[k] for norm in own_normed], axis=0) for k in range(2)
    )
    first_grad = norm_back(own_given, last_rows, last_normed, last_inverse)
    own_grad = jnp.where(first_section, first_grad, jnp.concatenate(second_grad, axis=0))
    input_gradients = layout.by_core(own_grad, layout.other_core(own_grad))
    second_out = (jnp.concatenate(layer_input, axis=0) + last_rows + row_bias).astype(BF16)
    own_out = jnp.where(first_section, jnp.concatenate(first_out, axis=0), second_out)
    layer_outputs = layout.by_core(own_out, layout.other_core(own_out))

    out_rows = out_held.shape[0] // core_heads
    share_rows = out_rows // layout.groups
    head_blocks = []
    for turn in range(core_heads):
        slot = layout.head_turn(chip, turn)
        out_part = lax.dynamic_slice_in_dim(out_held, slot * out_rows, out_rows, 0)
        out_part = out_part.reshape(layout.groups, share_rows, width // head_size, head_size)
        head_blocks.append(
            jnp.concatenate(
                [
                    lax.dynamic_slice_in_dim(joined_held, slot * block_rows, block_rows, 0),
                    out_part.transpose(0, 2, 1, 3).reshape(block_rows, head_size),
                ],
                axis=1,
            )
        )
    queue = Queue(3)
    gain_cols = gain_rows[:, :, None]
    blocks = {
        ("up", 0): lax.dynamic_slice_in_dim(hidden_held, chip * block_rows, block_rows, 0)
    }
    up_weight_grad = None
    for k, (kind, which) in enumerate(back_order):
        if kind == "head":
            block = head_blocks[which]
        else:
            block = lax.dynamic_slice_in_dim(
                hidden_held, (chip ^ which) * block_rows, block_rows, 0
            )
        if k == 0:
            block = ordered(block, *head_blocks)
        if k == 6:
            block = ordered(block, joint[0])
        if k == 8:
            block = ordered(block, joint[1])
        if k == 10:
            block = ordered(block, joint[2])
        if k == len(back_order) - 3:
            block = ordered(block, down_weight_grad)
        if k == len(back_order) - 1:
            block = ordered(block, last_rows, joined_weight_grad)
        block = queue.ready(block)
        block = layout.return_head(block, which) if kind == "head" else layout.swap(block, which)
        queue.put(block)
        blocks[kind, which] = block
        if kind == "head" and which == core_heads - 1:
            heads_in = [blocks["head", turn] for turn in range(core_heads)]
            if layout.groups > 1:
                heads_in = [layout.scatter_groups(item, 0) for item in heads_in]
            joined_weight_grad, out_weight_grad = call_whole(
                functools.partial(heads_kernel, core_heads),
                [
                    jnp.stack([layout.head_turn(chip, turn) for turn in range(core_heads)]),
                    *heads_in,
                    gain_cols[0],
                ],
                [
                    jax.ShapeDtypeStruct((shard, core_heads, joined_size), F32),
                    jax.ShapeDtypeStruct((core_heads, share_rows, width), F32),
                ],
                [
                    pltpu.VMEM((core_heads, *heads_in[0].shape), heads_in[0].dtype),
                    pltpu.SemaphoreType.DMA((core_heads,)),
                ],
                range(1, 1 + core_heads),
            )
            down_weight_grad = weight_grad(
                late_active[:, :hidden_part], upstream
            ) + down_taken.astype(F32)
            if layout.groups > 1:
                down_weight_grad = layout.scatter_groups(down_weight_grad, 0)
        if k in (len(back_order) - 3, len(back_order) - 1):
            masks = [mask for mask in range(chips) if ("up", mask) in blocks]
            columns = [blocks.pop(("up", mask)) for mask in masks]
            if layout.groups > 1:
                columns = [layout.scatter_groups(item, 0) for item in columns]
            chain = [] if up_weight_grad is None else [up_weight_grad]
            (up_weight_grad,) = call_whole(
                functools.partial(up_kernel, len(columns), len(chain)),
                [jnp.stack([chip ^ mask for mask in masks]), *columns, gain_cols[1], *chain],
                [jax.ShapeDtypeStruct((shard, chips * hidden_part), F32)],
                [
                    pltpu.VMEM((len(columns), *columns[0].shape), F32),
                    pltpu.SemaphoreType.DMA((len(columns),)),
                ],
                range(len(columns) + 2, len(columns) + 3 + len(chain)),
                {len(columns) + 2: 0} if chain else None,
            )

    return (
        layer_outputs[None],
        input_gradients[None],
        norm_sums[0][None],
        norm_sums[1][None],
        joined_weight_grad[None],
        joined_bias_grad[None],
        out_weight_grad[None],
        out_bias_grad[None],
        up_weight_grad[None],
        up_bias_grad[None],
        down_weight_grad[None],
        out_bias_grad[None],
    )


def solution(mesh):
    def whole(*arrays):
        layout = Layout(mesh, arrays[5].shape[2])

        def local(*blocks):
            return on_device(layout, *blocks)

        return jax.shard_map(
            local,
            mesh=mesh,
            in_specs=(
                P("dp", None),
                P("dp", None),
                P("dp", None),
                P("section", None, None),
                P("section", None, None),
                P("section", "dp", "tensor", None),
                P("section", "tensor", None),
                P("section", "tensor", "dp", None),
                P("section", None),
                P("section", "dp", "tensor"),
                P("section", "tensor"),
                P("section", ("tensor", "dp"), None),
                P("section", None),
            ),
            out_specs=(
                P("section", "dp", None),
                P("section", "dp", None),
                P("section", None, None),
                P("section", None, None),
                P("section", "dp", "tensor", None),
                P("section", "tensor", None),
                P("section", "tensor", "dp", None),
                P("section", None),
                P("section", "dp", "tensor"),
                P("section", "tensor"),
                P("section", ("tensor", "dp"), None),
                P("section", None),
            ),
            check_vma=False,
        )(*arrays)

    return whole
```

```python
import functools
import math

import jax
import jax.numpy as jnp
from jax import lax
from jax.experimental import pallas as pl
from jax.experimental.layout import Layout as Format
from jax.experimental.layout import with_layout_constraint
from jax.experimental.pallas import tpu as pltpu
from jax.sharding import PartitionSpec as P

ROT = 64
LANES = 128
NORM_EPSILON = 1e-05
MASK_VALUE = -1e30
ROOT_HALF = 0.7071067811865476
DENSITY_SCALE = 0.3989422804014327
F32 = jnp.float32
BF16 = jnp.bfloat16
VMEM_BYTES = 24 * 1024 * 1024


def contract_rows(left_side, right_side):
    return lax.dot_general(
        left_side, right_side, (((0,), (0,)), ((), ())), preferred_element_type=F32
    )


def contract_cols(left_side, right_side):
    return lax.dot_general(
        left_side, right_side, (((1,), (1,)), ((), ())), preferred_element_type=F32
    )


def matmul(left_side, right_side):
    return jnp.dot(left_side, right_side, preferred_element_type=F32)


def normalize(values):
    centered = values - jnp.mean(values, axis=-1, keepdims=True)
    inverse = lax.rsqrt(jnp.mean(centered * centered, axis=-1, keepdims=True) + NORM_EPSILON)
    return (centered * inverse, inverse)


def sequence_tables(segments):
    places = jnp.arange(segments.shape[1], dtype=jnp.int32)
    same_doc = segments[:, :, None] == segments[:, None, :]
    earlier = places[None, :] < places[:, None]
    position = jnp.sum(jnp.where(same_doc & earlier, 1, 0).astype(jnp.int32), axis=2)
    allowed = same_doc & (places[None, :] <= places[:, None])
    exponent = jnp.arange(ROT // 2, dtype=F32) * (2.0 / ROT)
    frequency = 10000.0 ** (-exponent)
    angles = position.astype(F32)[..., None] * frequency
    cosine, sine = jnp.cos(angles), jnp.sin(angles)
    rest = jnp.zeros(angles.shape[:2] + (LANES - ROT,), F32)
    count = segments.shape[0] * segments.shape[1]
    return (
        jnp.concatenate([cosine, cosine, rest + 1.0], axis=-1).reshape(count, LANES),
        jnp.concatenate([-sine, sine, rest], axis=-1).reshape(count, LANES),
        jnp.where(allowed, 0.0, MASK_VALUE).astype(F32).reshape(count, segments.shape[1]),
    )


class Layout:
    def __init__(self, mesh, heads):
        self.cores = mesh.shape["tensor"]
        self.dp = mesh.shape["dp"]
        self.chips = heads
        self.groups = self.dp // heads
        self.core_heads = heads // self.cores
        self.ring = list(range(0, heads, 2)) + list(range(heads - 1, 0, -2))
        self.slots = []
        for k in range(heads // 2):
            self.slots += [-k % heads, k + 1]

    def place(self):
        dp_index = lax.axis_index("dp")
        self.core = lax.axis_index("tensor")
        self.chip = dp_index // self.groups
        self.group = dp_index % self.groups

    def between_chips(self, block, target_of, sections=None):
        pairs = [
            (chip * self.groups + group, target_of(chip) * self.groups + group)
            for chip in range(self.chips)
            for group in range(self.groups)
        ]
        if sections is None:
            return lax.ppermute(block, "dp", pairs)
        pairs = [
            (section * self.dp + source, section * self.dp + target)
            for section in sections
            for source, target in pairs
        ]
        return lax.ppermute(block, ("section", "dp"), pairs)

    def ring_step(self, block, distance, sections=None):
        size = len(self.ring)

        def target_of(chip):
            return self.ring[(self.ring.index(chip) + distance) % size]

        return self.between_chips(block, target_of, sections)

    def between_groups(self, block, distance):
        pairs = [
            (chip * self.groups + group, chip * self.groups + (group + distance) % self.groups)
            for chip in range(self.chips)
            for group in range(self.groups)
        ]
        return lax.ppermute(block, "dp", pairs)

    def other_core(self, block):
        return lax.ppermute(block, "tensor", [(0, 1), (1, 0)])

    def by_core(self, own, other):
        first = self.core == 0
        return jnp.concatenate(
            [jnp.where(first, own, other), jnp.where(first, other, own)], axis=0
        )

    def gather_groups(self, block, axis):
        if self.groups == 1:
            return block
        size = block.shape[axis]
        shape = list(block.shape)
        shape[axis] = size * self.groups
        total = jnp.zeros(shape, block.dtype)
        for distance in range(self.groups):
            part = self.between_groups(block, distance) if distance else block
            source = (self.group - distance) % self.groups
            total = lax.dynamic_update_slice_in_dim(total, part, source * size, axis)
        return total

    def scatter_groups(self, block, axis):
        if self.groups == 1:
            return block.astype(F32)
        size = block.shape[axis] // self.groups
        total = lax.dynamic_slice_in_dim(block, self.group * size, size, axis).astype(F32)
        for distance in range(1, self.groups):
            target = (self.group + distance) % self.groups
            part = lax.dynamic_slice_in_dim(block, target * size, size, axis)
            total = total + self.between_groups(part.astype(BF16), distance).astype(F32)
        return total

    def sum_steps(self, block):
        held = [block + self.other_core(block)]
        mask = 1
        while mask < self.chips:
            held.append(held[-1] + self.between_chips(held[-1], lambda chip: chip ^ mask))
            mask *= 2
        if self.groups > 1:
            total = held[-1]
            for distance in range(1, self.groups):
                total = total + self.between_groups(held[-1], distance)
            held.append(total)
        return held

    def ring_gather(self, parts, sections=None):
        half = self.chips // 2
        held = [{0: part} for part in parts]
        for step in range(1, half + 1):
            for at, slots in enumerate(held):
                down = half - at % 2
                if step <= down:
                    slots[step] = self.ring_step(slots[step - 1], -1, sections)
                if step <= self.chips - 1 - down:
                    slots[self.chips - step] = self.ring_step(
                        slots[(self.chips - step + 1) % self.chips], 1, sections
                    )
        return {slot: [slots[slot] for slots in held] for slot in range(self.chips)}

    def ring_scatter(self, pieces, sections=None, waits=None):
        half = self.chips // 2
        totals = []
        for at in range(len(pieces[0])):
            parts = [pieces[slot][at] for slot in range(self.chips)]
            up = half - at % 2
            total = parts[0].astype(F32)
            for way, slots in (
                (1, range(up, 0, -1)),
                (-1, range(up + 1, self.chips)),
            ):
                moving = None
                for step, slot in enumerate(slots):
                    if moving is None:
                        moving = parts[slot]
                    else:
                        moving = (moving.astype(F32) + parts[slot].astype(F32)).astype(BF16)
                    if waits and step in waits:
                        moving = ordered(moving, *waits[step])
                    moving = self.ring_step(moving, way, sections)
                total = total + moving.astype(F32)
            totals.append(total)
        return totals

    def head_turn(self, chip, turn):
        return (chip % self.core_heads) ^ turn

    def head_route(self, turn):
        pairs = []
        for core in range(self.cores):
            for chip in range(self.chips):
                target_core = chip // self.core_heads
                target = core * self.core_heads + self.head_turn(chip, turn)
                for group in range(self.groups):
                    pairs.append(
                        (
                            core * self.dp + chip * self.groups + group,
                            target_core * self.dp + target * self.groups + group,
                        )
                    )
        return pairs

    def send_head(self, block, turn):
        return lax.ppermute(block, ("tensor", "dp"), self.head_route(turn))

    def return_head(self, block, turn):
        pairs = [(target, source) for source, target in self.head_route(turn)]
        return lax.ppermute(block, ("tensor", "dp"), pairs)

    def swap(self, block, mask):
        return self.between_chips(block, lambda chip: chip ^ mask)


def message_orders(chips, core_heads):
    near = [("up", mask) for mask in range(chips // 2 - 1, 0, -1)]
    far = [("up", mask) for mask in range(chips - 1, chips // 2 - 1, -1)]
    heads = [("head", turn) for turn in range(core_heads)]
    out = heads[:1]
    for k, head in enumerate(heads[1:]):
        out += [head] + near[k : k + 1]
    out += near[len(heads) - 1 :] + far
    mixed = [item for pair in zip(near, far) for item in pair][: len(heads)]
    back = [item for pair in zip(heads, mixed) for item in pair]
    rest = [item for item in far if item not in back]
    back += rest[:-1] + [item for item in near if item not in back] + rest[-1:]
    return (out, back)


def ordered(block, *earlier):
    return lax.optimization_barrier((block,) + earlier)[0]


class Queue:
    def __init__(self, window, first=()):
        self.window = window
        self.results = [first] * window

    def ready(self, block):
        earlier = self.results[-self.window]
        return ordered(block, *earlier) if earlier else block

    def put(self, *result):
        self.results.append(result)


def turn_head(values, cosine, sine):
    first = values[:, :LANES]
    lane = lax.broadcasted_iota(jnp.int32, first.shape, 1)
    half = ROT // 2
    swapped = jnp.where(
        lane < half, pltpu.roll(first, LANES - half, 1), pltpu.roll(first, half, 1)
    )
    return jnp.concatenate([first * cosine + swapped * sine, values[:, LANES:]], axis=1)


def attend(joined, cosine, sine, mask):
    size = joined.shape[1] // 3
    queries = turn_head(joined[:, :size], cosine, sine).astype(BF16)
    key_rows = turn_head(joined[:, size : 2 * size], cosine, sine).astype(BF16)
    values = joined[:, 2 * size :].astype(BF16)
    scores = contract_cols(queries, key_rows) * (1.0 / math.sqrt(size)) + mask
    powered = jnp.exp(scores - jnp.max(scores, axis=-1, keepdims=True))
    attention = powered / jnp.sum(powered, axis=-1, keepdims=True)
    attended = matmul(attention.astype(BF16), values).astype(BF16)
    return (queries, key_rows, values, attention, attended)


def attend_back(queries, key_rows, values, attention, attended_grad, cosine, sine):
    scale = 1.0 / math.sqrt(queries.shape[1])
    values_grad = contract_rows(attention.astype(BF16), attended_grad)
    attention_grad = contract_cols(attended_grad, values)
    row_dots = jnp.sum(attention_grad * attention, axis=-1, keepdims=True)
    scores_grad = (attention * (attention_grad - row_dots)).astype(BF16)
    queries_grad = turn_head(matmul(scores_grad, key_rows) * scale, cosine, -sine)
    keys_grad = turn_head(contract_rows(scores_grad, queries) * scale, cosine, -sine)
    return jnp.concatenate([queries_grad, keys_grad, values_grad], axis=1).astype(BF16)


def fold_rows(values):
    return jnp.sum(values.reshape(values.shape[0] // 8, 8, values.shape[1]), axis=0)


def store_rows(refs, cols, values):
    rows = values.shape[0] // len(refs)
    for at, ref in enumerate(refs):
        ref[:, cols] = values[at * rows : (at + 1) * rows].astype(BF16)


def steps(size):
    step = min(256, size)
    return [slice(at, at + step) for at in range(0, size, step)]


def load_rows(refs, target, shift=0.0):
    rows = target.shape[0] // len(refs)
    for at, ref in enumerate(refs):
        values = ref[:rows]
        if not isinstance(shift, float):
            values = (values.astype(F32) + shift).astype(BF16)
        target[at * rows : (at + 1) * rows] = values


def split_heads(heads, wo):
    size = wo.shape[0]
    rows = heads.shape[0] // wo.shape[1] * size
    cols = heads.shape[1] - size
    part = size * rows // heads.shape[0]
    for at in range(0, heads.shape[0], rows):
        for k in range(rows // part):
            wo[at // rows * part : (at // rows + 1) * part, k * size : (k + 1) * size] = heads[
                at + k * part : at + (k + 1) * part, cols:
            ]
    return heads.at[:, :cols]


def forward_kernel(count, pieces, *refs):
    blocks, refs = refs[:count], refs[count:]
    heads, wu, wd, bq, bu, ratio, cosine, sine, mask = refs[:9]
    outs, refs = refs[9 : 9 + pieces], refs[9 + pieces :]
    first_norm, second_norm, attended, active, wo = refs
    wq = split_heads(heads, wo)
    length = mask.shape[1]
    load_rows(blocks, first_norm, ratio[0:1])
    load_rows(blocks, second_norm, ratio[1:2])
    joined = matmul(first_norm[...], wq[...]) + bq[...]
    for s in range(mask.shape[0] // length):
        rows = slice(s * length, (s + 1) * length)
        attended[rows] = attend(joined[rows], cosine[rows], sine[rows], mask[rows])[4]
    for cols in steps(wu.shape[1]):
        hidden = matmul(second_norm[...], wu[:, cols]) + bu[:, cols]
        active[:, cols] = (hidden * (0.5 * (1.0 + lax.erf(hidden * ROOT_HALF)))).astype(BF16)
    for cols in steps(wo.shape[1]):
        total = matmul(attended[...], wo[:, cols]) + matmul(active[...], wd[:, cols])
        store_rows(outs, cols, total)


def upstream_kernel(count, *refs):
    grads, refs = refs[:count], refs[count:]
    heads, wd, attended_grad, active_grad, upstream, wo = refs
    split_heads(heads, wo)
    load_rows(grads, upstream)
    attended_grad[...] = contract_cols(upstream[...], wo[...]).astype(BF16)
    for rows in steps(wd.shape[0]):
        active_grad[:, rows] = contract_cols(upstream[...], wd[rows]).astype(BF16)


def both_kernel(count, pieces, chained, *refs):
    blocks, refs = refs[:count], refs[count:]
    heads, wu, bq, bu, ratio, cosine, sine, mask, attended_grad, active_grad = refs[:10]
    refs = refs[10 + chained :]
    first_norm, second_norm, qkv, attention, attended, active, slope = refs[:7]
    outs, (joined_grad, hidden_grad) = refs[7 : 7 + pieces], refs[7 + pieces :]
    length = mask.shape[1]
    size = attended_grad.shape[1]
    wq = heads.at[:, : 3 * size]
    part = wu.shape[1] // 2
    load_rows(blocks, first_norm, ratio[0:1])
    load_rows(blocks, second_norm, ratio[1:2])
    joined = matmul(first_norm[...], wq[...]) + bq[...]

    def attention_of(s):
        rows = slice(s * length, (s + 1) * length)
        queries, key_rows, values, weights, result = attend(
            joined[rows], cosine[rows], sine[rows], mask[rows]
        )
        qkv[rows, :size] = queries
        qkv[rows, size : 2 * size] = key_rows
        qkv[rows, 2 * size :] = values
        attention[rows] = weights
        attended[rows] = result
        joined_grad[rows] = attend_back(
            queries, key_rows, values, weights, attended_grad[rows], cosine[rows], sine[rows]
        )

    for k in range(2):
        attention_of(k)
        for cols in steps(part):
            at = slice(k * part + cols.start, k * part + cols.stop)
            hidden = matmul(second_norm[...], wu[:, at]) + bu[:, at]
            normal_cdf = 0.5 * (1.0 + lax.erf(hidden * ROOT_HALF))
            normal_pdf = jnp.exp(-0.5 * hidden * hidden) * DENSITY_SCALE
            active[:, at] = (hidden * normal_cdf).astype(BF16)
            change = normal_cdf + hidden * normal_pdf
            slope[:, at] = change.astype(BF16)
            hidden_grad[:, at] = (active_grad[:, at].astype(F32) * change).astype(BF16)
    for rows in steps(wq.shape[0]):
        total = contract_cols(joined_grad[...], wq[rows]) + contract_cols(
            hidden_grad[...], wu[rows]
        )
        store_rows(outs, rows, total)


def backward_kernel(count, chained, *refs):
    grads, refs = refs[:count], refs[count:]
    heads, wd, cosine, sine, qkv, attention, slope = refs[:7]
    upstream, joined_grad, hidden_grad, joined_sum, hidden_sum, wo = refs[7 + chained :]
    split_heads(heads, wo)
    length = attention.shape[1]
    size = wo.shape[0]
    part = wd.shape[0] // 2
    load_rows(grads, upstream)
    attended_grad = contract_cols(upstream[...], wo[...]).astype(BF16)
    for k in range(2):
        rows = slice(k * length, (k + 1) * length)
        joined_grad[rows] = attend_back(
            qkv[rows, :size],
            qkv[rows, size : 2 * size],
            qkv[rows, 2 * size :],
            attention[rows],
            attended_grad[rows],
            cosine[rows],
            sine[rows],
        )
        for cols in steps(part):
            at = slice(k * part + cols.start, k * part + cols.stop)
            active_grad = contract_cols(upstream[...], wd[at])
            grad = (active_grad * slope[:, at].astype(F32)).astype(BF16)
            hidden_grad[:, at] = grad
            hidden_sum[:, at] = fold_rows(grad.astype(F32))
    joined_sum[...] = fold_rows(joined_grad[...].astype(F32))


def scaled_kernel(second, heads, wu, wd, *refs):
    first_norm, second_norm, attended, active, joined_grad, hidden_grad = refs[:6]
    out, norm_sums, wo = refs[6:]
    wq = split_heads(heads, wo)

    @pl.when(pl.program_id(0) == 0)
    def _():
        norm_sums[...] = jnp.zeros_like(norm_sums)

    for cols in steps(wq.shape[0]):
        first = contract_cols(joined_grad[...], wq[cols])
        other = contract_cols(hidden_grad[...], wu[cols])
        norm_sums[0:8, cols] += fold_rows(first * first_norm[:, cols].astype(F32))
        norm_sums[8:16, cols] += fold_rows(other * second_norm[:, cols].astype(F32))
        norm_sums[16:24, cols] += fold_rows(first)
        norm_sums[24:32, cols] += fold_rows(other)
        out[:, cols] = (first + other).astype(BF16)

    @pl.when(second[0] != 0)
    def _():
        for cols in steps(wq.shape[0]):
            total = matmul(attended[...], wo[:, cols]) + matmul(active[...], wd[:, cols])
            out[:, cols] = total.astype(BF16)


def sums_kernel(pairs, *refs):
    where, norm_sums, parts = refs[0], refs[1], refs[2 : 2 + 2 * pairs]
    given, sums = refs[2 + 2 * pairs :]
    joined_sum, hidden_sum = (
        functools.reduce(jnp.add, [parts[2 * pair + k][...] for pair in range(pairs)])
        for k in range(2)
    )
    rows, width = sums.shape[0], given.shape[1]
    size = joined_sum.shape[1]
    chip, core = where[0], where[1]
    upstream = jnp.sum(given[...].astype(F32), axis=0, keepdims=True)
    for k in range(4):
        sums[k : k + 1, :width] = jnp.sum(norm_sums[8 * k : 8 * k + 8], axis=0, keepdims=True)
    sums[4:5, :width] = upstream
    sums[5:rows, :width] = jnp.zeros((rows - 5, width), F32)
    mine = lax.broadcasted_iota(jnp.int32, (rows, 1), 0) == chip
    joined = jnp.sum(joined_sum, axis=0, keepdims=True)
    sums[:, width : width + size] = jnp.where(mine, joined, 0.0)
    hidden = jnp.sum(hidden_sum, axis=0, keepdims=True)
    half = hidden.shape[1] // 2
    own, other = hidden[:, :half], hidden[:, half:]
    hidden = jnp.concatenate(
        [jnp.where(core == 0, own, other), jnp.where(core == 0, other, own)], axis=1
    )
    sums[:, width + size :] = jnp.where(mine, hidden, 0.0)


def heads_kernel(count, *refs):
    which, blocks, refs = refs[0], refs[1 : 1 + count], refs[1 + count :]
    gain, qkv_grad, out_grad, held, signals = refs
    copies = [
        pltpu.make_async_copy(block, held.at[which[k]], signals.at[k])
        for k, block in enumerate(blocks)
    ]
    for copy in copies:
        copy.start()
    for copy in copies:
        copy.wait()
    size = qkv_grad.shape[2]
    rows, width = out_grad.shape[1:]
    part = held.shape[2] - size
    for head in range(count):
        qkv_grad[:, head] = held[head, :, :size].astype(F32) * gain[...]
        for k in range(width // part):
            out_grad[head, :, k * part : (k + 1) * part] = held[
                head, k * rows : (k + 1) * rows, size:
            ].astype(F32)


def up_kernel(count, chained, *refs):
    which, blocks, refs = refs[0], refs[1 : 1 + count], refs[1 + count :]
    gain, refs = refs[0], refs[1 + chained :]
    up_grad, held, signals = refs
    size = blocks[0].shape[1]
    copies = []
    for k, block in enumerate(blocks):
        held[k] = block[...].astype(F32) * gain[...]
        place = pl.multiple_of(which[k] * size, size)
        copies.append(
            pltpu.make_async_copy(held.at[k], up_grad.at[:, pl.ds(place, size)], signals.at[k])
        )
        copies[-1].start()
    for copy in copies:
        copy.wait()


def rows_spec(array, count, pair):
    return pl.BlockSpec((count, array.shape[1]), lambda i: (pair, 0))


def call_rows(
    kernel, whole, by_rows, chain, outs_by_rows, outs_whole, scratch, at, rows, flops
):
    out_shape = list(outs_by_rows) + list(outs_whole)
    out_specs = [rows_spec(item, rows, at) for item in outs_by_rows] + [
        pl.BlockSpec(item.shape, lambda i: (0, 0)) for item in outs_whole
    ]
    operands = [*whole, *by_rows]
    in_specs = [
        pl.BlockSpec(memory_space=pltpu.SMEM if item.ndim == 1 else pltpu.VMEM) for item in whole
    ] + [rows_spec(item, rows, at) for item in by_rows]
    aliases = {}
    for k, item in enumerate(chain or ()):
        aliases[len(operands)] = k
        operands.append(item)
        in_specs.append(pl.BlockSpec(memory_space=pl.ANY))
    return pl.pallas_call(
        kernel,
        grid=(1,),
        out_shape=out_shape,
        in_specs=in_specs,
        out_specs=out_specs,
        scratch_shapes=scratch,
        input_output_aliases=aliases,
        cost_estimate=pl.CostEstimate(flops=flops, bytes_accessed=rows * 8192, transcendentals=0),
        compiler_params=pltpu.CompilerParams(vmem_limit_bytes=VMEM_BYTES),
    )(*operands)


def call_whole(kernel, operands, outs, scratch, outside=(), aliases=None):
    spaces = [
        pltpu.SMEM if item.dtype == jnp.int32 else pl.ANY if k in outside else pltpu.VMEM
        for k, item in enumerate([*operands, *outs])
    ]
    specs = [pl.BlockSpec(memory_space=space) for space in spaces]
    return pl.pallas_call(
        kernel,
        out_shape=outs,
        in_specs=specs[: len(operands)],
        out_specs=specs[len(operands) :],
        scratch_shapes=scratch,
        input_output_aliases=aliases or {},
        compiler_params=pltpu.CompilerParams(vmem_limit_bytes=VMEM_BYTES),
    )(*operands)


def on_device(
    layout,
    tokens,
    segments,
    cotangent,
    norm_gain,
    norm_bias,
    qkv_weight,
    qkv_bias,
    out_weight,
    out_bias,
    up_weight,
    up_bias,
    down_weight,
    down_bias,
):
    layout.place()
    first_section = lax.axis_index("section") == 0
    cores, chips, chip, core = layout.cores, layout.chips, layout.chip, layout.core
    length = segments.shape[1]
    width = tokens.shape[1]
    core_heads, joined_size = qkv_weight.shape[2:]
    head_size = joined_size // 3
    hidden_part = up_weight.shape[2] // chips
    hidden_size = cores * hidden_part
    row_count = chips * length

    def core_rows(block):
        return lax.dynamic_slice_in_dim(block, core * length, length, 0)

    def parts_of(rows, count=2):
        size = rows.shape[0] // count
        return [rows[k * size : (k + 1) * size] for k in range(count)]

    gains = norm_gain[0].astype(F32)
    shifts = norm_bias[0].astype(F32)
    own_tokens = core_rows(tokens).astype(F32)
    own_cotangent = core_rows(cotangent)
    own_normed, _ = normalize(own_tokens)

    own_segments = lax.dynamic_index_in_dim(segments, core, 0, keepdims=True).astype(BF16)
    own_segments = jnp.pad(own_segments, ((0, 15), (0, width - length)))
    first_block = jnp.where(first_section, own_normed.astype(BF16), own_cotangent)
    first_block = jnp.concatenate([first_block, own_segments], axis=0)
    gathered = layout.ring_gather([first_block])
    all_segments = jnp.concatenate(
        [gathered[slot][0][length : length + 1, :length] for slot in layout.slots], axis=0
    )
    cosine, sine, mask = sequence_tables(all_segments.astype(jnp.int32))

    shard = qkv_weight.shape[1]
    at = lax.axis_index("dp") * shard
    gain_rows = lax.dynamic_slice_in_dim(gains, at, shard, 1)
    qkv_scaled = qkv_weight[0].reshape(shard, core_heads * joined_size).astype(F32)
    qkv_scaled = layout.gather_groups((qkv_scaled * gain_rows[0][:, None]).astype(BF16), 0)
    up_scaled = (up_weight[0].astype(F32) * gain_rows[1][:, None]).astype(BF16)
    up_scaled = layout.gather_groups(up_scaled, 0)
    out_shard = layout.gather_groups(out_weight[0], 1)
    wd0 = layout.gather_groups(down_weight[0], 0)
    wd = jnp.concatenate([wd0, layout.other_core(wd0)], axis=0)
    block_rows = qkv_scaled.shape[0]

    ratio = shifts / gains
    biases = jnp.concatenate([qkv_bias[0].reshape(-1), up_bias[0]]).astype(F32)[None]
    both = jnp.concatenate([biases, layout.other_core(biases)], axis=0)
    joined_biases = both[:, : core_heads * joined_size]
    joined_biases = jnp.where(
        chip // core_heads == core, joined_biases[0], joined_biases[1]
    ).reshape(core_heads, joined_size)
    bq = lax.dynamic_index_in_dim(joined_biases, chip % core_heads, 0, keepdims=True)
    bu = lax.dynamic_slice_in_dim(
        both, core_heads * joined_size + chip * hidden_part, hidden_part, 1
    ).reshape(1, hidden_size)

    hd_rows = out_shard.shape[1]
    head_blocks = []
    for turn in range(core_heads):
        head = layout.head_turn(chip, turn)
        out_part = lax.dynamic_index_in_dim(out_shard, head, 0, keepdims=False)
        out_part = out_part.reshape(hd_rows, width // head_size, head_size).transpose(1, 0, 2)
        head_blocks.append(
            jnp.concatenate(
                [
                    lax.dynamic_slice_in_dim(qkv_scaled, head * joined_size, joined_size, 1),
                    out_part.reshape(block_rows, head_size),
                ],
                axis=1,
            )
        )
    up_blocks = [
        lax.dynamic_slice_in_dim(up_scaled, (chip ^ up_mask) * hidden_part, hidden_part, 1)
        for up_mask in range(chips)
    ]
    queue = Queue(3)
    order, back_order = message_orders(chips, core_heads)
    heads = jnp.zeros((core_heads * block_rows, joined_size + head_size), BF16)
    wu0 = jnp.zeros((chips * block_rows, hidden_part), BF16)
    wu0 = lax.dynamic_update_slice_in_dim(wu0, up_blocks[0], chip * block_rows, 0)
    for k, (kind, which) in enumerate(order):
        block = head_blocks[which] if kind == "head" else up_blocks[which]
        if k == 1:
            block = ordered(block, *head_blocks)
        if k == 2:
            block = ordered(block, *up_blocks)
        if k == len(order) - 1:
            block = ordered(block, cosine, sine, mask, bq, bu, wd)
        block = queue.ready(block)
        if kind == "head":
            block = layout.send_head(block, which)
            slot = layout.head_turn(chip, which)
            heads = lax.dynamic_update_slice_in_dim(heads, block, slot * block_rows, 0)
        else:
            block = layout.swap(block, which)
            wu0 = lax.dynamic_update_slice_in_dim(wu0, block, (chip ^ which) * block_rows, 0)
        queue.put(block)
    wu = jnp.concatenate([wu0, layout.other_core(wu0)], axis=1)
    heads = layout.by_core(heads, layout.other_core(heads))

    row_bias = (out_bias[0].astype(F32) + down_bias[0].astype(F32))[None]

    part_rows = length // 2
    piece = jax.ShapeDtypeStruct((part_rows, width), BF16)

    def by_rows(cols, dtype):
        return jax.ShapeDtypeStruct((row_count, cols), dtype)

    matrix_flops = 4 * length * width * (joined_size + head_size + 2 * hidden_size)

    def pair_blocks(blocks, pair):
        return blocks[layout.slots[2 * pair]] + blocks[layout.slots[2 * pair + 1]]

    def put_pieces(pieces, pair, blocks):
        pieces[layout.slots[2 * pair]] = blocks[:2]
        pieces[layout.slots[2 * pair + 1]] = blocks[2:]

    def norm_back(upstream, scaled, normed, inverse):
        return upstream.astype(F32) + inverse * (
            scaled
            - jnp.mean(scaled, axis=-1, keepdims=True)
            - normed * jnp.mean(scaled * normed, axis=-1, keepdims=True)
        )

    cotangent_blocks = [block for slot in layout.slots for block in gathered[slot]]
    attended_grad, active_grad = call_rows(
        functools.partial(upstream_kernel, len(cotangent_blocks)),
        (*cotangent_blocks, heads, wd),
        (),
        None,
        (),
        [by_rows(head_size, BF16), by_rows(hidden_size, BF16)],
        [pltpu.VMEM((row_count, width), BF16), pltpu.VMEM((head_size, width), BF16)],
        0,
        row_count,
        2 * row_count * width * (head_size + hidden_size),
    )

    matrices = (heads, wu, wd)
    pieces = {}
    for at in range(chips // 2 - 1, -1, -1):
        slots = layout.slots[2 * at : 2 * at + 2]
        blocks = [block for slot in slots for block in gathered[slot]]
        rows = 2 * length
        results = call_rows(
            functools.partial(forward_kernel, len(blocks), 2 * len(slots)),
            (*blocks, *matrices, bq, bu, ratio),
            (cosine, sine, mask),
            None,
            (),
            [piece] * (2 * len(slots)),
            [
                pltpu.VMEM((rows, width), BF16),
                pltpu.VMEM((rows, width), BF16),
                pltpu.VMEM((rows, head_size), BF16),
                pltpu.VMEM((rows, hidden_size), BF16),
                pltpu.VMEM((head_size, width), BF16),
            ],
            at,
            rows,
            matrix_flops,
        )
        for k, slot in enumerate(slots):
            pieces[slot] = results[2 * k : 2 * k + 2]
    branch_rows = layout.ring_scatter(pieces)
    first_out = [
        (rows + branch + row_bias).astype(BF16)
        for rows, branch in zip(parts_of(own_tokens), branch_rows)
    ]

    layer_input = [
        jnp.where(first_section, rows, lax.ppermute(sent, "section", [(0, 1), (1, 0)]).astype(F32))
        for rows, sent in zip(parts_of(own_tokens), first_out)
    ]
    own_normed = [normalize(rows) for rows in layer_input]
    normed_blocks = layout.ring_gather([rows.astype(BF16) for rows, _ in own_normed])
    kept_shapes = (
        by_rows(width, BF16),
        by_rows(width, BF16),
        by_rows(joined_size, BF16),
        by_rows(length, F32),
        by_rows(head_size, BF16),
        by_rows(hidden_size, BF16),
        by_rows(hidden_size, BF16),
    )
    kept = None
    pieces = {}
    for pair in range(chips // 2):
        blocks = pair_blocks(normed_blocks, pair)
        results = call_rows(
            functools.partial(both_kernel, len(blocks), 4, len(kept_shapes) if kept else 0),
            (*blocks, heads, wu, bq, bu, ratio),
            (cosine, sine, mask, attended_grad, active_grad),
            kept,
            kept_shapes,
            [piece] * 4,
            [
                pltpu.VMEM((2 * length, joined_size), BF16),
                pltpu.VMEM((2 * length, hidden_size), BF16),
            ],
            pair,
            2 * length,
            2 * matrix_flops,
        )
        kept = results[: len(kept_shapes)]
        put_pieces(pieces, pair, results[len(kept_shapes) :])
    first_norm, second_norm, qkv, attention, attended, active, slope = kept
    scaled_rows = layout.ring_scatter(pieces)
    second_grad = [
        norm_back(given, scaled, *norm)
        for given, scaled, norm in zip(parts_of(own_cotangent), scaled_rows, own_normed)
    ]

    arrived_grad = [
        lax.ppermute(rows.astype(BF16), "section", [(0, 1), (1, 0)]) for rows in second_grad
    ]
    own_upstream = [
        jnp.where(first_section, arrived, given)
        for arrived, given in zip(arrived_grad, parts_of(own_cotangent))
    ]
    upstream_blocks = layout.ring_gather(own_upstream)
    second_section = jnp.where(first_section, 0, 1).astype(jnp.int32).reshape(1)
    grad_shapes = (by_rows(width, BF16), by_rows(joined_size, BF16), by_rows(hidden_size, BF16))
    grads = None
    sums = []
    for pair in range(chips // 2):
        blocks = pair_blocks(upstream_blocks, pair)
        results = call_rows(
            functools.partial(
                backward_kernel, len(blocks), len(grad_shapes) if grads else 0
            ),
            (*blocks, heads, wd),
            (cosine, sine, qkv, attention, slope),
            grads,
            grad_shapes,
            [
                jax.ShapeDtypeStruct((8, joined_size), F32),
                jax.ShapeDtypeStruct((8, hidden_size), F32),
            ],
            [pltpu.VMEM((head_size, width), BF16)],
            pair,
            2 * length,
            matrix_flops // 2,
        )
        grads = results[: len(grad_shapes)]
        sums.append(results[len(grad_shapes) :])
    upstream, joined_grad, hidden_grad = grads

    def half_of(array, which):
        size = array.shape[1] // cores
        return lax.dynamic_slice_in_dim(array, which * size, size, 1)

    row_major = Format(major_to_minor=(0, 1))

    def weight_grad(left_side, right_side):
        return with_layout_constraint(contract_rows(left_side, right_side), row_major)

    joined_given = weight_grad(half_of(first_norm, 1 - core), joined_grad).astype(BF16)
    out_given = weight_grad(half_of(attended, 1 - core), upstream).astype(BF16)
    hidden_given = weight_grad(second_norm, hidden_grad[:, hidden_part:]).astype(BF16)
    joined_taken, out_taken, hidden_taken = (
        layout.other_core(item) for item in (joined_given, out_given, hidden_given)
    )

    def core_sum(own, taken):
        return (own + taken.astype(F32)).astype(BF16)

    late_grad, late_attended = (
        ordered(item, joined_given, out_given, hidden_given) for item in (joined_grad, attended)
    )
    joined_held = core_sum(weight_grad(half_of(first_norm, core), late_grad), joined_taken)
    out_held = core_sum(weight_grad(half_of(late_attended, core), upstream), out_taken)
    late_grad = ordered(hidden_grad, joined_held, out_held)
    hidden_held = core_sum(weight_grad(second_norm, late_grad[:, :hidden_part]), hidden_taken)
    late_active = ordered(active, hidden_held)
    down_taken = layout.other_core(
        weight_grad(late_active[:, hidden_part:], upstream).astype(BF16)
    )

    late_grad = ordered(joined_grad, joined_held, out_held, hidden_held)
    pair_rows = 2 * length

    def by_pair(item):
        return pl.BlockSpec((pair_rows, item.shape[1]), lambda i: (i, 0))

    row_items = (first_norm, second_norm, attended, active, late_grad, hidden_grad)
    last_rows, norm_parts = pl.pallas_call(
        scaled_kernel,
        grid=(row_count // pair_rows,),
        out_shape=[by_rows(width, BF16), jax.ShapeDtypeStruct((32, width), F32)],
        in_specs=[pl.BlockSpec(memory_space=pltpu.SMEM)]
        + [pl.BlockSpec(memory_space=pltpu.VMEM)] * 3
        + [by_pair(item) for item in row_items],
        out_specs=[
            by_pair(by_rows(width, BF16)),
            pl.BlockSpec((32, width), lambda i: (0, 0)),
        ],
        scratch_shapes=[pltpu.VMEM((head_size, width), BF16)],
        cost_estimate=pl.CostEstimate(
            flops=2 * matrix_flops, bytes_accessed=row_count * 8192, transcendentals=0
        ),
        compiler_params=pltpu.CompilerParams(vmem_limit_bytes=VMEM_BYTES),
    )(second_section, heads, wu, wd, *row_items)
    last_pieces = {
        slot: [last_rows[k * length : (k + 1) * length]] for k, slot in enumerate(layout.slots)
    }

    own_given = jnp.concatenate(own_upstream, axis=0)
    (local_sums,) = call_whole(
        functools.partial(sums_kernel, len(sums)),
        [
            jnp.stack([chip, core]),
            norm_parts,
            *[item for pair in sums for item in pair],
            own_given,
        ],
        [jax.ShapeDtypeStruct((chips, width + joined_size + hidden_size), F32)],
        [],
    )
    joint = layout.sum_steps(local_sums)

    whole_sums = joint[-1]
    norm_sums = whole_sums[:4, :width].reshape(2, 2, width)
    norm_sums = jnp.stack([norm_sums[0] - ratio * norm_sums[1], norm_sums[1]]) / gains
    out_bias_grad = whole_sums[4, :width]
    joined_bias_grad = lax.dynamic_slice_in_dim(
        whole_sums[:, width : width + joined_size], core * core_heads, core_heads, 0
    )
    up_bias_grad = lax.dynamic_slice_in_dim(
        whole_sums[:, width + joined_size :], core * hidden_part, hidden_part, 1
    ).reshape(-1)

    (last_rows,) = layout.ring_scatter(last_pieces)
    last_normed, last_inverse = (
        jnp.concatenate([norm[k] for norm in own_normed], axis=0) for k in range(2)
    )
    first_grad = norm_back(own_given, last_rows, last_normed, last_inverse)
    own_grad = jnp.where(first_section, first_grad, jnp.concatenate(second_grad, axis=0))
    input_gradients = layout.by_core(own_grad, layout.other_core(own_grad))
    second_out = (jnp.concatenate(layer_input, axis=0) + last_rows + row_bias).astype(BF16)
    own_out = jnp.where(first_section, jnp.concatenate(first_out, axis=0), second_out)
    layer_outputs = layout.by_core(own_out, layout.other_core(own_out))

    out_rows = out_held.shape[0] // core_heads
    share_rows = out_rows // layout.groups
    head_blocks = []
    for turn in range(core_heads):
        slot = layout.head_turn(chip, turn)
        out_part = lax.dynamic_slice_in_dim(out_held, slot * out_rows, out_rows, 0)
        out_part = out_part.reshape(layout.groups, share_rows, width // head_size, head_size)
        head_blocks.append(
            jnp.concatenate(
                [
                    lax.dynamic_slice_in_dim(joined_held, slot * block_rows, block_rows, 0),
                    out_part.transpose(0, 2, 1, 3).reshape(block_rows, head_size),
                ],
                axis=1,
            )
        )
    queue = Queue(3)
    gain_cols = gain_rows[:, :, None]
    blocks = {
        ("up", 0): lax.dynamic_slice_in_dim(hidden_held, chip * block_rows, block_rows, 0)
    }
    up_weight_grad = None
    for k, (kind, which) in enumerate(back_order):
        if kind == "head":
            block = head_blocks[which]
        else:
            block = lax.dynamic_slice_in_dim(
                hidden_held, (chip ^ which) * block_rows, block_rows, 0
            )
        if k == 0:
            block = ordered(block, *head_blocks)
        if k == 6:
            block = ordered(block, joint[0])
        if k == 8:
            block = ordered(block, joint[1])
        if k == 10:
            block = ordered(block, joint[2])
        if k == len(back_order) - 3:
            block = ordered(block, down_weight_grad)
        if k == len(back_order) - 1:
            block = ordered(block, last_rows, joined_weight_grad)
        block = queue.ready(block)
        block = layout.return_head(block, which) if kind == "head" else layout.swap(block, which)
        queue.put(block)
        blocks[kind, which] = block
        if kind == "head" and which == core_heads - 1:
            heads_in = [blocks["head", turn] for turn in range(core_heads)]
            if layout.groups > 1:
                heads_in = [layout.scatter_groups(item, 0) for item in heads_in]
            joined_weight_grad, out_weight_grad = call_whole(
                functools.partial(heads_kernel, core_heads),
                [
                    jnp.stack([layout.head_turn(chip, turn) for turn in range(core_heads)]),
                    *heads_in,
                    gain_cols[0],
                ],
                [
                    jax.ShapeDtypeStruct((shard, core_heads, joined_size), F32),
                    jax.ShapeDtypeStruct((core_heads, share_rows, width), F32),
                ],
                [
                    pltpu.VMEM((core_heads, *heads_in[0].shape), heads_in[0].dtype),
                    pltpu.SemaphoreType.DMA((core_heads,)),
                ],
                range(1, 1 + core_heads),
            )
            down_weight_grad = weight_grad(
                late_active[:, :hidden_part], upstream
            ) + down_taken.astype(F32)
            if layout.groups > 1:
                down_weight_grad = layout.scatter_groups(down_weight_grad, 0)
        if k in (len(back_order) - 3, len(back_order) - 1):
            masks = [mask for mask in range(chips) if ("up", mask) in blocks]
            columns = [blocks.pop(("up", mask)) for mask in masks]
            if layout.groups > 1:
                columns = [layout.scatter_groups(item, 0) for item in columns]
            chain = [] if up_weight_grad is None else [up_weight_grad]
            (up_weight_grad,) = call_whole(
                functools.partial(up_kernel, len(columns), len(chain)),
                [jnp.stack([chip ^ mask for mask in masks]), *columns, gain_cols[1], *chain],
                [jax.ShapeDtypeStruct((shard, chips * hidden_part), F32)],
                [
                    pltpu.VMEM((len(columns), *columns[0].shape), F32),
                    pltpu.SemaphoreType.DMA((len(columns),)),
                ],
                range(len(columns) + 2, len(columns) + 3 + len(chain)),
                {len(columns) + 2: 0} if chain else None,
            )

    return (
        layer_outputs[None],
        input_gradients[None],
        norm_sums[0][None],
        norm_sums[1][None],
        joined_weight_grad[None],
        joined_bias_grad[None],
        out_weight_grad[None],
        out_bias_grad[None],
        up_weight_grad[None],
        up_bias_grad[None],
        down_weight_grad[None],
        out_bias_grad[None],
    )


def solution(mesh):
    def whole(*arrays):
        layout = Layout(mesh, arrays[5].shape[2])

        def local(*blocks):
            return on_device(layout, *blocks)

        return jax.shard_map(
            local,
            mesh=mesh,
            in_specs=(
                P("dp", None),
                P("dp", None),
                P("dp", None),
                P("section", None, None),
                P("section", None, None),
                P("section", "dp", "tensor", None),
                P("section", "tensor", None),
                P("section", "tensor", "dp", None),
                P("section", None),
                P("section", "dp", "tensor"),
                P("section", "tensor"),
                P("section", ("tensor", "dp"), None),
                P("section", None),
            ),
            out_specs=(
                P("section", "dp", None),
                P("section", "dp", None),
                P("section", None, None),
                P("section", None, None),
                P("section", "dp", "tensor", None),
                P("section", "tensor", None),
                P("section", "tensor", "dp", None),
                P("section", None),
                P("section", "dp", "tensor"),
                P("section", "tensor"),
                P("section", ("tensor", "dp"), None),
                P("section", None),
            ),
            check_vma=False,
        )(*arrays)

    return whole
```
